32 devices in a mesh: filt: 4 (over y, x), dp: 8 (over z, core).
Axes of the slice: x: 2, y: 2, z: 4, core: 2. Of those that a mesh axis runs over, the one named last changes fastest.
Arguments:
- char_ids: int32 [16384, 50], P('dp'), may hold values from 0 to 261
- word_lengths: int32 [16384], P('dp'), may hold values from 1 to 50, as said below
- out_grad: bfloat16 [16384, 768], P(('dp', 'filt')), may hold values from -6 to 6
- highway_owner: int32 [4], replicated, may hold values from 0 to 3, as said below
- char_table: float32 [262, 16], replicated, may hold values from -6 to 6
- conv_weight: float32 [112, 2048], P(None, 'filt'), may hold values from -0.75 to 0.75
- conv_bias: float32 [2048], P('filt'), may hold values from -4 to 4
- highway_weight: float32 [8, 2048, 2048], P('filt', 'dp'), may hold values from -0.125 to 0.125
- proj_weight: float32 [2048, 768], P(('filt', 'dp')), may hold values from -0.125 to 0.125
- dense_bias: float32 [8960], replicated, may hold values from -4 to 4
- table_moment_one: float32 [262, 16], replicated, may hold values from -2.5 to 2.5
- table_moment_two: float32 [262, 16], replicated, may hold values from 0.0073728 to 0.1179648
- conv_moment_one: float32 [112, 2048], P(None, 'filt'), may hold values from -4 to 4
- conv_moment_two: float32 [112, 2048], P(None, 'filt'), may hold values from 0.02048 to 0.32768
- conv_bias_moment_one: float32 [2048], P('filt'), may hold values from -14 to 14
- conv_bias_moment_two: float32 [2048], P('filt'), may hold values from 0.180224 to 2.94912
- highway_moment_one: float32 [8, 2048, 2048], P('filt', 'dp'), may hold values from -20 to 20
- highway_moment_two: float32 [8, 2048, 2048], P('filt', 'dp'), may hold values from 0.507904 to 8.192
- highway_average: float32 [8, 2048, 2048], P('filt', 'dp'), may hold values from -0.125 to 0.125
- proj_moment_one: float32 [2048, 768], P(('filt', 'dp')), may hold values from -64 to 64
- proj_moment_two: float32 [2048, 768], P(('filt', 'dp')), may hold values from 4.096 to 63.8976
- bias_moment_one: float32 [8960], replicated, may hold values from -24 to 24
- bias_moment_two: float32 [8960], replicated, may hold values from 0.73728 to 11.79648
Outputs:
- word_vectors: float32 [16384, 768], P(('dp', 'filt'))
- table_grad: float32 [262, 16], replicated
- table_second: float32 [262, 16], replicated
- table_new: float32 [262, 16], replicated
- conv_grad: float32 [112, 2048], P(None, 'filt')
- conv_second: float32 [112, 2048], P(None, 'filt')
- conv_new: float32 [112, 2048], P(None, 'filt')
- conv_bias_grad: float32 [2048], P('filt')
- conv_bias_second: float32 [2048], P('filt')
- conv_bias_new: float32 [2048], P('filt')
- highway_grad: float32 [8, 2048, 2048], P('filt', 'dp')
- highway_second: float32 [8, 2048, 2048], P('filt', 'dp')
- highway_new: float32 [8, 2048, 2048], P('filt', 'dp')
- highway_average_new: float32 [8, 2048, 2048], P('filt', 'dp')
- proj_grad: float32 [2048, 768], P(('filt', 'dp'))
- proj_second: float32 [2048, 768], P(('filt', 'dp'))
- proj_new: float32 [2048, 768], P(('filt', 'dp'))
- bias_grad: float32 [8960], replicated
- bias_second: float32 [8960], replicated
- bias_new: float32 [8960], replicated
The draws below stay inside these ranges and needn't reach their ends.
Inputs may be any that keep to these rules, and one draw needn't show every extreme that they name: `word_lengths`: number of characters of each word; characters at positions from the length on are ignored, and some word has 50. `highway_owner`: an index of filt owns at most 2 of the 4 highway matrices, and one index owns exactly 2.
All inputs are finite; a program needn't handle non-finite values.
Results may differ from the reference program's by a relative error of at most 0.0087.
Values may be sent and summed in bfloat16 or wider, within the bound.
No kernel may reach another device: no remote copies, remote signals or barrier semaphores. Data moves between devices by JAX's collectives and lax.ppermute only.
A program may use at most 320 MiB of HBM per device.

```python
import math
import jax
import jax.numpy as jnp
import numpy as np
from jax import lax

VOCAB = 262
CHAR_DIM = 16
MAX_CHARS = 50
MAX_WIDTH = 7
FILTERS = 2048
OUT_DIM = 768
UNITS = 4
SLOTS = 2
WORD_DEV = 2048
STEP = 10
WORDS = 16384
N_FILT = 4
N_DP = 8


def draw_word_lengths(key, part):
    key = jax.random.fold_in(key, 7)
    key_upper, key_length, key_spot = jax.random.split(key, 3)
    upper = jax.random.randint(key_upper, (WORDS,), 2, MAX_CHARS + 2)
    lengths = jax.random.randint(key_length, (WORDS,), 1, upper)
    spot = jax.random.randint(key_spot, (), 0, WORDS)
    return lengths.at[spot].set(MAX_CHARS).astype(jnp.int32)


def draw_highway_owner(key, part):
    key = jax.random.fold_in(key, 13)
    key_owner, key_order = jax.random.split(key)
    chosen = jax.random.permutation(key_owner, N_FILT)[:3]
    owners = jnp.stack([chosen[0], chosen[0], chosen[1], chosen[2]])
    order = jax.random.permutation(key_order, UNITS)
    return owners[order].astype(jnp.int32)


def plant(entries, own_key, smallest, top_value):
    shape = entries.shape
    place = [jax.random.randint(jax.random.fold_in(own_key, axis), (), 0, shape[axis]) for axis in range(len(shape))]
    entries = entries.at[tuple(place)].set(smallest)
    longest = shape.index(max(shape))
    place[longest] = (place[longest] + 1) % shape[longest]
    return entries.at[tuple(place)].set(top_value)


def levels(stream_key, extent, cuts, least, high):
    factor_of, own = 1.0, jax.random.fold_in(stream_key, 6)
    for dim, blocks in cuts:
        steps = jnp.exp(jax.random.uniform(jax.random.fold_in(own, dim), (blocks,), jnp.float32, least / len(cuts), high / len(cuts)))
        factor_of = factor_of * jnp.repeat(steps, extent[dim] // blocks).reshape([-1 if axis == dim else 1 for axis in range(len(extent))])
    return factor_of


def cumulative_ranks(amount, lean):
    portions = [(1 << 20) // math.isqrt(standing ** lean) + 1 for standing in range(1, amount + 1)]
    width = 1 + sum(portions) // (1 << 30)
    return np.cumsum(np.array([max(1, weight // width) for weight in portions]))


def skewed_ids(rng, shape, count, lean):
    table = cumulative_ranks(count, lean)
    ticket = jax.random.randint(jax.random.fold_in(rng, 1), shape, 0, int(table[count - 1]))
    grade = jnp.searchsorted(jnp.asarray(table, jnp.int32), ticket, side="right")
    return jax.random.permutation(jax.random.fold_in(rng, 2), count)[grade].astype(jnp.int32)


def bell_draw(stream_key, shape, scale, limit, cuts=(), kind=jnp.bfloat16):
    values = scale * jax.random.normal(stream_key, shape, jnp.float32)
    if cuts:
        values = values * levels(stream_key, shape, cuts, -0.22, 0.18)
    return jnp.clip(values, -limit, limit).astype(kind)


def setup_inputs(seed: int = 0) -> dict:
    key_of = jax.random.split(jax.random.key(seed), 24)
    return {
        "char_ids": plant(skewed_ids(key_of[0], (WORDS, MAX_CHARS), VOCAB, 2), jax.random.fold_in(key_of[0], 3), 0, VOCAB - 1).astype(jnp.int32),
        "word_lengths": draw_word_lengths(jax.random.fold_in(key_of[23], 71), 0),
        "out_grad": bell_draw(key_of[2], (WORDS, OUT_DIM), 1.0, 6.0, ((0, 32),)),
        "highway_owner": draw_highway_owner(jax.random.fold_in(key_of[23], 71), 0),
        "char_table": bell_draw(key_of[4], (VOCAB, CHAR_DIM), 1.0, 6.0, (), jnp.float32),
        "conv_weight": bell_draw(key_of[5], (MAX_WIDTH * CHAR_DIM, FILTERS), (4 * CHAR_DIM) ** -0.5, 0.75, ((1, 4),), jnp.float32),
        "conv_bias": bell_draw(key_of[6], (FILTERS,), 0.3, 4.0, ((0, 4),), jnp.float32),
        "highway_weight": bell_draw(key_of[7], (N_FILT * SLOTS, FILTERS, FILTERS), FILTERS ** -0.5, 0.125, ((0, 4), (1, 8)), jnp.float32),
        "proj_weight": bell_draw(key_of[8], (FILTERS, OUT_DIM), FILTERS ** -0.5, 0.125, ((0, 32),), jnp.float32),
        "dense_bias": bell_draw(key_of[9], (4 * FILTERS + OUT_DIM,), 0.3, 4.0, (), jnp.float32),
        "table_moment_one": bell_draw(key_of[10], (VOCAB, CHAR_DIM), (0.0033 * (WORD_DEV * N_DP) ** 0.5), 2.5, (), jnp.float32),
        "table_moment_two": jnp.clip(jnp.exp(jax.random.uniform(key_of[11], (VOCAB, CHAR_DIM), jnp.float32, math.log(0.0073728), math.log(0.1179648))), 0.0073728, 0.1179648),
        "conv_moment_one": bell_draw(key_of[12], (MAX_WIDTH * CHAR_DIM, FILTERS), (0.0055 * (WORD_DEV * N_DP) ** 0.5), 4.0, ((1, 4),), jnp.float32),
        "conv_moment_two": jnp.clip(jnp.exp(math.log(0.32768) - 2.7725887 * jax.random.uniform(key_of[13], (MAX_WIDTH * CHAR_DIM, FILTERS), jnp.float32) ** levels(key_of[13], (MAX_WIDTH * CHAR_DIM, FILTERS), ((1, 4),), -0.2, 0.2)), 0.02048, 0.32768),
        "conv_bias_moment_one": bell_draw(key_of[14], (FILTERS,), (0.017 * (WORD_DEV * N_DP) ** 0.5), 14.0, ((0, 4),), jnp.float32),
        "conv_bias_moment_two": jnp.clip(jnp.exp(math.log(2.94912) - 2.7950616 * jax.random.uniform(key_of[15], (FILTERS,), jnp.float32) ** levels(key_of[15], (FILTERS,), ((0, 4),), -0.2, 0.2)), 0.180224, 2.94912),
        "highway_moment_one": bell_draw(key_of[16], (N_FILT * SLOTS, FILTERS, FILTERS), (0.028 * (WORD_DEV * N_DP) ** 0.5), 20.0, ((0, 4), (1, 8)), jnp.float32),
        "highway_moment_two": jnp.clip(jnp.exp(math.log(8.192) - 2.780621 * jax.random.uniform(key_of[17], (N_FILT * SLOTS, FILTERS, FILTERS), jnp.float32) ** levels(key_of[17], (N_FILT * SLOTS, FILTERS, FILTERS), ((0, 4), (1, 8)), -0.2, 0.2)), 0.507904, 8.192),
        "highway_average": bell_draw(key_of[18], (N_FILT * SLOTS, FILTERS, FILTERS), FILTERS ** -0.5, 0.125, ((0, 4), (1, 8)), jnp.float32),
        "proj_moment_one": bell_draw(key_of[19], (FILTERS, OUT_DIM), (0.077 * (WORD_DEV * N_DP) ** 0.5), 64.0, ((0, 32),), jnp.float32),
        "proj_moment_two": jnp.clip(jnp.exp(math.log(63.8976) - 2.7472708 * jax.random.uniform(key_of[20], (FILTERS, OUT_DIM), jnp.float32) ** levels(key_of[20], (FILTERS, OUT_DIM), ((0, 32),), -0.2, 0.2)), 4.096, 63.8976),
        "bias_moment_one": bell_draw(key_of[21], (4 * FILTERS + OUT_DIM,), (0.033 * (WORD_DEV * N_DP) ** 0.5), 24.0, (), jnp.float32),
        "bias_moment_two": jnp.clip(jnp.exp(jax.random.uniform(key_of[22], (4 * FILTERS + OUT_DIM,), jnp.float32, math.log(0.73728), math.log(11.79648))), 0.73728, 11.79648),
    }


@jax.custom_vjp
def low(v):
    return lax.optimization_barrier(v.astype(jnp.bfloat16)).astype(jnp.float32)

@jax.custom_vjp
def low_back(v):
    return v

def low_keep(v):
    return (low(v), None)

def low_pass(kept, grad):
    return (grad,)

def back_keep(v):
    return (v, None)

def back_low(kept, grad):
    return (low(grad),)
low.defvjp(low_keep, low_pass)
low_back.defvjp(back_keep, back_low)
beta_one = 0.9
beta_two = 0.999
adam_eps = 1e-08
decay_rate = 0.01
average_keep = 0.9

def channel_widths(count):
    channel = jnp.arange(count, dtype=jnp.int32)
    widths = jnp.ones((count,), jnp.int32)
    for power in range(6):
        widths = widths + (channel >= count * 2 ** power // 64).astype(jnp.int32)
    return widths

def unit_slots(owners, slots_each):
    order = jnp.arange(owners.shape[0], dtype=jnp.int32)
    before = (owners[:, None] == owners[None, :]) & (order[:, None] > order[None, :])
    return (owners * slots_each + lax.optimization_barrier(jnp.sum(before.astype(jnp.int32), axis=1))).astype(jnp.int32)

def pooling(conv_pre, lengths, widths, dtype):
    span_left = jnp.maximum(lengths[:, None] - widths[None, :], 0)
    inside = jnp.arange(MAX_CHARS, dtype=jnp.int32)[None, :, None] <= span_left[:, None, :]
    masked = jnp.where(inside, conv_pre, -1e+30)
    highest = lax.optimization_barrier(jnp.max(masked, axis=1))
    shifted = jnp.where(inside, jnp.exp(masked - highest[:, None, :]), 0.0)
    summed = lax.optimization_barrier(jnp.sum(shifted, axis=1))
    return highest + jnp.log(summed) - jnp.log((span_left + 1).astype(dtype))

def adam_update(weight, grad, moment_one, moment_two, rate):
    first_new = beta_one * moment_one + (1 - beta_one) * grad
    second_new = beta_two * moment_two + (1 - beta_two) * grad * grad
    corrected_one = first_new / (1 - beta_one ** STEP)
    corrected_two = second_new / (1 - beta_two ** STEP)
    updated = weight - rate * (corrected_one / (jnp.sqrt(corrected_two) + adam_eps) + decay_rate * weight)
    return (second_new, updated)

def reference(char_ids, word_lengths, out_grad, highway_owner, char_table, conv_weight, conv_bias, highway_weight, proj_weight, dense_bias, table_moment_one, table_moment_two, conv_moment_one, conv_moment_two, conv_bias_moment_one, conv_bias_moment_two, highway_moment_one, highway_moment_two, highway_average, proj_moment_one, proj_moment_two, bias_moment_one, bias_moment_two):
    highest_prec = lax.Precision.HIGHEST
    block_words = min(256, WORDS)
    count_blocks = WORDS // block_words
    id_blocks = char_ids.reshape(count_blocks, block_words, MAX_CHARS)
    length_blocks = word_lengths.reshape(count_blocks, block_words)
    widths = channel_widths(FILTERS)
    offsets = jnp.arange(MAX_WIDTH * CHAR_DIM, dtype=jnp.int32) // CHAR_DIM
    tap_mask = (offsets[:, None] < widths[None, :]).astype(jnp.float32)
    slot_index = unit_slots(highway_owner, SLOTS)
    units = highway_weight[slot_index]

    def forward(table, conv_w, conv_b, unit_w, proj_w, dense_b):
        conv_low = low(conv_w * tap_mask.astype(conv_w.dtype))
        unit_low = low(unit_w)
        proj_low = low(proj_w)
        bias_low = low(dense_b)
        layer_weights = [jnp.concatenate([unit_low[2 * layer], unit_low[2 * layer + 1]], axis=1) for layer in range(2)]

        def word_block(pieces):
            block_ids, block_lengths = pieces
            present = (jnp.arange(MAX_CHARS, dtype=jnp.int32)[None, :] < block_lengths[:, None]).astype(table.dtype)
            embedded = low(table[block_ids] * present[:, :, None])
            padded = jnp.pad(embedded, ((0, 0), (0, MAX_WIDTH - 1), (0, 0)))
            windows = jnp.concatenate([padded[:, offset:offset + MAX_CHARS, :] for offset in range(MAX_WIDTH)], axis=2)
            conv_pre = low_back(jnp.einsum('bpk,kc->bpc', windows, conv_low, precision=highest_prec) + conv_b)
            pooled = pooling(conv_pre, block_lengths, widths, table.dtype)
            current = low(low_back(jax.nn.silu(pooled)))
            for layer in range(2):
                entering = current if layer == 0 else low(current)
                hidden = low_back(jnp.dot(entering, layer_weights[layer], precision=highest_prec) + bias_low[2 * layer * FILTERS:2 * (layer + 1) * FILTERS])
                nonlinear = jax.nn.silu(hidden[:, :FILTERS])
                gate_value = jax.nn.sigmoid(hidden[:, FILTERS:])
                current = gate_value * current + (1 - gate_value) * nonlinear
            return jnp.dot(low(current), proj_low, precision=highest_prec) + bias_low[4 * FILTERS:]
        outputs = lax.map(jax.checkpoint(word_block), (id_blocks, length_blocks))
        return outputs.reshape(WORDS, OUT_DIM)
    word_vectors, pullback = jax.vjp(forward, char_table, conv_weight, conv_bias, units, proj_weight, dense_bias)
    table_grad, conv_grad, conv_bias_grad, units_grad, proj_grad, bias_grad = pullback(out_grad.astype(jnp.float32))
    highway_grad = jnp.zeros_like(highway_weight).at[slot_index].set(units_grad)
    table_second, table_new = adam_update(char_table, table_grad, table_moment_one, table_moment_two, 1.0)
    conv_second, conv_new = adam_update(conv_weight, conv_grad, conv_moment_one, conv_moment_two, 0.1)
    conv_bias_second, conv_bias_new = adam_update(conv_bias, conv_bias_grad, conv_bias_moment_one, conv_bias_moment_two, 0.3)
    highway_second, highway_new = adam_update(highway_weight, highway_grad, highway_moment_one, highway_moment_two, 0.02)
    highway_average_new = average_keep * highway_average + (1 - average_keep) * highway_new
    proj_second, proj_new = adam_update(proj_weight, proj_grad, proj_moment_one, proj_moment_two, 0.02)
    bias_second, bias_new = adam_update(dense_bias, bias_grad, bias_moment_one, bias_moment_two, 0.3)
    return (word_vectors, table_grad, table_second, table_new, conv_grad, conv_second, conv_new, conv_bias_grad, conv_bias_second, conv_bias_new, highway_grad, highway_second, highway_new, highway_average_new, proj_grad, proj_second, proj_new, bias_grad, bias_second, bias_new)
```

```python
import functools

import jax
import jax.numpy as jnp
from jax import lax
from jax.experimental import pallas as pl
from jax.experimental.pallas import tpu as pltpu
from jax.sharding import PartitionSpec as P

CHAR_DIM = 16
MAX_CHARS = 50
MAX_WIDTH = 7
FILTERS = 2048
UNITS = 4
SLOTS = 2
STEP = 10
TAPS = MAX_WIDTH * CHAR_DIM
DEPTH = 128
ID_SHIFT = 128
ID_ROWS = 64
SLOTS_E = MAX_CHARS + MAX_WIDTH - 1 + 8
LANES = 128
STEP_P = 4
beta_one = 0.9
beta_two = 0.999
adam_eps = 1e-08
decay_rate = 0.01
average_keep = 0.9
F32, BF16 = jnp.float32, jnp.bfloat16
MIB = 1 << 20


def nt(a, b):
    return lax.dot_general(a, b, (((1,), (1,)), ((), ())), preferred_element_type=F32)


def nn(a, b):
    return lax.dot_general(a, b, (((1,), (0,)), ((), ())), preferred_element_type=F32)


def tn(a, b):
    return lax.dot_general(a, b, (((0,), (0,)), ((), ())), preferred_element_type=F32)


def embed_tile(ids_ref, table_ref, lens, e_ref, longest):
    tile = lens.shape[1]
    e_ref[...] = jnp.zeros_like(e_ref)
    pieces = table_ref.shape[1] // LANES

    def fill(p, carry):
        row = ids_ref[pl.ds(p, 1), :].astype(jnp.int32)
        parts = []
        for lane in range(tile // LANES):
            idx = jnp.broadcast_to(row[:, lane * LANES : (lane + 1) * LANES], (CHAR_DIM, LANES))
            low = jnp.bitwise_and(idx, LANES - 1)
            value = jnp.zeros((CHAR_DIM, LANES), F32)
            for piece in range(pieces):
                got = jnp.take_along_axis(table_ref[:, piece * LANES : (piece + 1) * LANES], low, axis=1)
                value = jnp.where(lax.shift_right_logical(idx, 7) == piece, got, value)
            parts.append(value)
        value = jnp.concatenate(parts, axis=1) if len(parts) > 1 else parts[0]
        value = jnp.where(p < lens, value, 0.0)
        e_ref[pl.ds(pl.multiple_of(p * CHAR_DIM, CHAR_DIM), CHAR_DIM), :] = value.astype(BF16)
        return carry

    lax.fori_loop(0, longest, fill, 0)


def limits_of(lens):
    row = lax.broadcasted_iota(jnp.int32, (CHAR_DIM, lens.shape[1]), 0)
    past = jnp.maximum(lens - (row - 2), 0)
    return jnp.where(row < 3, -1, jnp.where(row < 3 + MAX_WIDTH, past, 1 << 20))


def window_at(e_ref, limit, p):
    extra = jnp.where(p > limit, 1.0, 0.0).astype(BF16)
    taps = e_ref[pl.ds(pl.multiple_of(p * CHAR_DIM, CHAR_DIM), TAPS), :]
    return jnp.concatenate([taps, extra], axis=0)


def steps_of(longest, narrow):
    return (jnp.maximum(longest - narrow, 0) + STEP_P) // STEP_P


def conv_forward_kernel(cblock, narrow_ref, rank_ref, data_ref, table_ref, conv_ref, width_ref, feat_ref, lse_ref, ids_ref, e_ref, top, total, pre):
    tile = ids_ref.shape[1]
    words = rank_ref.shape[0]
    first = pl.program_id(0) * tile
    lane = first + lax.broadcasted_iota(jnp.int32, (words, tile), 1)
    hot = jnp.where(rank_ref[...] == lane, 1.0, 0.0).astype(BF16)
    moved = nn(data_ref[...], hot)
    shift = jnp.where(lax.broadcasted_iota(jnp.int32, moved.shape, 0) < MAX_CHARS, float(ID_SHIFT), 0.0)
    moved = moved + shift
    ids_ref[...] = moved
    lens = (moved[MAX_CHARS : MAX_CHARS + 1, :] + 0.5).astype(jnp.int32)
    longest = jnp.max(lens)
    embed_tile(ids_ref, table_ref, lens, e_ref, longest)
    limit = limits_of(lens)
    channels = conv_ref.shape[0]
    for block in range(channels // cblock):
        rows = pl.ds(block * cblock, cblock)
        top[...] = jnp.full_like(top, -1e30)
        total[...] = jnp.zeros_like(total)

        def step(s, carry):
            best = top[...]
            for i in range(STEP_P):
                value = nn(conv_ref[rows, :], window_at(e_ref, limit, s * STEP_P + i))
                pre[i] = value
                best = jnp.maximum(best, value)
            summed = total[...] * jnp.exp(top[...] - best)
            for i in range(STEP_P):
                summed = summed + jnp.exp(pre[i] - best)
            total[...] = summed
            top[...] = best
            return carry

        lax.fori_loop(0, steps_of(longest, narrow_ref[block]), step, 0)
        span = jnp.maximum(lens - width_ref[rows, :], 0)
        lse = top[...] + jnp.log(total[...])
        lse_ref[rows, :] = lse
        pooled = lse - jnp.log((span + 1).astype(F32))
        feat_ref[rows, :] = (pooled * jax.nn.sigmoid(pooled)).astype(BF16)


def place_kernel(rank_ref, feat_ref, out_ref):
    shape = (rank_ref.shape[0], feat_ref.shape[1])
    hot = jnp.where(rank_ref[...] == lax.broadcasted_iota(jnp.int32, shape, 1), 1.0, 0.0).astype(BF16)
    out_ref[...] = nt(hot, feat_ref[...]).astype(BF16)


def conv_forward(rank, data, table_t, conv_t, widths, narrow, cblock):
    words, channels = rank.shape[0], conv_t.shape[0]
    tile = min(256, words)
    full = lambda *shape: pl.BlockSpec(shape, lambda i: (0,) * len(shape))
    feat, lse, ids = pl.pallas_call(
        functools.partial(conv_forward_kernel, cblock),
        grid=(words // tile,),
        in_specs=[
            pl.BlockSpec(memory_space=pltpu.SMEM),
            full(words, 1),
            full(*data.shape),
            full(*table_t.shape),
            full(*conv_t.shape),
            full(channels, 1),
        ],
        out_specs=[
            pl.BlockSpec((channels, tile), lambda i: (0, i)),
            pl.BlockSpec((channels, tile), lambda i: (0, i)),
            pl.BlockSpec((ID_ROWS, tile), lambda i: (0, i)),
        ],
        out_shape=[
            jax.ShapeDtypeStruct((channels, words), BF16),
            jax.ShapeDtypeStruct((channels, words), F32),
            jax.ShapeDtypeStruct((ID_ROWS, words), F32),
        ],
        scratch_shapes=[
            pltpu.VMEM((SLOTS_E * CHAR_DIM, tile), BF16),
            pltpu.VMEM((cblock, tile), F32),
            pltpu.VMEM((cblock, tile), F32),
            pltpu.VMEM((STEP_P, cblock, tile), F32),
        ],
        compiler_params=pltpu.CompilerParams(vmem_limit_bytes=48 * MIB),
        name="conv_forward",
    )(narrow, rank, data, table_t, conv_t, widths)
    return feat, lse, ids


def conv_backward_kernel(cblock, n_parts, narrow_ref, ids_ref, table_ref, conv_ref, back_ref, width_ref, lse_ref, *refs):
    ranks, grads, refs = refs[:n_parts], refs[n_parts : 2 * n_parts], refs[2 * n_parts :]
    conv_grad_ref, table_grad_ref, e_ref, de_ref, dpool, d_pre = refs
    tile = ids_ref.shape[1]
    words = ranks[0].shape[0]
    vocab = table_grad_ref.shape[1]
    first = pl.program_id(0) * tile

    @pl.when(pl.program_id(0) == 0)
    def _():
        conv_grad_ref[...] = jnp.zeros_like(conv_grad_ref)
        table_grad_ref[...] = jnp.zeros_like(table_grad_ref)

    lane = first + lax.broadcasted_iota(jnp.int32, (words, tile), 1)
    hots = [jnp.where(rank_ref[...] == lane, 1.0, 0.0).astype(BF16) for rank_ref in ranks]
    lens = (ids_ref[MAX_CHARS : MAX_CHARS + 1, :] + 0.5).astype(jnp.int32)
    longest = jnp.max(lens)
    embed_tile(ids_ref, table_ref, lens, e_ref, longest)
    limit = limits_of(lens)
    de_ref[...] = jnp.zeros_like(de_ref)
    channels = conv_ref.shape[0]
    for block in range(channels // cblock):
        rows = pl.ds(block * cblock, cblock)
        span = jnp.maximum(lens - width_ref[rows, :], 0)
        pooled = lse_ref[rows, :] - jnp.log((span + 1).astype(F32))
        sigma = jax.nn.sigmoid(pooled)
        slope = sigma + pooled * sigma * (1 - sigma)
        dpool[...] = sum(tn(grad_ref[:, rows], hot) for grad_ref, hot in zip(grads, hots)) * slope

        def step(s, carry):
            windows = []
            for i in range(STEP_P):
                p = s * STEP_P + i
                window = window_at(e_ref, limit, p)
                value = nn(conv_ref[rows, :], window)
                d = (jnp.exp(value - lse_ref[rows, :]) * dpool[...]).astype(BF16)
                d_pre[:, i * tile : (i + 1) * tile] = d
                windows.append(window)
                at = pl.ds(pl.multiple_of(p * CHAR_DIM, CHAR_DIM), DEPTH)
                de_ref[at, :] += nn(back_ref[:, rows], d)
            conv_grad_ref[rows, :] += nt(d_pre[...], jnp.concatenate(windows, axis=1))
            return carry

        lax.fori_loop(0, steps_of(longest, narrow_ref[block]), step, 0)

    letter = lax.broadcasted_iota(jnp.int32, (vocab, tile), 0)

    def spread(p, carry):
        at = pl.ds(pl.multiple_of(p * CHAR_DIM, CHAR_DIM), CHAR_DIM)
        value = jnp.where(p < lens, de_ref[at, :], 0.0)
        high = value.astype(BF16)
        both = jnp.concatenate([high, (value - high.astype(F32)).astype(BF16)], axis=0)
        row = ids_ref[pl.ds(p, 1), :].astype(jnp.int32)
        found = jnp.where(letter == row, 1.0, 0.0).astype(BF16)
        table_grad_ref[...] += nt(both, found)
        return carry

    lax.fori_loop(0, longest, spread, 0)


def conv_backward(ranks, ids, table_t, conv_t, conv_back, widths, narrow, lse, grads, cblock):
    channels, words = conv_t.shape[0], ids.shape[1]
    tile = min(256, words)
    vocab = table_t.shape[1]
    full = lambda *shape: pl.BlockSpec(shape, lambda i: (0,) * len(shape))
    return pl.pallas_call(
        functools.partial(conv_backward_kernel, cblock, len(ranks)),
        grid=(words // tile,),
        in_specs=[
            pl.BlockSpec(memory_space=pltpu.SMEM),
            pl.BlockSpec((ID_ROWS, tile), lambda i: (0, i)),
            full(*table_t.shape),
            full(*conv_t.shape),
            full(*conv_back.shape),
            full(channels, 1),
            pl.BlockSpec((channels, tile), lambda i: (0, i)),
        ]
        + [full(*part.shape) for part in ranks]
        + [full(*part.shape) for part in grads],
        out_specs=[full(channels, DEPTH), full(2 * CHAR_DIM, vocab)],
        out_shape=[
            jax.ShapeDtypeStruct((channels, DEPTH), F32),
            jax.ShapeDtypeStruct((2 * CHAR_DIM, vocab), F32),
        ],
        scratch_shapes=[
            pltpu.VMEM((SLOTS_E * CHAR_DIM, tile), BF16),
            pltpu.VMEM((SLOTS_E * CHAR_DIM, tile), F32),
            pltpu.VMEM((cblock, tile), F32),
            pltpu.VMEM((cblock, STEP_P * tile), BF16),
        ],
        compiler_params=pltpu.CompilerParams(vmem_limit_bytes=48 * MIB),
        name="conv_backward",
    )(narrow, ids, table_t, conv_t, conv_back, widths, lse, *ranks, *grads)


def word_order(lengths):
    count = lengths.shape[0]
    key = lengths * count - jnp.arange(count, dtype=jnp.int32)
    return jnp.sum((key[None, :] > key[:, None]).astype(jnp.int32), axis=1, keepdims=True)


def conv_operands(char_ids, lengths, char_table, conv_weight, conv_bias, widths, cblock):
    words = char_ids.shape[0]
    channels = conv_weight.shape[1]
    vocab = char_table.shape[0]
    lanes = -(-vocab // LANES) * LANES
    rank = word_order(lengths)
    data = jnp.concatenate([char_ids.T - ID_SHIFT, lengths[None, :]], axis=0)
    data = jnp.pad(data, ((0, ID_ROWS - MAX_CHARS - 1), (0, 0))).astype(BF16)
    offsets = jnp.arange(TAPS, dtype=jnp.int32) // CHAR_DIM
    taps = jnp.where(offsets[:, None] < widths[None, :], conv_weight, 0.0).astype(BF16)
    parts, rest = [], conv_bias
    for _ in range(3):
        part = lax.reduce_precision(rest, 8, 7)
        parts.append(part)
        rest = rest - part
    kinds = jnp.arange(1, MAX_WIDTH + 1, dtype=jnp.int32)
    spans = jnp.where(kinds[:, None] == widths[None, :], -1e30, 0.0)
    under = jnp.concatenate([jnp.stack(parts), spans, jnp.zeros((DEPTH - TAPS - 3 - MAX_WIDTH, channels), F32)])
    conv_all = jnp.concatenate([taps, under.astype(BF16)])
    conv_back = jnp.pad(taps, ((0, DEPTH - TAPS), (0, 0)))
    table_t = jnp.pad(lax.reduce_precision(char_table, 8, 7).T, ((0, 0), (0, lanes - vocab)))
    narrow = widths[::cblock]
    return rank, data, table_t, conv_all.T, conv_back, widths[:, None], narrow


def channel_widths(start, count, whole):
    channel = start + jnp.arange(count, dtype=jnp.int32)
    widths = jnp.ones((count,), jnp.int32)
    for power in range(6):
        widths = widths + (channel >= whole * 2**power // 64).astype(jnp.int32)
    return widths


def unit_slots(owners, slots_each):
    order = jnp.arange(owners.shape[0], dtype=jnp.int32)
    before = (owners[:, None] == owners[None, :]) & (order[:, None] > order[None, :])
    return owners * slots_each + jnp.sum(before.astype(jnp.int32), axis=1)


def place_words(rank, feat):
    words, channels = rank.shape[0], feat.shape[0]
    rows = min(256, words)
    return pl.pallas_call(
        place_kernel,
        grid=(words // rows,),
        in_specs=[
            pl.BlockSpec((rows, 1), lambda i: (i, 0)),
            pl.BlockSpec(feat.shape, lambda i: (0, 0)),
        ],
        out_specs=pl.BlockSpec((rows, channels), lambda i: (i, 0)),
        out_shape=jax.ShapeDtypeStruct((words, channels), BF16),
        compiler_params=pltpu.CompilerParams(vmem_limit_bytes=48 * MIB),
        name="place_words",
    )(rank, feat)


def load_pieces(table_ref, pieces, dest, sems, half=None):
    rows, cols = pieces[0].shape[2:]
    depth = dest.shape[1]

    def each(act):
        at = 0
        for ref in pieces:
            for j in range(ref.shape[0]):
                row, col = table_ref[0, at], table_ref[1, at]
                row = row if half is None else row - half * depth
                sem = sems.at[at]

                def go(ref=ref, j=j, row=row, col=col, sem=sem):
                    place = (slice(None), pl.ds(pl.multiple_of(row, rows), rows), pl.ds(pl.multiple_of(col, cols), cols))
                    act(pltpu.make_async_copy(ref.at[j], dest.at[place], sem))

                if half is None:
                    go()
                else:
                    pl.when((row >= 0) & (row < depth))(go)
                at += 1

    each(lambda copy: copy.start())
    each(lambda copy: copy.wait())


def hidden_of(xs, weight, unit, cols, bias_ref):
    at, total = 0, None
    for x in xs:
        term = nn(x[...], weight[unit, at : at + x.shape[1], cols])
        total = term if total is None else total + term
        at += x.shape[1]
    return total + bias_ref[unit : unit + 1, cols]


def forward_kernel(n_own, n_pieces, width, table_ref, bias_ref, *refs):
    own, refs = refs[:n_own], refs[n_own:]
    mate, refs = refs[:n_own], refs[n_own:]
    pieces, refs = refs[:n_pieces], refs[n_pieces:]
    next_ref, low_ref, first_ref, gate_ref, weight, sems = refs

    @pl.when(pl.program_id(0) == 0)
    def _():
        load_pieces(table_ref, pieces, weight, sems)

    for j, x in enumerate(own):
        cols = slice(j * width, (j + 1) * width)
        a = hidden_of(own + mate, weight, 0, cols, bias_ref)
        g = hidden_of(own + mate, weight, 1, cols, bias_ref)
        first_ref[:, cols] = a
        gate_ref[:, cols] = g
        gate = jax.nn.sigmoid(g)
        value = gate * x[...].astype(F32) + (1 - gate) * (a * jax.nn.sigmoid(a))
        next_ref[:, cols] = value
        low_ref[:, cols] = value.astype(BF16)


def slopes(dy, x, a, g):
    s = jax.nn.sigmoid(a)
    gate = jax.nn.sigmoid(g)
    nonlinear = a * s
    d_first = dy * (1 - gate) * (s + nonlinear * (1 - s))
    d_gate = dy * (x - nonlinear) * gate * (1 - gate)
    return d_first.astype(BF16), d_gate.astype(BF16), dy * gate, gate * x + (1 - gate) * nonlinear


def turn_kernel(n_pieces, width, table_ref, bias_ref, own, mate, exact, out_grad, proj, *refs):
    pieces, refs = refs[:n_pieces], refs[n_pieces:]
    low_ref, d_first_ref, d_gate_ref, up_ref, sums_ref, weight, sems = refs

    @pl.when(pl.program_id(0) == 0)
    def _():
        load_pieces(table_ref, pieces, weight, sems)
        sums_ref[...] = jnp.zeros_like(sums_ref)

    for j in range(own.shape[1] // width):
        cols = slice(j * width, (j + 1) * width)
        a = hidden_of((own, mate), weight, 0, cols, bias_ref)
        g = hidden_of((own, mate), weight, 1, cols, bias_ref)
        dy = nt(out_grad[...], proj[cols, :])
        d_first, d_gate, up, value = slopes(dy, exact[:, cols], a, g)
        low_ref[:, cols] = value.astype(BF16)
        d_first_ref[:, cols] = d_first
        d_gate_ref[:, cols] = d_gate
        up_ref[:, cols] = up
        sums_ref[0:1, cols] += jnp.sum(d_first.astype(F32), axis=0, keepdims=True)
        sums_ref[1:2, cols] += jnp.sum(d_gate.astype(F32), axis=0, keepdims=True)


def slope_kernel(n_own, width, partial, arrived, first_ref, gate_ref, *refs):
    own, refs = refs[:n_own], refs[n_own:]
    d_first_ref, d_gate_ref, up_ref, sums_ref = refs

    @pl.when(pl.program_id(0) == 0)
    def _():
        sums_ref[...] = jnp.zeros_like(sums_ref)

    for j, x in enumerate(own):
        cols = slice(j * width, (j + 1) * width)
        dy = partial[:, cols] + arrived[:, cols].astype(F32)
        d_first, d_gate, up, _ = slopes(dy, x[...].astype(F32), first_ref[:, cols], gate_ref[:, cols])
        d_first_ref[:, cols] = d_first
        d_gate_ref[:, cols] = d_gate
        up_ref[:, cols] = up
        sums_ref[0:1, cols] += jnp.sum(d_first.astype(F32), axis=0, keepdims=True)
        sums_ref[1:2, cols] += jnp.sum(d_gate.astype(F32), axis=0, keepdims=True)


def back_kernel(half, n_pieces, with_up, table_ref, d_first, d_gate, *refs):
    if with_up:
        up, refs = refs[0], refs[1:]
    pieces, refs = refs[:n_pieces], refs[n_pieces:]
    out_ref, weight, sems = refs

    @pl.when(pl.program_id(0) == 0)
    def _():
        load_pieces(table_ref, pieces, weight, sems, half)

    width = min(512, out_ref.shape[1])
    for j in range(out_ref.shape[1] // width):
        cols = slice(j * width, (j + 1) * width)
        value = nt(d_first[...], weight[0, cols, :]) + nt(d_gate[...], weight[1, cols, :])
        if with_up:
            value = value + up[:, cols]
        out_ref[:, cols] = value.astype(out_ref.dtype)


def weight_grad_kernel(n_own, width, table_ref, *refs):
    xs, refs = refs[: 2 * n_own], refs[2 * n_own :]
    d_first, d_gate, refs = refs[0], refs[1], refs[2:]
    outs, turned = refs[:-1], refs[-1]
    rows = outs[0].shape[2]

    @pl.when(pl.program_id(0) == 0)
    def _():
        at = 0
        for x in xs:
            turned[at : at + x.shape[1], :] = x[...].T
            at += x.shape[1]

    blocks = d_first.shape[1] // width
    for side in range(2):
        row = table_ref[side, pl.program_id(0)]
        left = turned[pl.ds(pl.multiple_of(row, rows), rows), :]
        for j in range(blocks):
            cols = slice(j * width, (j + 1) * width)
            out = outs[side * blocks + j]
            out[0, 0] = nn(left, d_first[:, cols]).astype(BF16)
            out[0, 1] = nn(left, d_gate[:, cols]).astype(BF16)


SMEM_SPEC = pl.BlockSpec(memory_space=pltpu.SMEM)
ANY_SPEC = pl.BlockSpec(memory_space=pl.ANY)


def whole(array):
    return pl.BlockSpec(array.shape, lambda i: (0,) * array.ndim)


def by_rows(rows, width):
    return pl.BlockSpec((rows, width), lambda i: (i, 0))


def params(**kw):
    return pltpu.CompilerParams(vmem_limit_bytes=58 * MIB, **kw)


def count_of(pieces):
    return sum(piece.shape[0] for piece in pieces)


def cost(flops, *arrays):
    return pl.CostEstimate(flops=flops, bytes_accessed=sum(a.size * a.dtype.itemsize for a in arrays), transcendentals=0)


def highway_forward(table, pieces, bias, own, mate):
    words, width = own[0].shape
    half = width * len(own)
    rows = min(512, words)
    tile = by_rows(rows, width)
    out = by_rows(rows, half)
    return pl.pallas_call(
        functools.partial(forward_kernel, len(own), len(pieces), width),
        grid=(words // rows,),
        in_specs=[SMEM_SPEC, whole(bias)] + [tile] * (2 * len(own)) + [ANY_SPEC] * len(pieces),
        out_specs=[out] * 4,
        out_shape=[jax.ShapeDtypeStruct((words, half), kind) for kind in (F32, BF16, F32, F32)],
        scratch_shapes=[pltpu.VMEM((2, 2 * half, half), BF16), pltpu.SemaphoreType.DMA((count_of(pieces),))],
        compiler_params=params(),
        cost_estimate=cost(8 * words * half * half, *pieces, *own, *own, *own),
        name="highway_forward",
    )(table, bias, *own, *mate, *pieces)


def highway_turn(table, pieces, bias, own, mate, exact, out_grad, proj, width):
    words, half = own.shape
    rows = min(512, words)
    tile = by_rows(rows, half)
    return pl.pallas_call(
        functools.partial(turn_kernel, len(pieces), width),
        grid=(words // rows,),
        in_specs=[SMEM_SPEC, whole(bias), tile, tile, tile, by_rows(rows, out_grad.shape[1]), whole(proj)] + [ANY_SPEC] * len(pieces),
        out_specs=[tile, tile, tile, tile, pl.BlockSpec((2, half), lambda i: (0, 0))],
        out_shape=[jax.ShapeDtypeStruct((words, half), kind) for kind in (BF16, BF16, BF16, F32)] + [jax.ShapeDtypeStruct((2, half), F32)],
        scratch_shapes=[pltpu.VMEM((2, 2 * half, half), BF16), pltpu.SemaphoreType.DMA((count_of(pieces),))],
        compiler_params=params(),
        cost_estimate=cost(8 * words * half * half, *pieces, own, mate, exact, exact),
        name="highway_turn",
    )(table, bias, own, mate, exact, out_grad, proj, *pieces)


def highway_slopes(partial, arrived, first, gate, own):
    words, half = partial.shape
    width = own[0].shape[1]
    rows = min(256, words)
    tile = by_rows(rows, half)
    return pl.pallas_call(
        functools.partial(slope_kernel, len(own), width),
        grid=(words // rows,),
        in_specs=[tile] * 4 + [by_rows(rows, width)] * len(own),
        out_specs=[tile, tile, tile, pl.BlockSpec((2, half), lambda i: (0, 0))],
        out_shape=[jax.ShapeDtypeStruct((words, half), kind) for kind in (BF16, BF16, F32)] + [jax.ShapeDtypeStruct((2, half), F32)],
        compiler_params=params(),
        cost_estimate=cost(0, partial, partial, first, gate, arrived),
        name="highway_slopes",
    )(partial, arrived, first, gate, *own)


def highway_back(half, table, pieces, d_first, d_gate, up=None):
    words, width = d_first.shape
    rows = min(512, words)
    tile = by_rows(rows, width)
    ups = [] if up is None else [up]
    return pl.pallas_call(
        functools.partial(back_kernel, half, len(pieces), up is not None),
        grid=(words // rows,),
        in_specs=[SMEM_SPEC, tile, tile] + [tile] * len(ups) + [ANY_SPEC] * len(pieces),
        out_specs=tile,
        out_shape=jax.ShapeDtypeStruct((words, width), BF16 if up is None else F32),
        scratch_shapes=[pltpu.VMEM((2, width, width), BF16), pltpu.SemaphoreType.DMA((count_of(pieces),))],
        compiler_params=params(),
        cost_estimate=cost(4 * words * width * width, *pieces, d_first, d_gate),
        name="highway_back",
    )(table, d_first, d_gate, *ups, *pieces)


def highway_weight_grad(table, own, mate, d_first, d_gate, rows, width):
    words, half = d_first.shape
    xs = list(own) + list(mate)
    steps = table.shape[1]
    blocks = half // width
    block = pl.BlockSpec((1, 2, rows, width), lambda i: (i, 0, 0, 0))
    return pl.pallas_call(
        functools.partial(weight_grad_kernel, len(own), width),
        grid=(steps,),
        in_specs=[SMEM_SPEC] + [whole(x) for x in xs] + [whole(d_first), whole(d_gate)],
        out_specs=[block] * (2 * blocks),
        out_shape=[jax.ShapeDtypeStruct((steps, 2, rows, width), BF16)] * (2 * blocks),
        scratch_shapes=[pltpu.VMEM((2 * half, words), BF16)],
        compiler_params=params(),
        cost_estimate=cost(8 * words * half * half, *xs, d_first, d_gate, d_first, d_gate),
        name="highway_weight_grad",
    )(table, *xs, d_first, d_gate)


def adam_update(weight, grad, moment_one, moment_two, rate):
    first_new = beta_one * moment_one + (1 - beta_one) * grad
    second_new = beta_two * moment_two + (1 - beta_two) * grad * grad
    corrected_one = first_new / (1 - beta_one**STEP)
    corrected_two = second_new / (1 - beta_two**STEP)
    updated = weight - rate * (
        corrected_one / (jnp.sqrt(corrected_two) + adam_eps) + decay_rate * weight
    )
    return (second_new, updated)


def owner_kernel(at_ref, grad_in, weight, one, two, average, grad, second, new, average_new):
    value = grad_in[0].astype(F32)
    grad[...] = value
    second_new, updated = adam_update(weight[...], value, one[...], two[...], 0.02)
    second[...] = second_new
    new[...] = updated
    average_new[...] = average_keep * average[...] + (1 - average_keep) * updated


def owner_update(at, grads, weight, one, two, average):
    slots, rows, width = grads.shape[1:]
    part = min(128, rows)
    block = pl.BlockSpec((slots, part, width), lambda j, r, at: (0, r, at[j]))
    return pl.pallas_call(
        owner_kernel,
        grid_spec=pltpu.PrefetchScalarGridSpec(
            num_scalar_prefetch=1,
            grid=(grads.shape[0], rows // part),
            in_specs=[pl.BlockSpec((1, slots, part, width), lambda j, r, at: (j, 0, r, 0))] + [block] * 4,
            out_specs=[block] * 4,
        ),
        out_shape=[jax.ShapeDtypeStruct(weight.shape, F32)] * 4,
        compiler_params=params(),
        cost_estimate=cost(0, weight, weight, weight, weight, weight, weight, weight, weight),
        name="owner_update",
    )(at, grads, weight, one, two, average)


class Places:
    def __init__(self):
        self.n_filt, self.n_dp = lax.axis_size("filt"), lax.axis_size("dp")
        self.n_y, self.n_z = self.n_filt // 2, self.n_dp // 2
        self.f, self.d = lax.axis_index("filt"), lax.axis_index("dp")
        self.y, self.x = self.f // 2, self.f % 2
        self.z, self.c = self.d // 2, self.d % 2
        self.direct = self.n_y * self.n_z <= 8

    def over_filt(self, value, step):
        return lax.ppermute(value, "filt", [(i, i ^ step) for i in range(self.n_filt)])

    def over_x(self, value):
        return self.over_filt(value, 1)

    def over_y(self, value, step):
        return self.over_filt(value, 2 * step)

    def over_core(self, value):
        return lax.ppermute(value, "dp", [(i, i ^ 1) for i in range(self.n_dp)])

    def over_z(self, value, step):
        pairs = [(i, (i // 2 + step) % self.n_z * 2 + i % 2) for i in range(self.n_dp)]
        return lax.ppermute(value, "dp", pairs)

    def far_first(self):
        return sorted(range(1, self.n_z), key=lambda k: (min(k, self.n_z - k), k))

    def row_of(self, d, rows, width):
        f = d * rows // width
        half = self.n_y * width
        return (f % 2 ^ self.x) * half + (f // 2 ^ self.y) * width + d * rows % width


def gather_layer(place, piece):
    rows, width = piece.shape[1:]
    if place.direct:
        found = {0: piece}
        for k in place.far_first():
            found[k] = place.over_z(piece, k)
        pieces, at_rows, at_cols = [], [], []
        for k in [0] + place.far_first():
            for step in range(place.n_y):
                mine = found[k] if step == 0 else place.over_y(found[k], step)
                for other in range(2):
                    pieces.append((place.over_core(mine) if other else mine)[None])
                    d = (place.z - k) % place.n_z * 2 + (place.c ^ other)
                    at_rows.append(place.row_of(d, rows, width))
                    at_cols.append(jnp.int32(step * width))
        return pieces, jnp.stack([jnp.stack(at_rows), jnp.stack(at_cols)]).astype(jnp.int32), found
    spread = lax.all_gather(lax.all_gather(piece, "dp"), "filt")
    spread = spread.reshape((place.n_y, 2) + spread.shape[1:])
    spread = lax.dynamic_index_in_dim(spread, place.x, 1, keepdims=False)
    spread = spread.reshape((place.n_y * place.n_dp,) + piece.shape)
    d = jnp.tile(jnp.arange(place.n_dp, dtype=jnp.int32), place.n_y)
    y = jnp.repeat(jnp.arange(place.n_y, dtype=jnp.int32), place.n_dp)
    table = jnp.stack([place.row_of(d, rows, width), (y ^ place.y) * width]).astype(jnp.int32)
    return [spread], table, None


def sum_table(place, rows, width):
    z = jnp.arange(place.n_z, dtype=jnp.int32)
    z, c = ((place.z + z) % place.n_z, place.c) if place.direct else (z, 0)
    return jnp.stack([place.row_of(z * 2 + c, rows, width), place.row_of(z * 2 + (1 - c), rows, width)]).astype(jnp.int32)


def sum_layer(place, blocks):
    n_y = place.n_y
    near, far = blocks[:n_y], blocks[n_y:]
    if place.direct:
        arrived = {step: place.over_core(far[step]) for step in list(range(1, n_y)) + [0]}
        order = place.far_first()[::-1] + [0]
        both = lambda step, k: near[step][k].astype(F32) + arrived[step][k].astype(F32)
        turned = {}
        for k in order:
            turned[k] = [place.over_y(both(step, k).astype(BF16), step) for step in range(1, n_y)]
        total = None
        for k in order:
            value = both(0, k)
            for term in turned[k]:
                value = value + term.astype(F32)
            if k:
                value = place.over_z(value.astype(BF16), k).astype(F32)
            total = value if total is None else total + value
        return total
    steps = jnp.arange(n_y, dtype=jnp.int32) ^ place.y
    pairs = jnp.stack([jnp.stack(near), jnp.stack(far)], axis=2)
    pairs = jnp.take(pairs, steps, axis=0)
    pairs = pairs.reshape((n_y, place.n_dp) + pairs.shape[3:])
    mine = lax.psum_scatter(pairs, "dp", scatter_dimension=1)
    sides = jnp.arange(2, dtype=jnp.int32).reshape(1, 2, 1, 1, 1)
    mine = jnp.where(sides == place.x, mine[:, None], jnp.zeros((), BF16))
    mine = mine.reshape((place.n_filt,) + mine.shape[2:])
    return lax.psum_scatter(mine, "filt", scatter_dimension=0).astype(F32)


def per_device(
    char_ids,
    word_lengths,
    out_grad,
    highway_owner,
    char_table,
    conv_weight,
    conv_bias,
    highway_weight,
    proj_weight,
    dense_bias,
    table_moment_one,
    table_moment_two,
    conv_moment_one,
    conv_moment_two,
    conv_bias_moment_one,
    conv_bias_moment_two,
    highway_moment_one,
    highway_moment_two,
    highway_average,
    proj_moment_one,
    proj_moment_two,
    bias_moment_one,
    bias_moment_two,
):
    place = Places()
    n_y, n_filt = place.n_y, place.n_filt
    width = conv_weight.shape[1]
    rows, width_full = highway_weight.shape[1:]
    half = width_full // 2
    rows_proj, out_width = proj_weight.shape
    vocab_count = char_table.shape[0]
    words_dev = char_ids.shape[0]
    words_y = words_dev // n_y
    slot_index = unit_slots(highway_owner, SLOTS)

    def block_of(step):
        start = (place.f ^ step) * width
        return lax.dynamic_slice_in_dim(highway_weight, start, width, axis=2).astype(BF16)

    from_owner = [block_of(0)] + [place.over_filt(block_of(step), step) for step in range(1, n_filt)]

    def unit_block(unit):
        chosen = from_owner[0][0]
        for step in range(n_filt):
            for slot in range(SLOTS):
                here = slot_index[unit] == (place.f ^ step) * SLOTS + slot
                chosen = jnp.where(here, from_owner[step][slot], chosen)
        return chosen

    layer_blocks = [jnp.stack([unit_block(2 * layer), unit_block(2 * layer + 1)]) for layer in range(2)]
    gathered = [None, None]
    pieces, table, found = gather_layer(place, layer_blocks[0])
    gathered[0] = (pieces, table)
    second = layer_blocks[1]
    if found is not None:
        second, _ = lax.optimization_barrier((second, found[place.far_first()[-1]]))
    pieces, table, _ = gather_layer(place, second)
    gathered[1] = (pieces, table)

    proj_rows = lax.all_gather(proj_weight.astype(BF16), "dp", axis=0, tiled=True)
    proj_half = jnp.concatenate([proj_rows] + [place.over_y(proj_rows, step) for step in range(1, n_y)], axis=0)
    grad_mate = place.over_x(out_grad)
    mine_first = place.x == 0
    out_grad_y = jnp.concatenate([jnp.where(mine_first, out_grad, grad_mate), jnp.where(mine_first, grad_mate, out_grad)], axis=0)

    bias_float = lax.reduce_precision(dense_bias, 8, 7)

    def half_bias(unit):
        whole_bias = bias_float[unit * width_full : (unit + 1) * width_full].reshape(n_filt, width)
        return jnp.concatenate([lax.dynamic_index_in_dim(whole_bias, 2 * (place.y ^ step) + place.x, 0, keepdims=False) for step in range(n_y)])

    layer_bias = [jnp.stack([half_bias(2 * layer), half_bias(2 * layer + 1)]) for layer in range(2)]

    widths = channel_widths(place.f * width, width, FILTERS)
    offsets = jnp.arange(TAPS, dtype=jnp.int32) // CHAR_DIM
    tap_mask = (offsets[:, None] < widths[None, :]).astype(jnp.float32)
    cblock = min(256, width)
    rank, data, table_t, conv_t, conv_back, width_col, narrow = conv_operands(
        char_ids, word_lengths, char_table, conv_weight, conv_bias, widths, cblock
    )
    feature_rows, lse, sorted_ids = conv_forward(rank, data, table_t, conv_t, width_col, narrow, cblock)
    rank_parts = [lax.dynamic_slice_in_dim(rank, (place.y ^ step) * words_y, words_y, axis=0) for step in range(n_y)]
    placed = {step: place_words(rank_parts[step], feature_rows) for step in list(range(1, n_y)) + [0]}
    own = [placed[0]] + [place.over_y(placed[step], step) for step in range(1, n_y)]
    mate = [place.over_x(part) for part in own]

    x_one, x_one_low, first_zero, gate_zero = highway_forward(gathered[0][1], gathered[0][0], layer_bias[0], own, mate)
    x_one_mate = place.over_x(x_one_low)
    x_two_low, d_first, d_gate, up, sums_one = highway_turn(
        gathered[1][1], gathered[1][0], layer_bias[1], x_one_low, x_one_mate, x_one, out_grad_y, proj_half, width
    )
    targets = sum_table(place, rows, width)
    layer_sums = [None, None]
    leaving = highway_back(1, gathered[1][1], gathered[1][0], d_first, d_gate)
    arrived = place.over_x(leaving)
    blocks = highway_weight_grad(targets, [x_one_low], [x_one_mate], d_first, d_gate, rows, width)
    layer_sums[1] = sum_layer(place, blocks)
    partial = highway_back(0, gathered[1][1], gathered[1][0], d_first, d_gate, up)

    vectors = nn(x_two_low, proj_half)
    vectors_two = vectors.reshape(2, words_y // 2, out_width)
    vectors_away = lax.dynamic_index_in_dim(vectors_two, 1 - place.x, 0, keepdims=False).astype(BF16)
    vectors_here = lax.dynamic_index_in_dim(vectors_two, place.x, 0, keepdims=False)
    word_vectors = vectors_here + place.over_x(vectors_away).astype(F32) + bias_float[UNITS * width_full :]
    proj_part = tn(x_two_low, out_grad_y).reshape(n_y, width, out_width)
    proj_sum = proj_part[0]
    for step in range(1, n_y):
        proj_sum = proj_sum + place.over_y(proj_part[step].astype(BF16), step).astype(F32)
    proj_grad = lax.psum_scatter(proj_sum, "dp", scatter_dimension=0, tiled=True)

    d_first, d_gate, up, sums_zero = highway_slopes(partial, arrived, first_zero, gate_zero, own)
    leaving = highway_back(1, gathered[0][1], gathered[0][0], d_first, d_gate)
    arrived = place.over_x(leaving)
    blocks = highway_weight_grad(targets, own, mate, d_first, d_gate, rows, width)
    layer_sums[0] = sum_layer(place, blocks)
    partial = highway_back(0, gathered[0][1], gathered[0][0], d_first, d_gate, up)
    feature_grad = [(partial[:, step * width : (step + 1) * width] + arrived[:, step * width : (step + 1) * width].astype(F32)).astype(BF16) for step in range(n_y)]
    returned = [feature_grad[0]] + [place.over_y(feature_grad[step], step) for step in range(1, n_y)]

    conv_sums, table_sums = conv_backward(
        rank_parts, sorted_ids, table_t, conv_t, conv_back, width_col, narrow, lse, returned, cblock
    )
    table_local = (table_sums[:CHAR_DIM] + table_sums[CHAR_DIM:]).T[:vocab_count]
    conv_sums = lax.psum(conv_sums, "dp")
    conv_grad, conv_bias_grad = conv_sums[:, :TAPS].T * tap_mask, conv_sums[:, TAPS]

    home = jnp.arange(n_filt, dtype=jnp.int32)

    def natural(values):
        parts = values.reshape(n_y, 1, width)
        out = jnp.zeros((n_filt, width), F32)
        for step in range(n_y):
            out = jnp.where((home == 2 * (place.y ^ step) + place.x)[:, None], parts[step], out)
        return out.reshape(-1)

    bias_local = jnp.concatenate(
        [natural(sums[unit]) for sums in (sums_zero, sums_one) for unit in range(2)] + [jnp.sum(out_grad, axis=0, dtype=F32)]
    )
    table_grad, bias_grad = lax.psum((table_local, bias_local), ("filt", "dp"))

    units = [layer_sums[unit // 2][unit % 2].astype(BF16) for unit in range(UNITS)]

    def for_owner(step):
        slots = []
        for slot in range(SLOTS):
            value = jnp.zeros_like(units[0])
            for unit in range(UNITS):
                value = jnp.where(slot_index[unit] == (place.f ^ step) * SLOTS + slot, units[unit], value)
            slots.append(value)
        return jnp.stack(slots)

    slot_grads = [for_owner(0)] + [place.over_filt(for_owner(step), step) for step in range(1, n_filt)]
    columns = place.f ^ jnp.arange(n_filt, dtype=jnp.int32)
    highway_grad, highway_second, highway_new, highway_average_new = owner_update(
        columns, jnp.stack(slot_grads), highway_weight, highway_moment_one, highway_moment_two, highway_average
    )
    table_second, table_new = adam_update(
        char_table, table_grad, table_moment_one, table_moment_two, 1.0
    )
    conv_second, conv_new = adam_update(
        conv_weight, conv_grad, conv_moment_one, conv_moment_two, 0.1
    )
    conv_bias_second, conv_bias_new = adam_update(
        conv_bias, conv_bias_grad, conv_bias_moment_one, conv_bias_moment_two, 0.3
    )
    proj_second, proj_new = adam_update(
        proj_weight, proj_grad, proj_moment_one, proj_moment_two, 0.02
    )
    bias_second, bias_new = adam_update(
        dense_bias, bias_grad, bias_moment_one, bias_moment_two, 0.3
    )
    return (
        word_vectors,
        table_grad,
        table_second,
        table_new,
        conv_grad,
        conv_second,
        conv_new,
        conv_bias_grad,
        conv_bias_second,
        conv_bias_new,
        highway_grad,
        highway_second,
        highway_new,
        highway_average_new,
        proj_grad,
        proj_second,
        proj_new,
        bias_grad,
        bias_second,
        bias_new,
    )


def solution(mesh):
    return jax.shard_map(
        per_device,
        mesh=mesh,
        in_specs=(
            P("dp", None),
            P("dp"),
            P(("dp", "filt"), None),
            P(),
            P(),
            P(None, "filt"),
            P("filt"),
            P("filt", "dp", None),
            P(("filt", "dp"), None),
            P(),
            P(),
            P(),
            P(None, "filt"),
            P(None, "filt"),
            P("filt"),
            P("filt"),
            P("filt", "dp", None),
            P("filt", "dp", None),
            P("filt", "dp", None),
            P(("filt", "dp"), None),
            P(("filt", "dp"), None),
            P(),
            P(),
        ),
        out_specs=(
            P(("dp", "filt"), None),
            P(),
            P(),
            P(),
            P(None, "filt"),
            P(None, "filt"),
            P(None, "filt"),
            P("filt"),
            P("filt"),
            P("filt"),
            P("filt", "dp", None),
            P("filt", "dp", None),
            P("filt", "dp", None),
            P("filt", "dp", None),
            P(("filt", "dp"), None),
            P(("filt", "dp"), None),
            P(("filt", "dp"), None),
            P(),
            P(),
            P(),
        ),
        check_vma=False,
    )
```

```python
import functools

import jax
import jax.numpy as jnp
from jax import lax
from jax.experimental import pallas as pl
from jax.experimental.pallas import tpu as pltpu
from jax.sharding import PartitionSpec as P

CHAR_DIM = 16
MAX_CHARS = 50
MAX_WIDTH = 7
FILTERS = 2048
UNITS = 4
SLOTS = 2
STEP = 10
TAPS = MAX_WIDTH * CHAR_DIM
DEPTH = 128
ID_SHIFT = 128
ID_ROWS = 64
SLOTS_E = MAX_CHARS + MAX_WIDTH - 1 + 8
LANES = 128
STEP_P = 4
ROWS = 256
beta_one = 0.9
beta_two = 0.999
adam_eps = 1e-08
decay_rate = 0.01
average_keep = 0.9
F32, BF16 = jnp.float32, jnp.bfloat16
MIB = 1 << 20


def lasting(us):
    return pl.CostEstimate(flops=int(us * 1e7), bytes_accessed=int(us * 3e4), transcendentals=0)


def nt(a, b):
    return lax.dot_general(a, b, (((1,), (1,)), ((), ())), preferred_element_type=F32)


def nn(a, b):
    return lax.dot_general(a, b, (((1,), (0,)), ((), ())), preferred_element_type=F32)


def tn(a, b):
    return lax.dot_general(a, b, (((0,), (0,)), ((), ())), preferred_element_type=F32)


def embed_tile(ids_ref, table_ref, lens, e_ref, longest):
    tile = lens.shape[1]
    e_ref[...] = jnp.zeros_like(e_ref)
    pieces = table_ref.shape[1] // LANES

    def fill(s, carry):
        for i in range(STEP_P):
            p = s * STEP_P + i
            row = ids_ref[pl.ds(p, 1), :].astype(jnp.int32)
            parts = []
            for lane in range(tile // LANES):
                idx = jnp.broadcast_to(row[:, lane * LANES : (lane + 1) * LANES], (CHAR_DIM, LANES))
                low = jnp.bitwise_and(idx, LANES - 1)
                value = jnp.zeros((CHAR_DIM, LANES), F32)
                for piece in range(pieces):
                    got = jnp.take_along_axis(table_ref[:, piece * LANES : (piece + 1) * LANES], low, axis=1)
                    value = jnp.where(lax.shift_right_logical(idx, 7) == piece, got, value)
                parts.append(value)
            value = jnp.concatenate(parts, axis=1) if len(parts) > 1 else parts[0]
            value = jnp.where(p < lens, value, 0.0)
            e_ref[pl.ds(pl.multiple_of(p * CHAR_DIM, CHAR_DIM), CHAR_DIM), :] = value.astype(BF16)
        return carry

    lax.fori_loop(0, (longest + STEP_P - 1) // STEP_P, fill, 0)


def limits_of(lens):
    row = lax.broadcasted_iota(jnp.int32, (CHAR_DIM, lens.shape[1]), 0)
    past = jnp.maximum(lens - (row - 2), 0)
    return jnp.where(row < 3, -1, jnp.where(row < 3 + MAX_WIDTH, past, 1 << 20))


def window_at(e_ref, limit, p):
    extra = jnp.where(p > limit, 1.0, 0.0).astype(BF16)
    taps = e_ref[pl.ds(pl.multiple_of(p * CHAR_DIM, CHAR_DIM), TAPS), :]
    return jnp.concatenate([taps, extra], axis=0)


SUB = 32


def windows_at(e_ref, limit, s):
    return jnp.concatenate([window_at(e_ref, limit, s * STEP_P + i) for i in range(STEP_P)], axis=1)


def steps_of(longest, narrow):
    return (jnp.maximum(longest - narrow, 0) + STEP_P) // STEP_P


def conv_forward_kernel(cblock, base, narrow_ref, rank_ref, data_ref, table_ref, conv_ref, width_ref, feat_ref, lse_ref, ids_ref, e_ref, top, total, pre):
    tile = ids_ref.shape[1]
    words = rank_ref.shape[0]
    first = (base + pl.program_id(0)) * tile
    lane = first + lax.broadcasted_iota(jnp.int32, (words, tile), 1)
    hot = jnp.where(rank_ref[...] == lane, 1.0, 0.0).astype(BF16)
    moved = nn(data_ref[...], hot)
    shift = jnp.where(lax.broadcasted_iota(jnp.int32, moved.shape, 0) < MAX_CHARS, float(ID_SHIFT), 0.0)
    moved = moved + shift
    ids_ref[...] = moved
    lens = (moved[MAX_CHARS : MAX_CHARS + 1, :] + 0.5).astype(jnp.int32)
    longest = jnp.max(lens)
    embed_tile(ids_ref, table_ref, lens, e_ref, longest)
    limit = limits_of(lens)
    channels = conv_ref.shape[0]
    for block in range(channels // cblock):
        rows = pl.ds(block * cblock, cblock)
        top[...] = jnp.full_like(top, -1e30)
        total[...] = jnp.zeros_like(total)

        def step(s, carry):
            pre[...] = nn(conv_ref[rows, :], windows_at(e_ref, limit, s))
            for sub in range(0, cblock, SUB):
                part = slice(sub, sub + SUB)
                values = [pre[part, i * tile : (i + 1) * tile] for i in range(STEP_P)]
                before = top[part, :]
                best = functools.reduce(jnp.maximum, values, before)
                top[part, :] = best
                total[part, :] = total[part, :] * jnp.exp(before - best) + sum(jnp.exp(value - best) for value in values)
            return carry

        lax.fori_loop(0, steps_of(longest, narrow_ref[block]), step, 0)
        span = jnp.maximum(lens - width_ref[rows, :], 0)
        lse = top[...] + jnp.log(total[...])
        lse_ref[rows, :] = lse
        pooled = lse - jnp.log((span + 1).astype(F32))
        feat_ref[rows, :] = (pooled * jax.nn.sigmoid(pooled)).astype(BF16)


def place_kernel(rank_ref, *refs):
    feats, out_ref = refs[:-1], refs[-1]
    total, base = 0.0, 0
    for feat_ref in feats:
        shape = (rank_ref.shape[0], feat_ref.shape[1])
        lane = base + lax.broadcasted_iota(jnp.int32, shape, 1)
        hot = jnp.where(rank_ref[...] == lane, 1.0, 0.0).astype(BF16)
        total = total + nt(hot, feat_ref[...])
        base += shape[1]
    out_ref[...] = total.astype(BF16)


def conv_forward(rank, data, table_t, conv_t, widths, narrow, cblock, base, count):
    words, channels = rank.shape[0], conv_t.shape[0]
    tile = min(256, words)
    span = count * tile
    full = lambda *shape: pl.BlockSpec(shape, lambda i: (0,) * len(shape))
    column = lambda depth: pl.BlockSpec((depth, tile), lambda i: (0, i))
    return pl.pallas_call(
        functools.partial(conv_forward_kernel, cblock, base),
        grid=(count,),
        in_specs=[
            pl.BlockSpec(memory_space=pltpu.SMEM),
            full(words, 1),
            full(*data.shape),
            full(*table_t.shape),
            full(*conv_t.shape),
            full(channels, 1),
        ],
        out_specs=[column(channels), column(channels), column(ID_ROWS), column(SLOTS_E * CHAR_DIM)],
        out_shape=[
            jax.ShapeDtypeStruct((channels, span), BF16),
            jax.ShapeDtypeStruct((channels, span), F32),
            jax.ShapeDtypeStruct((ID_ROWS, span), F32),
            jax.ShapeDtypeStruct((SLOTS_E * CHAR_DIM, span), BF16),
        ],
        scratch_shapes=[
            pltpu.VMEM((cblock, tile), F32),
            pltpu.VMEM((cblock, tile), F32),
            pltpu.VMEM((cblock, STEP_P * tile), F32),
        ],
        compiler_params=pltpu.CompilerParams(vmem_limit_bytes=48 * MIB),
        cost_estimate=lasting(11),
        name="conv_forward",
    )(narrow, rank, data, table_t, conv_t, widths)


def place_words(rank, feats):
    words, channels = rank.shape[0], feats[0].shape[0]
    rows = min(256, words)
    return pl.pallas_call(
        place_kernel,
        grid=(words // rows,),
        in_specs=[pl.BlockSpec((rows, 1), lambda i: (i, 0))] + [pl.BlockSpec(feat.shape, lambda i: (0, 0)) for feat in feats],
        out_specs=pl.BlockSpec((rows, channels), lambda i: (i, 0)),
        out_shape=jax.ShapeDtypeStruct((words, channels), BF16),
        compiler_params=pltpu.CompilerParams(vmem_limit_bytes=48 * MIB),
        cost_estimate=lasting(4),
        name="place_words",
    )(rank, *feats)


def conv_backward_kernel(cblock, n_parts, base, narrow_ref, ids_ref, e_ref, conv_ref, back_ref, width_ref, lse_ref, *refs):
    ranks, grads, refs = refs[:n_parts], refs[n_parts : 2 * n_parts], refs[2 * n_parts :]
    so_far, sums_ref, table_grad_ref, de_ref, dpool, pre, d_pre, found = refs
    tile = ids_ref.shape[1]
    vocab = table_grad_ref.shape[0]
    channels = conv_ref.shape[0]
    first = (base + pl.program_id(0)) * tile

    @pl.when(pl.program_id(0) == 0)
    def _():
        sums_ref[...] = so_far[...]
        table_grad_ref[...] = jnp.zeros_like(table_grad_ref)

    lens = (ids_ref[MAX_CHARS : MAX_CHARS + 1, :] + 0.5).astype(jnp.int32)
    longest = jnp.max(lens)
    limit = limits_of(lens)
    de_ref[...] = jnp.zeros_like(de_ref)
    moved = 0.0
    for rank_ref, grad_ref in zip(ranks, grads):
        row = first + lax.broadcasted_iota(jnp.int32, (tile, rank_ref.shape[1]), 0)
        moved = moved + nn(jnp.where(rank_ref[...] == row, 1.0, 0.0).astype(BF16), grad_ref[...])
    moved = moved.T
    for block in range(channels // cblock):
        rows = slice(block * cblock, (block + 1) * cblock)
        span = jnp.maximum(lens - width_ref[rows, :], 0)
        pooled = lse_ref[rows, :] - jnp.log((span + 1).astype(F32))
        sigma = jax.nn.sigmoid(pooled)
        dpool[...] = moved[rows, :] * (sigma + pooled * sigma * (1 - sigma))

        def step(s, carry):
            windows = windows_at(e_ref, limit, s)
            pre[...] = nn(conv_ref[rows, :], windows)
            for sub in range(0, cblock, SUB):
                part = slice(sub, sub + SUB)
                low, scale = lse_ref[block * cblock + sub : block * cblock + sub + SUB, :], dpool[part, :]
                for i in range(STEP_P):
                    cols = slice(i * tile, (i + 1) * tile)
                    d_pre[part, cols] = (jnp.exp(pre[part, cols] - low) * scale).astype(BF16)
            back = nn(back_ref[:, rows], d_pre[...])
            for i in range(STEP_P):
                at = pl.ds(pl.multiple_of((s * STEP_P + i) * CHAR_DIM, CHAR_DIM), TAPS)
                de_ref[at, :] += back[:TAPS, i * tile : (i + 1) * tile]
            sums_ref[rows, :] += nt(d_pre[...], windows)
            return carry

        lax.fori_loop(0, steps_of(longest, narrow_ref[block]), step, 0)

    letter = lax.broadcasted_iota(jnp.int32, (vocab, tile), 0)

    def spread(s, carry):
        parts = []
        for i in range(STEP_P):
            p = s * STEP_P + i
            at = pl.ds(pl.multiple_of(p * CHAR_DIM, CHAR_DIM), CHAR_DIM)
            value = jnp.where(p < lens, de_ref[at, :], 0.0)
            high = value.astype(BF16)
            parts.append(jnp.concatenate([high, (value - high.astype(F32)).astype(BF16)], axis=0))
            row = ids_ref[pl.ds(p, 1), :].astype(jnp.int32)
            found[:, i * tile : (i + 1) * tile] = jnp.where(letter == row, 1.0, 0.0).astype(BF16)
        table_grad_ref[...] += nt(found[...], jnp.concatenate(parts, axis=1))
        return carry

    lax.fori_loop(0, (longest + STEP_P - 1) // STEP_P, spread, 0)

    @pl.when(pl.program_id(0) == pl.num_programs(0) - 1)
    def _():
        both = table_grad_ref[...].T
        total = both[:CHAR_DIM] + both[CHAR_DIM:]
        for piece in range(vocab // LANES):
            at = channels + piece * CHAR_DIM
            sums_ref[at : at + CHAR_DIM, :] += total[:, piece * LANES : (piece + 1) * LANES]


def conv_backward(ranks, ids, embedded, vocab, conv_t, conv_back, widths, narrow, lse, grads, cblock, base, tile, so_far):
    channels, words = conv_t.shape[0], ids.shape[1]
    full = lambda *shape: pl.BlockSpec(shape, lambda i: (0,) * len(shape))
    return pl.pallas_call(
        functools.partial(conv_backward_kernel, cblock, len(ranks), base),
        grid=(words // tile,),
        in_specs=[
            pl.BlockSpec(memory_space=pltpu.SMEM),
            pl.BlockSpec((ID_ROWS, tile), lambda i: (0, i)),
            pl.BlockSpec((SLOTS_E * CHAR_DIM, tile), lambda i: (0, i)),
            full(*conv_t.shape),
            full(*conv_back.shape),
            full(channels, 1),
            pl.BlockSpec((channels, tile), lambda i: (0, i)),
        ]
        + [full(*part.shape) for part in ranks]
        + [full(*part.shape) for part in grads]
        + [full(*so_far.shape)],
        out_specs=full(*so_far.shape),
        out_shape=jax.ShapeDtypeStruct(so_far.shape, F32),
        scratch_shapes=[
            pltpu.VMEM((vocab, 2 * CHAR_DIM), F32),
            pltpu.VMEM((SLOTS_E * CHAR_DIM, tile), F32),
            pltpu.VMEM((cblock, tile), F32),
            pltpu.VMEM((cblock, STEP_P * tile), F32),
            pltpu.VMEM((cblock, STEP_P * tile), BF16),
            pltpu.VMEM((vocab, STEP_P * tile), BF16),
        ],
        compiler_params=pltpu.CompilerParams(vmem_limit_bytes=48 * MIB),
        cost_estimate=lasting(15),
        name="conv_backward",
    )(narrow, ids, embedded, conv_t, conv_back, widths, lse, *ranks, *grads, so_far)


def word_order(lengths):
    count = lengths.shape[0]
    key = lengths * count - jnp.arange(count, dtype=jnp.int32)
    return jnp.sum((key[None, :] > key[:, None]).astype(jnp.int32), axis=1, keepdims=True)


def conv_operands(char_ids, lengths, char_table, conv_weight, conv_bias, widths, cblock):
    words = char_ids.shape[0]
    channels = conv_weight.shape[1]
    vocab = char_table.shape[0]
    lanes = -(-vocab // LANES) * LANES
    rank = word_order(lengths)
    data = jnp.concatenate([char_ids.T - ID_SHIFT, lengths[None, :]], axis=0)
    data = jnp.pad(data, ((0, ID_ROWS - MAX_CHARS - 1), (0, 0))).astype(BF16)
    offsets = jnp.arange(TAPS, dtype=jnp.int32) // CHAR_DIM
    taps = jnp.where(offsets[:, None] < widths[None, :], conv_weight, 0.0).astype(BF16)
    parts, rest = [], conv_bias
    for _ in range(3):
        part = lax.reduce_precision(rest, 8, 7)
        parts.append(part)
        rest = rest - part
    kinds = jnp.arange(1, MAX_WIDTH + 1, dtype=jnp.int32)
    spans = jnp.where(kinds[:, None] == widths[None, :], -1e30, 0.0)
    under = jnp.concatenate([jnp.stack(parts), spans, jnp.zeros((DEPTH - TAPS - 3 - MAX_WIDTH, channels), F32)])
    conv_all = jnp.concatenate([taps, under.astype(BF16)])
    conv_back = jnp.pad(taps, ((0, DEPTH - TAPS), (0, 0)))
    table_t = jnp.pad(lax.reduce_precision(char_table, 8, 7).T, ((0, 0), (0, lanes - vocab)))
    narrow = widths[::cblock]
    return rank, data, table_t, conv_all.T, conv_back, widths[:, None], narrow


def channel_widths(start, count, whole):
    channel = start + jnp.arange(count, dtype=jnp.int32)
    widths = jnp.ones((count,), jnp.int32)
    for power in range(6):
        widths = widths + (channel >= whole * 2**power // 64).astype(jnp.int32)
    return widths


def unit_slots(owners, slots_each):
    order = jnp.arange(owners.shape[0], dtype=jnp.int32)
    before = (owners[:, None] == owners[None, :]) & (order[:, None] > order[None, :])
    return owners * slots_each + jnp.sum(before.astype(jnp.int32), axis=1)


def load_pieces(table_ref, pieces, rows, dest, sems, half=None, proj=None):
    cols = pieces[0].shape[3]
    depth = dest.shape[1]

    def each(act):
        at = 0
        for ref in pieces:
            for j in range(ref.shape[0]):
                row, col = table_ref[0, at], table_ref[1, at]
                row = row if half is None else row - half * depth
                sem = sems.at[at]

                def go(ref=ref, j=j, row=row, col=col, sem=sem):
                    place = (slice(None), pl.ds(pl.multiple_of(row, rows), rows), pl.ds(pl.multiple_of(col, cols), cols))
                    act(pltpu.make_async_copy(ref.at[j, :, :rows, :], dest.at[place], sem))

                if half is None:
                    go()
                else:
                    pl.when((row >= 0) & (row < depth))(go)
                if proj is not None:
                    under = ref.shape[2] - rows
                    part = proj[0].shape[1] // 2
                    to = pl.ds(pl.multiple_of(table_ref[2, at], under), under)
                    for side in range(2):
                        source = ref.at[j, side, rows:, :part]
                        act(pltpu.make_async_copy(source, proj[0].at[to, side * part : (side + 1) * part], proj[1].at[2 * at + side]))
                at += 1

    each(lambda copy: copy.start())
    each(lambda copy: copy.wait())


def hidden_of(xs, weight, unit, cols, bias_ref):
    at, total = 0, None
    for x in xs:
        term = nn(x[...], weight[unit, at : at + x.shape[1], cols])
        total = term if total is None else total + term
        at += x.shape[1]
    return total + bias_ref[unit : unit + 1, cols]


def sigmoid(value):
    return 0.5 * jnp.tanh(0.5 * value) + 0.5


def factors(x, a, g):
    s = sigmoid(a)
    gate = sigmoid(g)
    nonlinear = a * s
    left = 1 - gate
    gap = x - nonlinear
    return nonlinear + gate * gap, left * (s + nonlinear * (1 - s)), gap * gate * left, gate


def forward_kernel(n_own, n_pieces, rows, width, table_ref, bias_ref, *refs):
    own, refs = refs[:n_own], refs[n_own:]
    mate, refs = refs[:n_own], refs[n_own:]
    pieces, refs = refs[:n_pieces], refs[n_pieces:]
    next_ref, low_ref, first_ref, second_ref, gate_ref, weight, sems = refs

    @pl.when(pl.program_id(0) == 0)
    def _():
        load_pieces(table_ref, pieces, rows, weight, sems)

    for j, x in enumerate(own):
        cols = slice(j * width, (j + 1) * width)
        a = hidden_of(own + mate, weight, 0, cols, bias_ref)
        g = hidden_of(own + mate, weight, 1, cols, bias_ref)
        value, first, second, gate = factors(x[...].astype(F32), a, g)
        next_ref[:, cols] = value
        low_ref[:, cols] = value.astype(BF16)
        first_ref[:, cols] = first.astype(BF16)
        second_ref[:, cols] = second.astype(BF16)
        gate_ref[:, cols] = gate.astype(BF16)


def column_sums(sums_ref, cols, d_first, d_gate):
    sums_ref[0:1, cols] += jnp.sum(d_first.astype(F32), axis=0, keepdims=True)
    sums_ref[1:2, cols] += jnp.sum(d_gate.astype(F32), axis=0, keepdims=True)


def product_back(out_ref, d_first, d_gate, weight, base, up=None):
    width = min(512, out_ref.shape[1])
    for j in range(out_ref.shape[1] // width):
        cols = slice(j * width, (j + 1) * width)
        rows = slice(base + j * width, base + (j + 1) * width)
        value = nt(d_first[...], weight[0, rows, :]) + nt(d_gate[...], weight[1, rows, :])
        if up is not None:
            value = value + up[:, cols]
        out_ref[:, cols] = value.astype(out_ref.dtype)


def turn_kernel(n_pieces, rows, width, packed, table_ref, bias_ref, own, mate, exact, out_grad, *refs):
    if packed:
        pieces, refs = refs[:n_pieces], refs[n_pieces:]
        low_ref, d_first_ref, d_gate_ref, up_ref, leaving_ref, vectors_ref, sums_ref, weight, sems, proj, proj_sems = refs
        proj_rows = (proj, proj_sems)
    else:
        proj, pieces, refs = refs[0], refs[1 : n_pieces + 1], refs[n_pieces + 1 :]
        low_ref, d_first_ref, d_gate_ref, up_ref, leaving_ref, vectors_ref, sums_ref, weight, sems = refs
        proj_rows = None

    @pl.when(pl.program_id(0) == 0)
    def _():
        load_pieces(table_ref, pieces, rows, weight, sems, None, proj_rows)
        sums_ref[...] = jnp.zeros_like(sums_ref)

    half = own.shape[1]
    for j in range(half // width):
        cols = slice(j * width, (j + 1) * width)
        a = hidden_of((own, mate), weight, 0, cols, bias_ref)
        g = hidden_of((own, mate), weight, 1, cols, bias_ref)
        dy = nt(out_grad[...], proj[cols, :])
        value, first, second, gate = factors(exact[:, cols], a, g)
        low_ref[:, cols] = value.astype(BF16)
        d_first, d_gate = (dy * first).astype(BF16), (dy * second).astype(BF16)
        d_first_ref[:, cols] = d_first
        d_gate_ref[:, cols] = d_gate
        up_ref[:, cols] = dy * gate
        column_sums(sums_ref, cols, d_first, d_gate)
    product_back(leaving_ref, d_first_ref, d_gate_ref, weight, half)
    vectors_ref[...] = nn(low_ref[...], proj[...])


def slope_kernel(n_pieces, rows, width, table_ref, partial, arrived, first_ref, second_ref, gate_ref, *refs):
    pieces, refs = refs[:n_pieces], refs[n_pieces:]
    d_first_ref, d_gate_ref, up_ref, leaving_ref, sums_ref, weight, sems = refs

    @pl.when(pl.program_id(0) == 0)
    def _():
        load_pieces(table_ref, pieces, rows, weight, sems, 1)
        sums_ref[...] = jnp.zeros_like(sums_ref)

    for j in range(partial.shape[1] // width):
        cols = slice(j * width, (j + 1) * width)
        dy = partial[:, cols] + arrived[:, cols].astype(F32)
        d_first, d_gate = (dy * first_ref[:, cols].astype(F32)).astype(BF16), (dy * second_ref[:, cols].astype(F32)).astype(BF16)
        d_first_ref[:, cols] = d_first
        d_gate_ref[:, cols] = d_gate
        up_ref[:, cols] = dy * gate_ref[:, cols].astype(F32)
        column_sums(sums_ref, cols, d_first, d_gate)
    product_back(leaving_ref, d_first_ref, d_gate_ref, weight, 0)


def back_kernel(n_pieces, rows, table_ref, d_first, d_gate, up, *refs):
    pieces, refs = refs[:n_pieces], refs[n_pieces:]
    out_ref, weight, sems = refs

    @pl.when(pl.program_id(0) == 0)
    def _():
        load_pieces(table_ref, pieces, rows, weight, sems, 0)

    product_back(out_ref, d_first, d_gate, weight, 0, up)


def weight_grad_kernel(n_chunks, n_cols, n_d, width, table_ref, *refs):
    xs, refs = refs[: n_chunks * n_cols], refs[n_chunks * n_cols :]
    d_first, d_gate, refs = refs[:n_d], refs[n_d : 2 * n_d], refs[2 * n_d :]
    outs, turned = refs[:-1], refs[-1]
    rows = outs[0].shape[2]

    @pl.when(pl.program_id(0) == 0)
    def _():
        word = 0
        for chunk in range(n_chunks):
            at = 0
            for x in xs[chunk * n_cols : (chunk + 1) * n_cols]:
                turned[at : at + x.shape[1], word : word + x.shape[0]] = x[...].T
                at += x.shape[1]
            word += x.shape[0]

    blocks = d_first[0].shape[1] // width
    for side in range(2):
        row = table_ref[side, pl.program_id(0)]
        left = turned[pl.ds(pl.multiple_of(row, rows), rows), :]
        for j in range(blocks):
            cols = slice(j * width, (j + 1) * width)
            out = outs[blocks].at[j] if side else outs[j]
            for unit, ds in enumerate((d_first, d_gate)):
                total, word = 0.0, 0
                for d in ds:
                    total = total + nn(left[:, word : word + d.shape[0]], d[:, cols])
                    word += d.shape[0]
                out[0, unit] = total.astype(BF16)


SMEM_SPEC = pl.BlockSpec(memory_space=pltpu.SMEM)
ANY_SPEC = pl.BlockSpec(memory_space=pl.ANY)


def whole(array):
    return pl.BlockSpec(array.shape, lambda i: (0,) * array.ndim)


def by_rows(rows, width, base=0):
    return pl.BlockSpec((rows, width), lambda i: (base + i, 0))


def params(**kw):
    return pltpu.CompilerParams(vmem_limit_bytes=58 * MIB, **kw)


def count_of(pieces):
    return sum(piece.shape[0] for piece in pieces)


def highway_forward(table, pieces, block_rows, bias, own, mate, chunk, words):
    width = own[0].shape[1]
    half = width * len(own)
    rows = min(ROWS, words)
    steps = words // rows
    tile = by_rows(rows, width, chunk * steps)
    out = by_rows(rows, half)
    return pl.pallas_call(
        functools.partial(forward_kernel, len(own), len(pieces), block_rows, width),
        grid=(steps,),
        in_specs=[SMEM_SPEC, whole(bias)] + [tile] * (2 * len(own)) + [ANY_SPEC] * len(pieces),
        out_specs=[out] * 5,
        out_shape=[jax.ShapeDtypeStruct((words, half), kind) for kind in (F32, BF16, BF16, BF16, BF16)],
        scratch_shapes=[pltpu.VMEM((2, 2 * half, half), BF16), pltpu.SemaphoreType.DMA((count_of(pieces),))],
        compiler_params=params(),
        cost_estimate=lasting(10),
        name="highway_forward",
    )(table, bias, *own, *mate, *pieces)


def highway_turn(table, pieces, block_rows, bias, own, mate, exact, out_grad, proj, width):
    words, half = own.shape
    out_width = out_grad.shape[1]
    rows = min(ROWS, words)
    tile = by_rows(rows, half)
    packed = proj is None
    scratch = [pltpu.VMEM((2, 2 * half, half), BF16), pltpu.SemaphoreType.DMA((count_of(pieces),))]
    if packed:
        scratch += [pltpu.VMEM((half, out_width), BF16), pltpu.SemaphoreType.DMA((2 * count_of(pieces),))]
    return pl.pallas_call(
        functools.partial(turn_kernel, len(pieces), block_rows, width, packed),
        grid=(words // rows,),
        in_specs=[SMEM_SPEC, whole(bias), tile, tile, tile, by_rows(rows, out_width)]
        + ([] if packed else [whole(proj)])
        + [ANY_SPEC] * len(pieces),
        out_specs=[tile] * 5 + [by_rows(rows, out_width), pl.BlockSpec((2, half), lambda i: (0, 0))],
        out_shape=[jax.ShapeDtypeStruct((words, half), kind) for kind in (BF16, BF16, BF16, F32, BF16)]
        + [jax.ShapeDtypeStruct((words, out_width), F32), jax.ShapeDtypeStruct((2, half), F32)],
        scratch_shapes=scratch,
        compiler_params=params(),
        cost_estimate=lasting(16),
        name="highway_turn",
    )(table, bias, own, mate, exact, out_grad, *([] if packed else [proj]), *pieces)


def highway_slopes(table, pieces, block_rows, partial, arrived, first, second, gate, width):
    words, half = partial.shape
    rows = min(ROWS, words)
    tile = by_rows(rows, half)
    return pl.pallas_call(
        functools.partial(slope_kernel, len(pieces), block_rows, width),
        grid=(words // rows,),
        in_specs=[SMEM_SPEC] + [tile] * 5 + [ANY_SPEC] * len(pieces),
        out_specs=[tile, tile, tile, tile, pl.BlockSpec((2, half), lambda i: (0, 0))],
        out_shape=[jax.ShapeDtypeStruct((words, half), kind) for kind in (BF16, BF16, F32, BF16)] + [jax.ShapeDtypeStruct((2, half), F32)],
        scratch_shapes=[pltpu.VMEM((2, half, half), BF16), pltpu.SemaphoreType.DMA((count_of(pieces),))],
        compiler_params=params(),
        cost_estimate=lasting(8),
        name="highway_slopes",
    )(table, partial, arrived, first, second, gate, *pieces)


def highway_back(table, pieces, block_rows, d_first, d_gate, up):
    words, width = d_first.shape
    rows = min(ROWS, words)
    tile = by_rows(rows, width)
    return pl.pallas_call(
        functools.partial(back_kernel, len(pieces), block_rows),
        grid=(words // rows,),
        in_specs=[SMEM_SPEC, tile, tile, tile] + [ANY_SPEC] * len(pieces),
        out_specs=tile,
        out_shape=jax.ShapeDtypeStruct((words, width), F32),
        scratch_shapes=[pltpu.VMEM((2, width, width), BF16), pltpu.SemaphoreType.DMA((count_of(pieces),))],
        compiler_params=params(),
        cost_estimate=lasting(6),
        name="highway_back",
    )(table, d_first, d_gate, up, *pieces)


def highway_weight_grad(table, xs, d_first, d_gate, rows, width):
    half = d_first[0].shape[1]
    words = sum(d.shape[0] for d in d_first)
    flat = [x for row in xs for x in row]
    steps = table.shape[1]
    blocks = half // width
    block = pl.BlockSpec((1, 2, rows, width), lambda i: (i, 0, 0, 0))
    return pl.pallas_call(
        functools.partial(weight_grad_kernel, len(xs), len(xs[0]), len(d_first), width),
        grid=(steps,),
        in_specs=[SMEM_SPEC] + [whole(x) for x in flat] + [whole(d) for d in d_first + d_gate],
        out_specs=[block] * blocks + [pl.BlockSpec((blocks, 1, 2, rows, width), lambda i: (0, i, 0, 0, 0))],
        out_shape=[jax.ShapeDtypeStruct((steps, 2, rows, width), BF16)] * blocks
        + [jax.ShapeDtypeStruct((blocks, steps, 2, rows, width), BF16)],
        scratch_shapes=[pltpu.VMEM((2 * half, words), BF16)],
        compiler_params=params(),
        cost_estimate=lasting(15),
        name="highway_weight_grad",
    )(table, *flat, *d_first, *d_gate)


def adam_update(weight, grad, moment_one, moment_two, rate):
    first_new = beta_one * moment_one + (1 - beta_one) * grad
    second_new = beta_two * moment_two + (1 - beta_two) * grad * grad
    corrected_one = first_new / (1 - beta_one**STEP)
    corrected_two = second_new / (1 - beta_two**STEP)
    updated = weight - rate * (
        corrected_one / (jnp.sqrt(corrected_two) + adam_eps) + decay_rate * weight
    )
    return (second_new, updated)


def owner_kernel(n_grads, at_ref, *refs):
    grads, refs = refs[:n_grads], refs[n_grads:]
    weight, one, two, average = refs[:4]
    grad, second, new, average_new = refs[-4:]
    width = grads[0].shape[2]
    for j, ref in enumerate(grads):
        at = pl.ds(pl.multiple_of(at_ref[j], LANES), width)
        grad[:, :, at] = ref[...].astype(F32)
    second_new, updated = adam_update(weight[...], grad[...], one[...], two[...], 0.02)
    second[...] = second_new
    new[...] = updated
    average_new[...] = average_keep * average[...] + (1 - average_keep) * updated


def owner_update(slot, at, grads, weight, one, two, average, so_far=()):
    slots, rows, width = grads[0].shape
    part = min(64, rows)
    block = pl.BlockSpec((1, part, weight.shape[2]), lambda i: (slot, i, 0))
    given = len(grads) + 5
    return pl.pallas_call(
        functools.partial(owner_kernel, len(grads)),
        grid=(rows // part,),
        in_specs=[SMEM_SPEC]
        + [pl.BlockSpec((1, part, width), lambda i: (slot, i, 0))] * len(grads)
        + [block] * 4
        + [ANY_SPEC] * len(so_far),
        out_specs=[block] * 4,
        out_shape=[jax.ShapeDtypeStruct(weight.shape, F32)] * 4,
        input_output_aliases={given + n: n for n in range(len(so_far))},
        compiler_params=params(),
        cost_estimate=lasting(8),
        name="owner_update",
    )(at, *grads, weight, one, two, average, *so_far)


def choose_kernel(n_from, table_ref, proj, *refs):
    arrived, outs = refs[:n_from], refs[n_from:]
    rows, width = arrived[0].shape[1:]
    for unit in range(UNITS):
        for step, ref in enumerate(arrived):

            @pl.when(table_ref[0, unit] == step)
            def _(ref=ref, unit=unit):
                outs[unit // 2][unit % 2, :rows, :] = ref[table_ref[1, unit]]

    under, part = proj.shape[0], proj.shape[1] // 2
    if outs[1].shape[1] > rows:
        outs[1][:, rows:, :] = jnp.zeros((2, under, width), BF16)
        for side in range(2):
            outs[1][side, rows:, :part] = proj[:, side * part : (side + 1) * part].astype(BF16)


def choose_units(table, arrived, proj, packed):
    slots, rows, width = arrived[0].shape
    shapes = [(2, rows, width), (2, rows + (proj.shape[0] if packed else 0), width)]
    return pl.pallas_call(
        functools.partial(choose_kernel, len(arrived)),
        grid=(1,),
        in_specs=[SMEM_SPEC, whole(proj)] + [whole(part) for part in arrived],
        out_specs=[pl.BlockSpec(shape, lambda i: (0, 0, 0)) for shape in shapes],
        out_shape=[jax.ShapeDtypeStruct(shape, BF16) for shape in shapes],
        compiler_params=params(),
        cost_estimate=lasting(3),
        name="choose_units",
    )(table, proj, *arrived)


def return_kernel(counts, table_ref, *refs):
    layers = (refs[: counts[0]], refs[counts[0] : counts[0] + counts[1]])
    for step, out in enumerate(refs[counts[0] + counts[1] :]):
        for slot in range(SLOTS):
            taken = table_ref[step, slot]
            for unit in range(UNITS):

                @pl.when(taken == unit)
                def _(unit=unit, out=out, slot=slot):
                    out[slot] = sum(ref[unit % 2].astype(F32) for ref in layers[unit // 2]).astype(BF16)

            @pl.when(taken < 0)
            def _(out=out, slot=slot):
                out[slot] = jnp.zeros(out.shape[1:], BF16)


def return_units(table, layers, count):
    shape = layers[0][0].shape
    part = min(64, shape[1])
    block = pl.BlockSpec((2, part, shape[2]), lambda i: (0, i, 0))
    terms = list(layers[0]) + list(layers[1])
    return pl.pallas_call(
        functools.partial(return_kernel, [len(layer) for layer in layers]),
        grid=(shape[1] // part,),
        in_specs=[SMEM_SPEC] + [block] * len(terms),
        out_specs=[block] * count,
        out_shape=[jax.ShapeDtypeStruct(shape, BF16)] * count,
        compiler_params=params(),
        cost_estimate=lasting(3),
        name="return_units",
    )(table, *terms)


class Places:
    def __init__(self):
        self.n_filt, self.n_dp = lax.axis_size("filt"), lax.axis_size("dp")
        self.n_y, self.n_z = self.n_filt // 2, self.n_dp // 2
        self.f, self.d = lax.axis_index("filt"), lax.axis_index("dp")
        self.y, self.x = self.f // 2, self.f % 2
        self.z, self.c = self.d // 2, self.d % 2
        self.direct = self.n_y == 2 and self.n_z == 4

    def over_filt(self, value, step):
        return lax.ppermute(value, "filt", [(i, i ^ step) for i in range(self.n_filt)])

    def over_x(self, value):
        return self.over_filt(value, 1)

    def over_y(self, value, step):
        return self.over_filt(value, 2 * step)

    def over_core(self, value):
        return lax.ppermute(value, "dp", [(i, i ^ 1) for i in range(self.n_dp)])

    def over_z(self, value, step):
        pairs = [(i, (i // 2 + step) % self.n_z * 2 + i % 2) for i in range(self.n_dp)]
        return lax.ppermute(value, "dp", pairs)

    def far_first(self):
        return sorted(range(1, self.n_z), key=lambda k: (min(k, self.n_z - k), k))

    def row_of(self, d, rows, width):
        f = d * rows // width
        half = self.n_y * width
        return (f % 2 ^ self.x) * half + (f // 2 ^ self.y) * width + d * rows % width


def after(value, *earlier):
    return lax.optimization_barrier((value, earlier))[0]


def settle(*values):
    return lax.optimization_barrier(values)


def gather_general(place, blocks):
    rows, width = blocks[0].shape[1:]
    out = []
    for piece in blocks:
        spread = lax.all_gather(lax.all_gather(piece, "dp"), "filt")
        spread = spread.reshape((place.n_y, 2) + spread.shape[1:])
        spread = lax.dynamic_index_in_dim(spread, place.x, 1, keepdims=False)
        spread = spread.reshape((place.n_y * place.n_dp,) + piece.shape)
        d = jnp.tile(jnp.arange(place.n_dp, dtype=jnp.int32), place.n_y)
        y = jnp.repeat(jnp.arange(place.n_y, dtype=jnp.int32), place.n_dp)
        table = jnp.stack([place.row_of(d, rows, width), (y ^ place.y) * width]).astype(jnp.int32)
        out.append((table, [spread]))
    return out


BLOCK_STEPS = (
    [(0, 0), (0, 1), (1, 0), (3, 0), (2, 0), (1, 1), (3, 1), (2, 1)],
    [(0, 0), (0, 1), (1, 0), (3, 0), (1, 1), (3, 1), (2, 0), (2, 1)],
)


def gather_table(place, layer, rows, width, rows_proj):
    at_rows, at_cols, at_proj = [], [], []
    for other in range(2):
        for k, step in BLOCK_STEPS[layer]:
            d = (place.z - k) % place.n_z * 2 + (place.c ^ other)
            at_rows.append(place.row_of(d, rows, width))
            at_cols.append(jnp.int32(step * width))
            at_proj.append(step * width + d * rows_proj)
    return jnp.stack([jnp.stack(at_rows), jnp.stack(at_cols), jnp.stack(at_proj)]).astype(jnp.int32)


def sum_table(place, rows, width):
    z = jnp.arange(place.n_z, dtype=jnp.int32)
    z, c = ((place.z + z) % place.n_z, place.c) if place.direct else (z, 0)
    return jnp.stack([place.row_of(z * 2 + c, rows, width), place.row_of(z * 2 + (1 - c), rows, width)]).astype(jnp.int32)


def sent_over_y(parts, group):
    near, arrived = parts
    return jnp.stack([(near[1][k].astype(F32) + arrived[1][k].astype(F32)).astype(BF16) for k in group])


def kept_over_y(parts, turned, group):
    near, arrived = parts
    return [near[0][k].astype(F32) + arrived[0][k].astype(F32) + turned[n].astype(F32) for n, k in enumerate(group)]


def sum_general(place, blocks):
    n_y = place.n_y
    near, far = blocks[:n_y], list(blocks[n_y])
    steps = jnp.arange(n_y, dtype=jnp.int32) ^ place.y
    pairs = jnp.stack([jnp.stack(near), jnp.stack(far)], axis=2)
    pairs = jnp.take(pairs, steps, axis=0)
    pairs = pairs.reshape((n_y, place.n_dp) + pairs.shape[3:])
    mine = lax.psum_scatter(pairs, "dp", scatter_dimension=1)
    sides = jnp.arange(2, dtype=jnp.int32).reshape(1, 2, 1, 1, 1)
    mine = jnp.where(sides == place.x, mine[:, None], jnp.zeros((), BF16))
    mine = mine.reshape((place.n_filt,) + mine.shape[2:])
    return lax.psum_scatter(mine, "filt", scatter_dimension=0).astype(F32)


def pick(array, at, axis=0):
    return lax.dynamic_index_in_dim(array, at, axis, keepdims=False)


def rows_over_core(place, value):
    parts = value.reshape((place.n_z, 2, -1) + value.shape[1:])
    return pick(parts, place.c, 1), over_core_low(place, pick(parts, 1 - place.c, 1))


def over_core_low(place, value):
    return place.over_core(value.astype(BF16))


def swap_z(place, value, step):
    pairs = [(i, i ^ (2 * step)) for i in range(place.n_dp)]
    return lax.ppermute(value, "dp", pairs)


def swap_rows(place, parts, step):
    upper = place.z // step % 2
    halves = parts.reshape((2, -1) + parts.shape[1:])
    return pick(halves, upper), swap_z(place, pick(halves, 1 - upper).astype(BF16), step)


def sum_filt(place, value):
    if not place.direct:
        return lax.psum(value, "filt")
    step = 1
    while step < place.n_filt:
        value = value + place.over_filt(value, step)
        step *= 2
    return value


def per_device(
    char_ids,
    word_lengths,
    out_grad,
    highway_owner,
    char_table,
    conv_weight,
    conv_bias,
    highway_weight,
    proj_weight,
    dense_bias,
    table_moment_one,
    table_moment_two,
    conv_moment_one,
    conv_moment_two,
    conv_bias_moment_one,
    conv_bias_moment_two,
    highway_moment_one,
    highway_moment_two,
    highway_average,
    proj_moment_one,
    proj_moment_two,
    bias_moment_one,
    bias_moment_two,
):
    place = Places()
    n_y, n_filt, direct = place.n_y, place.n_filt, place.direct
    width = conv_weight.shape[1]
    rows, width_full = highway_weight.shape[1:]
    half = width_full // 2
    rows_proj, out_width = proj_weight.shape
    vocab_count = char_table.shape[0]
    words_dev = char_ids.shape[0]
    words_y = words_dev // n_y
    chunks, chunk_words = range(2), words_y // 2
    steps_y = list(range(1, n_y))
    slot_index = unit_slots(highway_owner, SLOTS)
    mine_first = place.x == 0
    over_core, over_x, over_y, over_z = place.over_core, place.over_x, place.over_y, place.over_z

    widths = channel_widths(place.f * width, width, FILTERS)
    offsets = jnp.arange(TAPS, dtype=jnp.int32) // CHAR_DIM
    tap_mask = (offsets[:, None] < widths[None, :]).astype(jnp.float32)
    tile = min(256, words_dev)
    n_tiles = words_dev // tile
    cuts = [0, 1, 2, 4, 8] if n_tiles == 8 else [0, n_tiles]
    splits = list(zip(cuts[:-1], cuts[1:]))
    rank, data, table_t, conv_t, conv_back, width_col, narrow = conv_operands(
        char_ids, word_lengths, char_table, conv_weight, conv_bias, widths, width
    )
    rank_parts = [lax.dynamic_slice_in_dim(rank, (place.y ^ step) * words_y, words_y, axis=0) for step in range(n_y)]

    def convolve(some, narrow):
        return [conv_forward(rank, data, table_t, conv_t, width_col, narrow, width, begin, end - begin) for begin, end in some]

    def block_of(step):
        start = (place.f ^ step) * width
        return lax.dynamic_slice_in_dim(highway_weight, start, width, axis=2).astype(BF16)

    from_owner = [block_of(0)] + [place.over_filt(block_of(step), step) for step in range(1, n_filt)]
    kept = convolve(splits[: len(splits) // 2], narrow)
    from_owner, kept, narrow = settle(from_owner, kept, narrow)
    owner_table = jnp.stack([highway_owner ^ place.f, slot_index % SLOTS])
    blocks = choose_units(owner_table, from_owner, proj_weight, direct)
    bias_float = lax.reduce_precision(dense_bias, 8, 7)

    def half_bias(unit):
        starts = [unit * width_full + (2 * (place.y ^ step) + place.x) * width for step in range(n_y)]
        return jnp.concatenate([lax.dynamic_slice_in_dim(bias_float, start, width) for start in starts])

    layer_bias = [jnp.stack([half_bias(2 * layer), half_bias(2 * layer + 1)]) for layer in range(2)]

    blocks, narrow, sent = settle(blocks, narrow, out_grad)
    grad_mate = over_x(sent)
    if direct:
        first_y = [over_y(block, 1) for block in blocks]
        near = [over_z(blocks[0], k) for k in (1, 3)]
    kept = kept + convolve(splits[len(splits) // 2 :], narrow)
    placed = [place_words(part, [parts[0] for parts in kept]) for part in rank_parts]
    own = [placed[0]] + [over_y(placed[step], step) for step in steps_y]
    if direct:
        near, first_y, placed, grad_mate, blocks = settle(near, first_y, placed, grad_mate, blocks)
        own = [placed[0], over_y(placed[1], 1)]
        mate = [over_x(placed[0])]
        far = over_z(blocks[0], 2)
        own, mate, far, near, blocks, first_y, layer_bias, grad_mate = settle(
            own, mate, far, near, blocks, first_y, layer_bias, grad_mate
        )

        out_grads = [jnp.where(mine_first, out_grad, grad_mate), jnp.where(mine_first, grad_mate, out_grad)]
        sent = jnp.stack([near[0], near[1], far])
        sent_y = over_y(sent, 1)
        mate = mate + [over_x(own[1])]
        near_one = [over_z(blocks[1], k) for k in (1, 3)]
        sent_core = over_core(sent)
        start = jnp.stack([blocks[0], first_y[0]])
        sent_y, sent_core, start, mate, near_one, blocks = settle(sent_y, sent_core, start, mate, near_one, blocks)

        table = [gather_table(place, layer, rows, width, rows_proj) for layer in range(2)]
        gathered = [(table[0], [start, sent, sent_y, over_core(start), sent_core, over_core(sent_y)], rows)]
        far_one = over_z(blocks[1], 2)
        near_y = over_y(jnp.stack(near_one), 1)
    else:
        mate = [over_x(part) for part in own]
        gathered = [(*found, rows) for found in gather_general(place, blocks)]
        out_grads = [jnp.where(mine_first, out_grad, grad_mate), jnp.where(mine_first, grad_mate, out_grad)]

    forward, x_one_mate = [], []
    for chunk in chunks:
        forward.append(highway_forward(*gathered[0], layer_bias[0], own, mate, chunk, chunk_words))
        x_one_mate.append(over_x(forward[chunk][1]))
        if direct and chunk == 0:
            forward[0], near_one, layer_bias[0] = settle(forward[0], near_one, layer_bias[0])
            start = jnp.stack([blocks[1], first_y[1], near_one[0], near_one[1]])
            start_core = over_core(start)
    if direct:
        far_one, near_y, forward[1] = settle(far_one, near_y, forward[1])
        far_y = over_y(far_one, 1)
        far_y, x_one_mate[0] = settle(far_y, x_one_mate[0])
        last = jnp.stack([near_y[0], near_y[1], far_one, far_y])
        gathered.append((table[1], [start, last, start_core, over_core(last)], rows))
        proj_half = None
    else:
        proj_own = jnp.stack([proj_weight.astype(BF16)] + [over_y(proj_weight.astype(BF16), step) for step in steps_y])
        proj_half = lax.all_gather(proj_own, "dp", axis=1).reshape(half, out_width)
    x_one, x_one_low, first_zero, second_zero, gate_zero = zip(*forward)
    turned, arrived = [], []
    for chunk in chunks:
        bias_one = layer_bias[1] if chunk == 0 else settle(layer_bias[1], turned[0])[0]
        turned.append(
            highway_turn(*gathered[1], bias_one, x_one_low[chunk], x_one_mate[chunk], x_one[chunk], out_grads[chunk], proj_half, width)
        )
        arrived.append(over_x(turned[chunk][4]))
    x_two_low, d_first_one, d_gate_one, up_one, _, vectors, sums = (list(parts) for parts in zip(*turned))
    sums_one = sums[0] + sums[1]

    targets = sum_table(place, rows, width)
    blocks = highway_weight_grad(
        targets, [[x_one_low[chunk], x_one_mate[chunk]] for chunk in chunks], d_first_one, d_gate_one, rows, width
    )
    blocks, up_one[0], arrived[0] = settle(blocks, up_one[0], arrived[0])
    if not direct:
        sum_one = sum_general(place, blocks)

    partial, parts_zero, arrived_zero = [], [], []
    for chunk in chunks:
        partial.append(highway_back(*gathered[1], d_first_one[chunk], d_gate_one[chunk], up_one[chunk]))
        if chunk == 0 and direct:
            partial[0], arrived[1], blocks = settle(partial[0], arrived[1], blocks)
            one = (blocks[:2], over_core(blocks[2]))
        parts_zero.append(
            highway_slopes(*gathered[0], partial[chunk], arrived[chunk], first_zero[chunk], second_zero[chunk], gate_zero[chunk], width)
        )
        if chunk == 0 and direct:
            one, parts_zero[0], up_one[1] = settle(one, parts_zero[0], up_one[1])
            sent = sent_over_y(one, range(place.n_z))
            sent, up_one[1] = settle(sent, up_one[1])
            one_y = over_y(sent, 1)
        arrived_zero.append(over_x(parts_zero[chunk][3]))
    d_first, d_gate, up, _, sums = (list(parts) for parts in zip(*parts_zero))
    sums_zero = sums[0] + sums[1]
    blocks = highway_weight_grad(targets, [own + mate], d_first, d_gate, rows, width)
    blocks, up, arrived_zero[0] = settle(blocks, up, arrived_zero[0])
    groups = [[2, 1], [3, 0]]
    if not direct:
        sum_zero = sum_general(place, blocks)
    partial = [highway_back(*gathered[0], d_first[chunk], d_gate[chunk], up[chunk]) for chunk in chunks]
    if direct:
        partial, blocks, arrived_zero[1], one_y = settle(partial, blocks, arrived_zero[1], one_y)
        zero = (blocks[:2], over_core(blocks[2]))
    if direct:
        one_here = kept_over_y(one, one_y, range(place.n_z))
        one_sent = [one_here[k].astype(BF16) for k in (2, 1, 3)]
        one_here = one_here[0]
        one_sent, one_here, partial = settle(one_sent, one_here, partial)
        one_z = [over_z(value, k) for value, k in zip(one_sent, (2, 1, 3))]
    groups = [[2, 1], [3, 0]]
    if not direct:
        sum_zero = sum_general(place, blocks)
    partial = [highway_back(*gathered[0], d_first[chunk], d_gate[chunk], up[chunk]) for chunk in chunks]
    if direct:
        partial, blocks, arrived_zero[1], one_y = settle(partial, blocks, arrived_zero[1], one_y)
        zero = (blocks[:2], over_core(blocks[2]))
    feature_grad = []
    for step in range(n_y):
        cols = slice(step * width, (step + 1) * width)
        feature_grad.append(
            jnp.concatenate(
                [(partial[chunk][:, cols] + arrived_zero[chunk][:, cols].astype(F32)).astype(BF16) for chunk in chunks]
            )
        )
    groups = [[2, 1], [3, 0]]
    returned = [over_y(value, step) if step else value for step, value in enumerate(feature_grad)]
    if direct:
        returned[0], x_two_low, vectors = settle(returned[0], x_two_low, vectors)
        zero_y = [over_y(sent_over_y(zero, groups[0]), 1)]
    proj_part = (tn(x_two_low[0], out_grads[0]) + tn(x_two_low[1], out_grads[1])).reshape(n_y, width, out_width)
    proj_here, proj_away = proj_part[0], [proj_part[step].astype(BF16) for step in steps_y]
    vectors_away = jnp.where(mine_first, vectors[1], vectors[0]).astype(BF16)
    vectors_here = jnp.where(mine_first, vectors[0], vectors[1])
    ranks = [part.T for part in rank_parts]

    wanted = (place.f ^ jnp.arange(n_filt, dtype=jnp.int32))[:, None] * SLOTS + jnp.arange(SLOTS, dtype=jnp.int32)[None, :]
    fits = slot_index[None, None, :] == wanted[:, :, None]
    return_table = jnp.max(jnp.where(fits, jnp.arange(UNITS, dtype=jnp.int32), -1), axis=2)
    if direct:
        returned, narrow, ranks = settle(returned, narrow, ranks)

    def convolve_back(n, narrow, so_far):
        (begin, _), (_, lse, sorted_ids, embedded) = splits[n], kept[n]
        return conv_backward(
            ranks, sorted_ids, embedded, table_t.shape[1], conv_t, conv_back, width_col, narrow, lse, returned, width, begin, tile, so_far
        )

    home = jnp.arange(n_filt, dtype=jnp.int32)

    def natural(values):
        parts = values.reshape(n_y, 1, width)
        out = jnp.zeros((n_filt, width), F32)
        for step in range(n_y):
            out = jnp.where((home == 2 * (place.y ^ step) + place.x)[:, None], parts[step], out)
        return out.reshape(-1)

    bias_local = jnp.concatenate(
        [natural(sums[unit]) for sums in (sums_zero, sums_one) for unit in range(2)] + [jnp.sum(out_grad, axis=0, dtype=F32)]
    )
    table_rows = table_t.shape[1] // LANES * CHAR_DIM
    bias_rows = -(-bias_local.size // DEPTH)
    bias_rows += -(width + table_rows + bias_rows) % 16
    bias_flat = jnp.pad(bias_local, (0, bias_rows * DEPTH - bias_local.size)).reshape(bias_rows, DEPTH)
    small = jnp.concatenate([jnp.zeros((width + table_rows, DEPTH), F32), bias_flat])
    if direct:
        small, returned, narrow = settle(small, returned, narrow)
    back = small
    for n in range(len(splits)):
        back = convolve_back(n, narrow, back)
        if direct and n == 0:
            back, narrow, one_z, zero_y[0], zero, vectors_away, proj_away = settle(
                back, narrow, one_z, zero_y[0], zero, vectors_away, proj_away
            )
            zero_here = kept_over_y(zero, zero_y[0], groups[0])
            zero_z, zero_sent, narrow = settle([value.astype(BF16) for value in zero_here], sent_over_y(zero, groups[1]), narrow)
            zero_z = [over_z(value, k) for value, k in zip(zero_z, groups[0])]
            zero_y.append(over_y(zero_sent, 1))
            proj_y = over_y(proj_away[0], 1)
            vectors_arrived = over_x(vectors_away)
        if direct and n == 2:
            back, zero_z, narrow, zero_y, vectors_arrived, proj_y = settle(back, zero_z, narrow, zero_y, vectors_arrived, proj_y)
            last, zero_here = kept_over_y(zero, zero_y[1], groups[1])
            last, zero_here, narrow = settle(last.astype(BF16), zero_here, narrow)
            last = over_z(last, 3)
            proj_rows = rows_over_core(place, proj_here + proj_y.astype(F32))
    if direct:
        back, last, proj_rows = settle(back, last, proj_rows)
        slot_grads = return_units(return_table, [[zero_here] + zero_z + [last], [one_here] + one_z], n_filt)
    else:
        proj_y = [over_y(value, step) for value, step in zip(proj_away, steps_y)]
        proj_grad = lax.psum_scatter(proj_here + sum(value.astype(F32) for value in proj_y), "dp", scatter_dimension=0, tiled=True)
    if not direct:
        vectors_arrived = over_x(vectors_away)
    small = back
    if direct:
        small = small + over_core(small)
    else:
        small = lax.psum(small, "dp")
        small = jnp.concatenate([small[:width], sum_filt(place, small[width:])])

    optimizer = (highway_weight, highway_moment_one, highway_moment_two, highway_average)
    columns = (place.f ^ jnp.arange(n_filt, dtype=jnp.int32)) * width
    if direct:
        slot_grads, small, proj_rows, vectors_arrived = settle(slot_grads, small, proj_rows, vectors_arrived)
        arrived_slots = [place.over_filt(slot_grads[step], step) for step in range(1, n_filt)]
        small = small + swap_z(place, small.astype(BF16), 1).astype(F32)
        small = small + swap_z(place, small.astype(BF16), 2).astype(F32)
        small, arrived_slots = settle(small, arrived_slots)
        conv_sums, small = small[:width], small[width:]
        slot_grads = [slot_grads[0]] + arrived_slots
        small = small + over_x(small)
        proj_rows = swap_rows(place, proj_rows[0] + proj_rows[1].astype(F32), 2)
        updates = owner_update(0, columns, slot_grads, *optimizer)
        updates, small, proj_rows, slot_grads = settle(updates, small, proj_rows, slot_grads)
        small = small + over_y(small, 1)
        proj_rows = swap_rows(place, proj_rows[0] + proj_rows[1].astype(F32), 1)
        updates = owner_update(1, columns, slot_grads, *optimizer, updates)
        updates, small, proj_rows = settle(updates, small, proj_rows)
        proj_grad = (proj_rows[0] + proj_rows[1].astype(F32)).reshape(rows_proj, out_width)
    else:
        slot_grads = return_units(return_table, [[sum_zero], [sum_one]], n_filt)
        slot_grads = [slot_grads[0]] + [place.over_filt(slot_grads[step], step) for step in range(1, n_filt)]
        conv_sums, small = small[:width], small[width:]
        updates = owner_update(0, columns, slot_grads, *optimizer)
        updates = owner_update(1, columns, slot_grads, *optimizer, updates)
    highway_grad, highway_second, highway_new, highway_average_new = updates
    word_vectors = vectors_here + vectors_arrived.astype(F32) + bias_float[UNITS * width_full :]
    conv_grad, conv_bias_grad = conv_sums[:, :TAPS].T * tap_mask, conv_sums[:, TAPS]
    table_grad = small[:table_rows].reshape(-1, CHAR_DIM, LANES).transpose(0, 2, 1).reshape(-1, CHAR_DIM)[:vocab_count]
    bias_grad = small[table_rows:].reshape(-1)[: bias_local.size]
    table_second, table_new = adam_update(
        char_table, table_grad, table_moment_one, table_moment_two, 1.0
    )
    conv_second, conv_new = adam_update(
        conv_weight, conv_grad, conv_moment_one, conv_moment_two, 0.1
    )
    conv_bias_second, conv_bias_new = adam_update(
        conv_bias, conv_bias_grad, conv_bias_moment_one, conv_bias_moment_two, 0.3
    )
    proj_second, proj_new = adam_update(
        proj_weight, proj_grad, proj_moment_one, proj_moment_two, 0.02
    )
    bias_second, bias_new = adam_update(
        dense_bias, bias_grad, bias_moment_one, bias_moment_two, 0.3
    )
    return (
        word_vectors,
        table_grad,
        table_second,
        table_new,
        conv_grad,
        conv_second,
        conv_new,
        conv_bias_grad,
        conv_bias_second,
        conv_bias_new,
        highway_grad,
        highway_second,
        highway_new,
        highway_average_new,
        proj_grad,
        proj_second,
        proj_new,
        bias_grad,
        bias_second,
        bias_new,
    )


def solution(mesh):
    return jax.shard_map(
        per_device,
        mesh=mesh,
        in_specs=(
            P("dp", None),
            P("dp"),
            P(("dp", "filt"), None),
            P(),
            P(),
            P(None, "filt"),
            P("filt"),
            P("filt", "dp", None),
            P(("filt", "dp"), None),
            P(),
            P(),
            P(),
            P(None, "filt"),
            P(None, "filt"),
            P("filt"),
            P("filt"),
            P("filt", "dp", None),
            P("filt", "dp", None),
            P("filt", "dp", None),
            P(("filt", "dp"), None),
            P(("filt", "dp"), None),
            P(),
            P(),
        ),
        out_specs=(
            P(("dp", "filt"), None),
            P(),
            P(),
            P(),
            P(None, "filt"),
            P(None, "filt"),
            P(None, "filt"),
            P("filt"),
            P("filt"),
            P("filt"),
            P("filt", "dp", None),
            P("filt", "dp", None),
            P("filt", "dp", None),
            P("filt", "dp", None),
            P(("filt", "dp"), None),
            P(("filt", "dp"), None),
            P(("filt", "dp"), None),
            P(),
            P(),
            P(),
        ),
        check_vma=False,
    )
```

```python
import functools

import jax
import jax.numpy as jnp
from jax import lax
from jax.experimental import pallas as pl
from jax.experimental.pallas import tpu as pltpu
from jax.sharding import PartitionSpec as P

CHAR_DIM = 16
MAX_CHARS = 50
MAX_WIDTH = 7
FILTERS = 2048
UNITS = 4
SLOTS = 2
STEP = 10
TAPS = MAX_WIDTH * CHAR_DIM
DEPTH = 128
ID_SHIFT = 128
ID_ROWS = 64
SLOTS_E = MAX_CHARS + MAX_WIDTH - 1 + 8
LANES = 128
STEP_P = 4
ROWS = 256
beta_one = 0.9
beta_two = 0.999
adam_eps = 1e-08
decay_rate = 0.01
average_keep = 0.9
F32, BF16 = jnp.float32, jnp.bfloat16
MIB = 1 << 20


def lasting(us):
    return pl.CostEstimate(flops=int(us * 1e7), bytes_accessed=int(us * 3e4), transcendentals=0)


def nt(a, b):
    return lax.dot_general(a, b, (((1,), (1,)), ((), ())), preferred_element_type=F32)


def nn(a, b):
    return lax.dot_general(a, b, (((1,), (0,)), ((), ())), preferred_element_type=F32)


def tn(a, b):
    return lax.dot_general(a, b, (((0,), (0,)), ((), ())), preferred_element_type=F32)


def embed_tile(ids_ref, table_ref, lens, e_ref, longest):
    tile = lens.shape[1]
    e_ref[...] = jnp.zeros_like(e_ref)
    pieces = table_ref.shape[1] // LANES

    def fill(s, carry):
        for i in range(STEP_P):
            p = s * STEP_P + i
            row = ids_ref[pl.ds(p, 1), :].astype(jnp.int32)
            parts = []
            for lane in range(tile // LANES):
                idx = jnp.broadcast_to(row[:, lane * LANES : (lane + 1) * LANES], (CHAR_DIM, LANES))
                low = jnp.bitwise_and(idx, LANES - 1)
                value = jnp.zeros((CHAR_DIM, LANES), F32)
                for piece in range(pieces):
                    got = jnp.take_along_axis(table_ref[:, piece * LANES : (piece + 1) * LANES], low, axis=1)
                    value = jnp.where(lax.shift_right_logical(idx, 7) == piece, got, value)
                parts.append(value)
            value = jnp.concatenate(parts, axis=1) if len(parts) > 1 else parts[0]
            value = jnp.where(p < lens, value, 0.0)
            e_ref[pl.ds(pl.multiple_of(p * CHAR_DIM, CHAR_DIM), CHAR_DIM), :] = value.astype(BF16)
        return carry

    lax.fori_loop(0, (longest + STEP_P - 1) // STEP_P, fill, 0)


def limits_of(lens):
    row = lax.broadcasted_iota(jnp.int32, (CHAR_DIM, lens.shape[1]), 0)
    past = jnp.maximum(lens - (row - 2), 0)
    return jnp.where(row < 3, -1, jnp.where(row < 3 + MAX_WIDTH, past, 1 << 20))


def window_at(e_ref, limit, p):
    extra = jnp.where(p > limit, 1.0, 0.0).astype(BF16)
    taps = e_ref[pl.ds(pl.multiple_of(p * CHAR_DIM, CHAR_DIM), TAPS), :]
    return jnp.concatenate([taps, extra], axis=0)


SUB = 32


def windows_at(e_ref, limit, s):
    return jnp.concatenate([window_at(e_ref, limit, s * STEP_P + i) for i in range(STEP_P)], axis=1)


def in_halves(step, channels, longest, narrow_ref):
    both = steps_of(longest, narrow_ref[1])
    lax.fori_loop(0, both, functools.partial(step, channels), 0)
    lax.fori_loop(both, jnp.maximum(both, steps_of(longest, narrow_ref[0])), functools.partial(step, channels // 2), 0)


def steps_of(longest, narrow):
    return (jnp.maximum(longest - narrow, 0) + STEP_P) // STEP_P


def conv_forward_kernel(cblock, base, narrow_ref, rank_ref, data_ref, table_ref, conv_ref, width_ref, feat_ref, lse_ref, ids_ref, e_ref, top, total, pre):
    tile = ids_ref.shape[1]
    words = rank_ref.shape[0]
    first = (base + pl.program_id(0)) * tile
    lane = first + lax.broadcasted_iota(jnp.int32, (words, tile), 1)
    hot = jnp.where(rank_ref[...] == lane, 1.0, 0.0).astype(BF16)
    moved = nn(data_ref[...], hot)
    shift = jnp.where(lax.broadcasted_iota(jnp.int32, moved.shape, 0) < MAX_CHARS, float(ID_SHIFT), 0.0)
    moved = moved + shift
    ids_ref[...] = moved
    lens = (moved[MAX_CHARS : MAX_CHARS + 1, :] + 0.5).astype(jnp.int32)
    longest = jnp.max(lens)
    embed_tile(ids_ref, table_ref, lens, e_ref, longest)
    limit = limits_of(lens)
    channels = conv_ref.shape[0]
    top[...] = jnp.full_like(top, -1e30)
    total[...] = jnp.zeros_like(total)

    def step(rows, s, carry):
        pre[:rows, :] = nn(conv_ref[:rows, :], windows_at(e_ref, limit, s))
        for sub in range(0, rows, SUB):
            part = slice(sub, sub + SUB)
            values = [pre[part, i * tile : (i + 1) * tile] for i in range(STEP_P)]
            before = top[part, :]
            best = functools.reduce(jnp.maximum, values, before)
            top[part, :] = best
            total[part, :] = total[part, :] * jnp.exp(before - best) + sum(jnp.exp(value - best) for value in values)
        return carry

    in_halves(step, channels, longest, narrow_ref)
    span = jnp.maximum(lens - width_ref[...], 0)
    lse = top[...] + jnp.log(total[...])
    lse_ref[...] = lse
    pooled = lse - jnp.log((span + 1).astype(F32))
    feat_ref[...] = (pooled * jax.nn.sigmoid(pooled)).astype(BF16)


def place_kernel(rank_ref, *refs):
    feats, out_ref = refs[:-1], refs[-1]
    total, base = 0.0, 0
    for feat_ref in feats:
        shape = (rank_ref.shape[0], feat_ref.shape[1])
        lane = base + lax.broadcasted_iota(jnp.int32, shape, 1)
        hot = jnp.where(rank_ref[...] == lane, 1.0, 0.0).astype(BF16)
        total = total + nt(hot, feat_ref[...])
        base += shape[1]
    out_ref[...] = total.astype(BF16)


def conv_forward(rank, data, table_t, conv_t, widths, narrow, cblock, base, count):
    words, channels = rank.shape[0], conv_t.shape[0]
    tile = min(256, words)
    span = count * tile
    full = lambda *shape: pl.BlockSpec(shape, lambda i: (0,) * len(shape))
    column = lambda depth: pl.BlockSpec((depth, tile), lambda i: (0, i))
    return pl.pallas_call(
        functools.partial(conv_forward_kernel, cblock, base),
        grid=(count,),
        in_specs=[
            pl.BlockSpec(memory_space=pltpu.SMEM),
            full(words, 1),
            full(*data.shape),
            full(*table_t.shape),
            full(*conv_t.shape),
            full(channels, 1),
        ],
        out_specs=[column(channels), column(channels), column(ID_ROWS), column(SLOTS_E * CHAR_DIM)],
        out_shape=[
            jax.ShapeDtypeStruct((channels, span), BF16),
            jax.ShapeDtypeStruct((channels, span), F32),
            jax.ShapeDtypeStruct((ID_ROWS, span), F32),
            jax.ShapeDtypeStruct((SLOTS_E * CHAR_DIM, span), BF16),
        ],
        scratch_shapes=[
            pltpu.VMEM((cblock, tile), F32),
            pltpu.VMEM((cblock, tile), F32),
            pltpu.VMEM((cblock, STEP_P * tile), F32),
        ],
        compiler_params=pltpu.CompilerParams(vmem_limit_bytes=48 * MIB),
        cost_estimate=lasting(11),
        name="conv_forward",
    )(narrow, rank, data, table_t, conv_t, widths)


def place_words(rank, feats):
    words, channels = rank.shape[0], feats[0].shape[0]
    rows = min(256, words)
    return pl.pallas_call(
        place_kernel,
        grid=(words // rows,),
        in_specs=[pl.BlockSpec((rows, 1), lambda i: (i, 0))] + [pl.BlockSpec(feat.shape, lambda i: (0, 0)) for feat in feats],
        out_specs=pl.BlockSpec((rows, channels), lambda i: (i, 0)),
        out_shape=jax.ShapeDtypeStruct((words, channels), BF16),
        compiler_params=pltpu.CompilerParams(vmem_limit_bytes=48 * MIB),
        cost_estimate=lasting(4),
        name="place_words",
    )(rank, *feats)


def conv_backward_kernel(cblock, n_parts, base, narrow_ref, ids_ref, e_ref, conv_ref, back_ref, width_ref, lse_ref, *refs):
    ranks, grads, refs = refs[:n_parts], refs[n_parts : 2 * n_parts], refs[2 * n_parts :]
    so_far, sums_ref, table_grad_ref, de_ref, dpool, pre, d_pre, found = refs
    tile = ids_ref.shape[1]
    lanes = table_grad_ref.shape[0]
    channels = conv_ref.shape[0]
    first = (base + pl.program_id(0)) * tile

    @pl.when(pl.program_id(0) == 0)
    def _():
        sums_ref[...] = so_far[...]
        table_grad_ref[...] = jnp.zeros_like(table_grad_ref)

    lens = (ids_ref[MAX_CHARS : MAX_CHARS + 1, :] + 0.5).astype(jnp.int32)
    longest = jnp.max(lens)
    limit = limits_of(lens)
    de_ref[...] = jnp.zeros_like(de_ref)
    moved = 0.0
    for rank_ref, grad_ref in zip(ranks, grads):
        row = first + lax.broadcasted_iota(jnp.int32, (tile, rank_ref.shape[1]), 0)
        moved = moved + nn(jnp.where(rank_ref[...] == row, 1.0, 0.0).astype(BF16), grad_ref[...])
    moved = moved.T
    span = jnp.maximum(lens - width_ref[...], 0)
    pooled = lse_ref[...] - jnp.log((span + 1).astype(F32))
    sigma = jax.nn.sigmoid(pooled)
    dpool[...] = moved * (sigma + pooled * sigma * (1 - sigma))

    def step(rows, s, carry):
        windows = windows_at(e_ref, limit, s)
        pre[:rows, :] = nn(conv_ref[:rows, :], windows)
        for sub in range(0, rows, SUB):
            part = slice(sub, sub + SUB)
            low, scale = lse_ref[part, :], dpool[part, :]
            for i in range(STEP_P):
                cols = slice(i * tile, (i + 1) * tile)
                d_pre[part, cols] = (jnp.exp(pre[part, cols] - low) * scale).astype(BF16)
        back = nn(back_ref[:, :rows], d_pre[:rows, :])
        for i in range(STEP_P):
            at = pl.ds(pl.multiple_of((s * STEP_P + i) * CHAR_DIM, CHAR_DIM), TAPS)
            de_ref[at, :] += back[:TAPS, i * tile : (i + 1) * tile]
        sums_ref[:rows, :] += nt(d_pre[:rows, :], windows)
        return carry

    in_halves(step, channels, longest, narrow_ref)
    letter = lax.broadcasted_iota(jnp.int32, (found.shape[0], tile), 0)

    def spread(s, carry):
        parts = []
        for i in range(STEP_P):
            p = s * STEP_P + i
            at = pl.ds(pl.multiple_of(p * CHAR_DIM, CHAR_DIM), CHAR_DIM)
            value = jnp.where(p < lens, de_ref[at, :], 0.0)
            high = value.astype(BF16)
            parts.append(jnp.concatenate([high, (value - high.astype(F32)).astype(BF16)], axis=0))
            row = ids_ref[pl.ds(p, 1), :].astype(jnp.int32)
            found[:, i * tile : (i + 1) * tile] = jnp.where(letter == row, 1.0, 0.0).astype(BF16)
        table_grad_ref[: found.shape[0], :] += nt(found[...], jnp.concatenate(parts, axis=1))
        return carry

    lax.fori_loop(0, (longest + STEP_P - 1) // STEP_P, spread, 0)

    @pl.when(pl.program_id(0) == pl.num_programs(0) - 1)
    def _():
        both = table_grad_ref[...].T
        total = both[:CHAR_DIM] + both[CHAR_DIM:]
        for piece in range(lanes // LANES):
            at = channels + piece * CHAR_DIM
            sums_ref[at : at + CHAR_DIM, :] += total[:, piece * LANES : (piece + 1) * LANES]


def conv_backward(ranks, ids, embedded, vocab, conv_t, conv_back, widths, narrow, lse, grads, cblock, base, tile, so_far):
    channels, words = conv_t.shape[0], ids.shape[1]
    full = lambda *shape: pl.BlockSpec(shape, lambda i: (0,) * len(shape))
    return pl.pallas_call(
        functools.partial(conv_backward_kernel, cblock, len(ranks), base),
        grid=(words // tile,),
        in_specs=[
            pl.BlockSpec(memory_space=pltpu.SMEM),
            pl.BlockSpec((ID_ROWS, tile), lambda i: (0, i)),
            pl.BlockSpec((SLOTS_E * CHAR_DIM, tile), lambda i: (0, i)),
            full(*conv_t.shape),
            full(*conv_back.shape),
            full(channels, 1),
            pl.BlockSpec((channels, tile), lambda i: (0, i)),
        ]
        + [full(*part.shape) for part in ranks]
        + [full(*part.shape) for part in grads]
        + [full(*so_far.shape)],
        out_specs=full(*so_far.shape),
        out_shape=jax.ShapeDtypeStruct(so_far.shape, F32),
        scratch_shapes=[
            pltpu.VMEM((-(-vocab // LANES) * LANES, 2 * CHAR_DIM), F32),
            pltpu.VMEM((SLOTS_E * CHAR_DIM, tile), F32),
            pltpu.VMEM((cblock, tile), F32),
            pltpu.VMEM((cblock, STEP_P * tile), F32),
            pltpu.VMEM((cblock, STEP_P * tile), BF16),
            pltpu.VMEM((-(-vocab // 16) * 16, STEP_P * tile), BF16),
        ],
        compiler_params=pltpu.CompilerParams(vmem_limit_bytes=48 * MIB),
        cost_estimate=lasting(15),
        name="conv_backward",
    )(narrow, ids, embedded, conv_t, conv_back, widths, lse, *ranks, *grads, so_far)


def word_order(lengths):
    count = lengths.shape[0]
    key = lengths * count - jnp.arange(count, dtype=jnp.int32)
    return jnp.sum((key[None, :] > key[:, None]).astype(jnp.int32), axis=1, keepdims=True)


def conv_operands(char_ids, lengths, char_table, conv_weight, conv_bias, widths, cblock):
    words = char_ids.shape[0]
    channels = conv_weight.shape[1]
    vocab = char_table.shape[0]
    lanes = -(-vocab // LANES) * LANES
    rank = word_order(lengths)
    data = jnp.concatenate([char_ids.T - ID_SHIFT, lengths[None, :]], axis=0)
    data = jnp.pad(data, ((0, ID_ROWS - MAX_CHARS - 1), (0, 0))).astype(BF16)
    offsets = jnp.arange(TAPS, dtype=jnp.int32) // CHAR_DIM
    taps = jnp.where(offsets[:, None] < widths[None, :], conv_weight, 0.0).astype(BF16)
    parts, rest = [], conv_bias
    for _ in range(3):
        part = lax.reduce_precision(rest, 8, 7)
        parts.append(part)
        rest = rest - part
    kinds = jnp.arange(1, MAX_WIDTH + 1, dtype=jnp.int32)
    spans = jnp.where(kinds[:, None] == widths[None, :], -1e30, 0.0)
    under = jnp.concatenate([jnp.stack(parts), spans, jnp.zeros((DEPTH - TAPS - 3 - MAX_WIDTH, channels), F32)])
    conv_all = jnp.concatenate([taps, under.astype(BF16)])
    conv_back = jnp.pad(taps, ((0, DEPTH - TAPS), (0, 0)))
    table_t = jnp.pad(lax.reduce_precision(char_table, 8, 7).T, ((0, 0), (0, lanes - vocab)))
    narrow = widths[:: channels // 2]
    return rank, data, table_t, conv_all.T, conv_back, widths[:, None], narrow


def channel_widths(start, count, whole):
    channel = start + jnp.arange(count, dtype=jnp.int32)
    widths = jnp.ones((count,), jnp.int32)
    for power in range(6):
        widths = widths + (channel >= whole * 2**power // 64).astype(jnp.int32)
    return widths


def load_pieces(table_ref, pieces, rows, dest, sems, half=None, proj=None):
    cols = pieces[0].shape[3]
    depth = dest.shape[1]

    def each(act):
        at = 0
        for ref in pieces:
            for j in range(ref.shape[0]):
                row, col = table_ref[0, at], table_ref[1, at]
                row = row if half is None else row - half * depth
                sem = sems.at[at]

                def go(ref=ref, j=j, row=row, col=col, sem=sem):
                    place = (slice(None), pl.ds(pl.multiple_of(row, rows), rows), pl.ds(pl.multiple_of(col, cols), cols))
                    act(pltpu.make_async_copy(ref.at[j, :, :rows, :], dest.at[place], sem))

                if half is None:
                    go()
                else:
                    pl.when((row >= 0) & (row < depth))(go)
                if proj is not None:
                    under = ref.shape[2] - rows
                    part = proj[0].shape[1] // 2
                    to = pl.ds(pl.multiple_of(table_ref[2, at], under), under)
                    for side in range(2):
                        source = ref.at[j, side, rows:, :part]
                        act(pltpu.make_async_copy(source, proj[0].at[to, side * part : (side + 1) * part], proj[1].at[2 * at + side]))
                at += 1

    each(lambda copy: copy.start())
    each(lambda copy: copy.wait())


def hidden_of(xs, weight, unit, cols, bias_ref):
    at, total = 0, None
    for x in xs:
        term = nn(x[...], weight[unit, at : at + x.shape[1], cols])
        total = term if total is None else total + term
        at += x.shape[1]
    return total + bias_ref[unit : unit + 1, cols]


def sigmoid(value):
    return 0.5 * jnp.tanh(0.5 * value) + 0.5


def factors(x, a, g):
    s = sigmoid(a)
    gate = sigmoid(g)
    nonlinear = a * s
    left = 1 - gate
    gap = x - nonlinear
    return nonlinear + gate * gap, left * (s + nonlinear * (1 - s)), gap * gate * left, gate


def forward_kernel(n_own, n_pieces, rows, width, table_ref, bias_ref, *refs):
    own, refs = refs[:n_own], refs[n_own:]
    mate, refs = refs[:n_own], refs[n_own:]
    pieces, refs = refs[:n_pieces], refs[n_pieces:]
    next_ref, low_ref, first_ref, second_ref, gate_ref, weight, sems = refs

    @pl.when(pl.program_id(0) == 0)
    def _():
        load_pieces(table_ref, pieces, rows, weight, sems)

    for j, x in enumerate(own):
        cols = slice(j * width, (j + 1) * width)
        a = hidden_of(own + mate, weight, 0, cols, bias_ref)
        g = hidden_of(own + mate, weight, 1, cols, bias_ref)
        value, first, second, gate = factors(x[...].astype(F32), a, g)
        next_ref[:, cols] = value
        low_ref[:, cols] = value.astype(BF16)
        first_ref[:, cols] = first.astype(BF16)
        second_ref[:, cols] = second.astype(BF16)
        gate_ref[:, cols] = gate.astype(BF16)


def column_sums(sums_ref, cols, d_first, d_gate):
    sums_ref[0:1, cols] += jnp.sum(d_first.astype(F32), axis=0, keepdims=True)
    sums_ref[1:2, cols] += jnp.sum(d_gate.astype(F32), axis=0, keepdims=True)


def product_back(out_ref, d_first, d_gate, weight, base, up=None):
    width = min(512, out_ref.shape[1])
    for j in range(out_ref.shape[1] // width):
        cols = slice(j * width, (j + 1) * width)
        rows = slice(base + j * width, base + (j + 1) * width)
        value = nt(d_first[...], weight[0, rows, :]) + nt(d_gate[...], weight[1, rows, :])
        if up is not None:
            value = value + up[:, cols]
        out_ref[:, cols] = value.astype(out_ref.dtype)


def turn_kernel(n_pieces, rows, width, packed, table_ref, bias_ref, own, mate, exact, out_grad, *refs):
    if packed:
        pieces, refs = refs[:n_pieces], refs[n_pieces:]
        low_ref, d_first_ref, d_gate_ref, up_ref, leaving_ref, vectors_ref, sums_ref, weight, sems, proj, proj_sems = refs
        proj_rows = (proj, proj_sems)
    else:
        proj, pieces, refs = refs[0], refs[1 : n_pieces + 1], refs[n_pieces + 1 :]
        low_ref, d_first_ref, d_gate_ref, up_ref, leaving_ref, vectors_ref, sums_ref, weight, sems = refs
        proj_rows = None

    @pl.when(pl.program_id(0) == 0)
    def _():
        load_pieces(table_ref, pieces, rows, weight, sems, None, proj_rows)
        sums_ref[...] = jnp.zeros_like(sums_ref)

    half = own.shape[1]
    for j in range(half // width):
        cols = slice(j * width, (j + 1) * width)
        a = hidden_of((own, mate), weight, 0, cols, bias_ref)
        g = hidden_of((own, mate), weight, 1, cols, bias_ref)
        dy = nt(out_grad[...], proj[cols, :])
        value, first, second, gate = factors(exact[:, cols], a, g)
        low_ref[:, cols] = value.astype(BF16)
        d_first, d_gate = (dy * first).astype(BF16), (dy * second).astype(BF16)
        d_first_ref[:, cols] = d_first
        d_gate_ref[:, cols] = d_gate
        up_ref[:, cols] = dy * gate
        column_sums(sums_ref, cols, d_first, d_gate)
    product_back(leaving_ref, d_first_ref, d_gate_ref, weight, half)
    vectors_ref[...] = nn(low_ref[...], proj[...])


def slope_kernel(n_pieces, rows, width, table_ref, partial, arrived, first_ref, second_ref, gate_ref, *refs):
    pieces, refs = refs[:n_pieces], refs[n_pieces:]
    d_first_ref, d_gate_ref, up_ref, leaving_ref, sums_ref, weight, sems = refs

    @pl.when(pl.program_id(0) == 0)
    def _():
        load_pieces(table_ref, pieces, rows, weight, sems, 1)
        sums_ref[...] = jnp.zeros_like(sums_ref)

    for j in range(partial.shape[1] // width):
        cols = slice(j * width, (j + 1) * width)
        dy = partial[:, cols] + arrived[:, cols].astype(F32)
        d_first, d_gate = (dy * first_ref[:, cols].astype(F32)).astype(BF16), (dy * second_ref[:, cols].astype(F32)).astype(BF16)
        d_first_ref[:, cols] = d_first
        d_gate_ref[:, cols] = d_gate
        up_ref[:, cols] = dy * gate_ref[:, cols].astype(F32)
        column_sums(sums_ref, cols, d_first, d_gate)
    product_back(leaving_ref, d_first_ref, d_gate_ref, weight, 0)


def back_kernel(n_pieces, rows, table_ref, d_first, d_gate, up, *refs):
    pieces, refs = refs[:n_pieces], refs[n_pieces:]
    out_ref, weight, sems = refs

    @pl.when(pl.program_id(0) == 0)
    def _():
        load_pieces(table_ref, pieces, rows, weight, sems, 0)

    product_back(out_ref, d_first, d_gate, weight, 0, up)


def weight_grad_kernel(n_chunks, n_cols, n_d, width, table_ref, *refs):
    xs, refs = refs[: n_chunks * n_cols], refs[n_chunks * n_cols :]
    d_first, d_gate, refs = refs[:n_d], refs[n_d : 2 * n_d], refs[2 * n_d :]
    outs, turned = refs[:-1], refs[-1]
    rows = outs[0].shape[2]

    @pl.when(pl.program_id(0) == 0)
    def _():
        word = 0
        for chunk in range(n_chunks):
            at = 0
            for x in xs[chunk * n_cols : (chunk + 1) * n_cols]:
                turned[at : at + x.shape[1], word : word + x.shape[0]] = x[...].T
                at += x.shape[1]
            word += x.shape[0]

    blocks = d_first[0].shape[1] // width
    for side in range(2):
        row = table_ref[side, pl.program_id(0)]
        left = turned[pl.ds(pl.multiple_of(row, rows), rows), :]
        for j in range(blocks):
            cols = slice(j * width, (j + 1) * width)
            out = outs[blocks].at[j] if side else outs[j]
            for unit, ds in enumerate((d_first, d_gate)):
                total, word = 0.0, 0
                for d in ds:
                    total = total + nn(left[:, word : word + d.shape[0]], d[:, cols])
                    word += d.shape[0]
                out[0, unit] = total.astype(BF16)


SMEM_SPEC = pl.BlockSpec(memory_space=pltpu.SMEM)
ANY_SPEC = pl.BlockSpec(memory_space=pl.ANY)


def whole(array):
    return pl.BlockSpec(array.shape, lambda i: (0,) * array.ndim)


def by_rows(rows, width, base=0):
    return pl.BlockSpec((rows, width), lambda i: (base + i, 0))


def params(**kw):
    return pltpu.CompilerParams(vmem_limit_bytes=58 * MIB, **kw)


def count_of(pieces):
    return sum(piece.shape[0] for piece in pieces)


def highway_forward(table, pieces, block_rows, bias, own, mate, chunk, words):
    width = own[0].shape[1]
    half = width * len(own)
    rows = min(ROWS, words)
    steps = words // rows
    tile = by_rows(rows, width, chunk * steps)
    out = by_rows(rows, half)
    return pl.pallas_call(
        functools.partial(forward_kernel, len(own), len(pieces), block_rows, width),
        grid=(steps,),
        in_specs=[SMEM_SPEC, whole(bias)] + [tile] * (2 * len(own)) + [ANY_SPEC] * len(pieces),
        out_specs=[out] * 5,
        out_shape=[jax.ShapeDtypeStruct((words, half), kind) for kind in (F32, BF16, BF16, BF16, BF16)],
        scratch_shapes=[pltpu.VMEM((2, 2 * half, half), BF16), pltpu.SemaphoreType.DMA((count_of(pieces),))],
        compiler_params=params(),
        cost_estimate=lasting(10),
        name="highway_forward",
    )(table, bias, *own, *mate, *pieces)


def highway_turn(table, pieces, block_rows, bias, own, mate, exact, out_grad, proj, width):
    words, half = own.shape
    out_width = out_grad.shape[1]
    rows = min(ROWS, words)
    tile = by_rows(rows, half)
    packed = proj is None
    scratch = [pltpu.VMEM((2, 2 * half, half), BF16), pltpu.SemaphoreType.DMA((count_of(pieces),))]
    if packed:
        scratch += [pltpu.VMEM((half, out_width), BF16), pltpu.SemaphoreType.DMA((2 * count_of(pieces),))]
    return pl.pallas_call(
        functools.partial(turn_kernel, len(pieces), block_rows, width, packed),
        grid=(words // rows,),
        in_specs=[SMEM_SPEC, whole(bias), tile, tile, tile, by_rows(rows, out_width)]
        + ([] if packed else [whole(proj)])
        + [ANY_SPEC] * len(pieces),
        out_specs=[tile] * 5 + [by_rows(rows, out_width), pl.BlockSpec((2, half), lambda i: (0, 0))],
        out_shape=[jax.ShapeDtypeStruct((words, half), kind) for kind in (BF16, BF16, BF16, F32, BF16)]
        + [jax.ShapeDtypeStruct((words, out_width), F32), jax.ShapeDtypeStruct((2, half), F32)],
        scratch_shapes=scratch,
        compiler_params=params(),
        cost_estimate=lasting(16),
        name="highway_turn",
    )(table, bias, own, mate, exact, out_grad, *([] if packed else [proj]), *pieces)


def highway_slopes(table, pieces, block_rows, partial, arrived, first, second, gate, width):
    words, half = partial.shape
    rows = min(ROWS, words)
    tile = by_rows(rows, half)
    return pl.pallas_call(
        functools.partial(slope_kernel, len(pieces), block_rows, width),
        grid=(words // rows,),
        in_specs=[SMEM_SPEC] + [tile] * 5 + [ANY_SPEC] * len(pieces),
        out_specs=[tile, tile, tile, tile, pl.BlockSpec((2, half), lambda i: (0, 0))],
        out_shape=[jax.ShapeDtypeStruct((words, half), kind) for kind in (BF16, BF16, F32, BF16)] + [jax.ShapeDtypeStruct((2, half), F32)],
        scratch_shapes=[pltpu.VMEM((2, half, half), BF16), pltpu.SemaphoreType.DMA((count_of(pieces),))],
        compiler_params=params(),
        cost_estimate=lasting(8),
        name="highway_slopes",
    )(table, partial, arrived, first, second, gate, *pieces)


def highway_back(table, pieces, block_rows, d_first, d_gate, up):
    words, width = d_first.shape
    rows = min(ROWS, words)
    tile = by_rows(rows, width)
    return pl.pallas_call(
        functools.partial(back_kernel, len(pieces), block_rows),
        grid=(words // rows,),
        in_specs=[SMEM_SPEC, tile, tile, tile] + [ANY_SPEC] * len(pieces),
        out_specs=tile,
        out_shape=jax.ShapeDtypeStruct((words, width), F32),
        scratch_shapes=[pltpu.VMEM((2, width, width), BF16), pltpu.SemaphoreType.DMA((count_of(pieces),))],
        compiler_params=params(),
        cost_estimate=lasting(6),
        name="highway_back",
    )(table, d_first, d_gate, up, *pieces)


def highway_weight_grad(table, xs, d_first, d_gate, rows, width):
    half = d_first[0].shape[1]
    words = sum(d.shape[0] for d in d_first)
    flat = [x for row in xs for x in row]
    steps = table.shape[1]
    blocks = half // width
    block = pl.BlockSpec((1, 2, rows, width), lambda i: (i, 0, 0, 0))
    return pl.pallas_call(
        functools.partial(weight_grad_kernel, len(xs), len(xs[0]), len(d_first), width),
        grid=(steps,),
        in_specs=[SMEM_SPEC] + [whole(x) for x in flat] + [whole(d) for d in d_first + d_gate],
        out_specs=[block] * blocks + [pl.BlockSpec((blocks, 1, 2, rows, width), lambda i: (0, i, 0, 0, 0))],
        out_shape=[jax.ShapeDtypeStruct((steps, 2, rows, width), BF16)] * blocks
        + [jax.ShapeDtypeStruct((blocks, steps, 2, rows, width), BF16)],
        scratch_shapes=[pltpu.VMEM((2 * half, words), BF16)],
        compiler_params=params(),
        cost_estimate=lasting(15),
        name="highway_weight_grad",
    )(table, *flat, *d_first, *d_gate)


def adam_update(weight, grad, moment_one, moment_two, rate):
    first_new = beta_one * moment_one + (1 - beta_one) * grad
    second_new = beta_two * moment_two + (1 - beta_two) * grad * grad
    corrected_one = first_new / (1 - beta_one**STEP)
    corrected_two = second_new / (1 - beta_two**STEP)
    updated = weight - rate * (
        corrected_one / (jnp.sqrt(corrected_two) + adam_eps) + decay_rate * weight
    )
    return (second_new, updated)


def owner_kernel(n_grads, at_ref, *refs):
    grads, refs = refs[:n_grads], refs[n_grads:]
    weight, one, two, average = refs[:4]
    grad, second, new, average_new = refs[-4:]
    width = grads[0].shape[2]
    for j, ref in enumerate(grads):
        at = pl.ds(pl.multiple_of(at_ref[j], LANES), width)
        grad[:, :, at] = ref[...].astype(F32)
    second_new, updated = adam_update(weight[...], grad[...], one[...], two[...], 0.02)
    second[...] = second_new
    new[...] = updated
    average_new[...] = average_keep * average[...] + (1 - average_keep) * updated


def owner_update(slot, at, grads, weight, one, two, average, so_far=()):
    slots, rows, width = grads[0].shape
    part = min(64, rows)
    block = pl.BlockSpec((1, part, weight.shape[2]), lambda i: (slot, i, 0))
    given = len(grads) + 5
    return pl.pallas_call(
        functools.partial(owner_kernel, len(grads)),
        grid=(rows // part,),
        in_specs=[SMEM_SPEC]
        + [pl.BlockSpec((1, part, width), lambda i: (slot, i, 0))] * len(grads)
        + [block] * 4
        + [ANY_SPEC] * len(so_far),
        out_specs=[block] * 4,
        out_shape=[jax.ShapeDtypeStruct(weight.shape, F32)] * 4,
        input_output_aliases={given + n: n for n in range(len(so_far))},
        compiler_params=params(),
        cost_estimate=lasting(8),
        name="owner_update",
    )(at, *grads, weight, one, two, average, *so_far)


def slot_of(owner_ref, unit):
    return sum(jnp.where(owner_ref[before] == owner_ref[unit], 1, 0) for before in range(unit)) if unit else 0


def choose_kernel(n_from, owner_ref, proj, *refs):
    arrived, outs = refs[:n_from], refs[n_from:]
    rows, width = arrived[0].shape[1:]
    here = lax.axis_index("filt")
    for unit in range(UNITS):
        for step, ref in enumerate(arrived):

            @pl.when(owner_ref[unit] ^ here == step)
            def _(ref=ref, unit=unit):
                outs[unit // 2][unit % 2, :rows, :] = ref[slot_of(owner_ref, unit)]

    under, part = proj.shape[0], proj.shape[1] // 2
    if outs[1].shape[1] > rows:
        outs[1][:, rows:, :] = jnp.zeros((2, under, width), BF16)
        for side in range(2):
            outs[1][side, rows:, :part] = proj[:, side * part : (side + 1) * part].astype(BF16)


def choose_units(owners, arrived, proj, packed):
    slots, rows, width = arrived[0].shape
    shapes = [(2, rows, width), (2, rows + (proj.shape[0] if packed else 0), width)]
    return pl.pallas_call(
        functools.partial(choose_kernel, len(arrived)),
        grid=(1,),
        in_specs=[SMEM_SPEC, whole(proj)] + [whole(part) for part in arrived],
        out_specs=[pl.BlockSpec(shape, lambda i: (0, 0, 0)) for shape in shapes],
        out_shape=[jax.ShapeDtypeStruct(shape, BF16) for shape in shapes],
        compiler_params=params(),
        cost_estimate=lasting(3),
        name="choose_units",
    )(owners, proj, *arrived)


def return_kernel(counts, owner_ref, *refs):
    layers = (refs[: counts[0]], refs[counts[0] : counts[0] + counts[1]])
    here = lax.axis_index("filt")
    for step, out in enumerate(refs[counts[0] + counts[1] :]):
        for slot in range(SLOTS):
            taken = -1
            for unit in range(UNITS):
                fits = (owner_ref[unit] ^ here == step) & (slot_of(owner_ref, unit) == slot)
                taken = jnp.where(fits, unit, taken)
            for unit in range(UNITS):

                @pl.when(taken == unit)
                def _(unit=unit, out=out, slot=slot):
                    out[slot] = sum(ref[unit % 2].astype(F32) for ref in layers[unit // 2]).astype(BF16)

            @pl.when(taken < 0)
            def _(out=out, slot=slot):
                out[slot] = jnp.zeros(out.shape[1:], BF16)


def return_units(owners, layers, count):
    shape = layers[0][0].shape
    part = min(128, shape[1])
    block = pl.BlockSpec((2, part, shape[2]), lambda i: (0, i, 0))
    terms = list(layers[0]) + list(layers[1])
    return pl.pallas_call(
        functools.partial(return_kernel, [len(layer) for layer in layers]),
        grid=(shape[1] // part,),
        in_specs=[SMEM_SPEC] + [block] * len(terms),
        out_specs=[block] * count,
        out_shape=[jax.ShapeDtypeStruct(shape, BF16)] * count,
        compiler_params=params(),
        cost_estimate=lasting(3),
        name="return_units",
    )(owners, *terms)


class Places:
    def __init__(self):
        self.n_filt, self.n_dp = lax.axis_size("filt"), lax.axis_size("dp")
        self.n_y, self.n_z = self.n_filt // 2, self.n_dp // 2
        self.f, self.d = lax.axis_index("filt"), lax.axis_index("dp")
        self.y, self.x = self.f // 2, self.f % 2
        self.z, self.c = self.d // 2, self.d % 2
        self.direct = self.n_y == 2 and self.n_z == 4

    def over_filt(self, value, step):
        return lax.ppermute(value, "filt", [(i, i ^ step) for i in range(self.n_filt)])

    def over_x(self, value):
        return self.over_filt(value, 1)

    def over_y(self, value, step):
        return self.over_filt(value, 2 * step)

    def over_core(self, value):
        return lax.ppermute(value, "dp", [(i, i ^ 1) for i in range(self.n_dp)])

    def over_z(self, value, step):
        pairs = [(i, (i // 2 + step) % self.n_z * 2 + i % 2) for i in range(self.n_dp)]
        return lax.ppermute(value, "dp", pairs)

    def far_first(self):
        return sorted(range(1, self.n_z), key=lambda k: (min(k, self.n_z - k), k))

    def row_of(self, d, rows, width):
        f = d * rows // width
        half = self.n_y * width
        return (f % 2 ^ self.x) * half + (f // 2 ^ self.y) * width + d * rows % width


def after(value, *earlier):
    return lax.optimization_barrier((value, earlier))[0]


def settle(*values):
    return lax.optimization_barrier(values)


def gather_general(place, blocks):
    rows, width = blocks[0].shape[1:]
    out = []
    for piece in blocks:
        spread = lax.all_gather(lax.all_gather(piece, "dp"), "filt")
        spread = spread.reshape((place.n_y, 2) + spread.shape[1:])
        spread = lax.dynamic_index_in_dim(spread, place.x, 1, keepdims=False)
        spread = spread.reshape((place.n_y * place.n_dp,) + piece.shape)
        d = jnp.tile(jnp.arange(place.n_dp, dtype=jnp.int32), place.n_y)
        y = jnp.repeat(jnp.arange(place.n_y, dtype=jnp.int32), place.n_dp)
        table = jnp.stack([place.row_of(d, rows, width), (y ^ place.y) * width]).astype(jnp.int32)
        out.append((table, [spread]))
    return out


BLOCK_STEPS = (
    [(0, 0), (0, 1), (1, 0), (3, 0), (2, 0), (1, 1), (3, 1), (2, 1)],
    [(0, 0), (0, 1), (1, 0), (3, 0), (1, 1), (3, 1), (2, 0), (2, 1)],
)


def gather_table(place, layer, rows, width, rows_proj):
    at_rows, at_cols, at_proj = [], [], []
    for other in range(2):
        for k, step in BLOCK_STEPS[layer]:
            d = (place.z - k) % place.n_z * 2 + (place.c ^ other)
            at_rows.append(place.row_of(d, rows, width))
            at_cols.append(jnp.int32(step * width))
            at_proj.append(step * width + d * rows_proj)
    return jnp.stack([jnp.stack(at_rows), jnp.stack(at_cols), jnp.stack(at_proj)]).astype(jnp.int32)


def sum_table(place, rows, width):
    z = jnp.arange(place.n_z, dtype=jnp.int32)
    z, c = ((place.z + z) % place.n_z, place.c) if place.direct else (z, 0)
    return jnp.stack([place.row_of(z * 2 + c, rows, width), place.row_of(z * 2 + (1 - c), rows, width)]).astype(jnp.int32)


def sent_over_y(parts, group):
    near, arrived = parts
    return (near[1][group].astype(F32) + arrived[1][group].astype(F32)).astype(BF16)


def kept_over_y(parts, turned, group):
    near, arrived = parts
    steps = range(group.start, group.stop)
    return [near[0][k].astype(F32) + arrived[0][k].astype(F32) + turned[n].astype(F32) for n, k in enumerate(steps)]


def sum_general(place, blocks):
    n_y = place.n_y
    near, far = blocks[:n_y], list(blocks[n_y])
    steps = jnp.arange(n_y, dtype=jnp.int32) ^ place.y
    pairs = jnp.stack([jnp.stack(near), jnp.stack(far)], axis=2)
    pairs = jnp.take(pairs, steps, axis=0)
    pairs = pairs.reshape((n_y, place.n_dp) + pairs.shape[3:])
    mine = lax.psum_scatter(pairs, "dp", scatter_dimension=1)
    sides = jnp.arange(2, dtype=jnp.int32).reshape(1, 2, 1, 1, 1)
    mine = jnp.where(sides == place.x, mine[:, None], jnp.zeros((), BF16))
    mine = mine.reshape((place.n_filt,) + mine.shape[2:])
    return lax.psum_scatter(mine, "filt", scatter_dimension=0).astype(F32)


def pick(array, at, axis=0):
    return lax.dynamic_index_in_dim(array, at, axis, keepdims=False)


def rows_over_core(place, value):
    parts = value.reshape((place.n_z, 2, -1) + value.shape[1:])
    return pick(parts, place.c, 1), over_core_low(place, pick(parts, 1 - place.c, 1))


def over_core_low(place, value):
    return place.over_core(value.astype(BF16))


def swap_z(place, value, step):
    pairs = [(i, i ^ (2 * step)) for i in range(place.n_dp)]
    return lax.ppermute(value, "dp", pairs)


def swap_rows(place, parts, step):
    upper = place.z // step % 2
    halves = parts.reshape((2, -1) + parts.shape[1:])
    return pick(halves, upper), swap_z(place, pick(halves, 1 - upper).astype(BF16), step)


def sum_filt(place, value):
    if not place.direct:
        return lax.psum(value, "filt")
    step = 1
    while step < place.n_filt:
        value = value + place.over_filt(value, step)
        step *= 2
    return value


def per_device(
    char_ids,
    word_lengths,
    out_grad,
    highway_owner,
    char_table,
    conv_weight,
    conv_bias,
    highway_weight,
    proj_weight,
    dense_bias,
    table_moment_one,
    table_moment_two,
    conv_moment_one,
    conv_moment_two,
    conv_bias_moment_one,
    conv_bias_moment_two,
    highway_moment_one,
    highway_moment_two,
    highway_average,
    proj_moment_one,
    proj_moment_two,
    bias_moment_one,
    bias_moment_two,
):
    place = Places()
    n_y, n_filt, direct = place.n_y, place.n_filt, place.direct
    width = conv_weight.shape[1]
    rows, width_full = highway_weight.shape[1:]
    half = width_full // 2
    rows_proj, out_width = proj_weight.shape
    vocab_count = char_table.shape[0]
    words_dev = char_ids.shape[0]
    words_y = words_dev // n_y
    chunks, chunk_words = range(2), words_y // 2
    steps_y = list(range(1, n_y))
    mine_first = place.x == 0
    over_core, over_x, over_y, over_z = place.over_core, place.over_x, place.over_y, place.over_z

    widths = channel_widths(place.f * width, width, FILTERS)
    offsets = jnp.arange(TAPS, dtype=jnp.int32) // CHAR_DIM
    tap_mask = (offsets[:, None] < widths[None, :]).astype(jnp.float32)
    tile = min(256, words_dev)
    n_tiles = words_dev // tile
    cuts = [0, 1, 2, 4, 8] if n_tiles == 8 else [0, n_tiles]
    splits = list(zip(cuts[:-1], cuts[1:]))
    rank, data, table_t, conv_t, conv_back, width_col, narrow = conv_operands(
        char_ids, word_lengths, char_table, conv_weight, conv_bias, widths, width
    )
    rank_parts = [lax.dynamic_slice_in_dim(rank, (place.y ^ step) * words_y, words_y, axis=0) for step in range(n_y)]

    def convolve(some, narrow):
        return [conv_forward(rank, data, table_t, conv_t, width_col, narrow, width, begin, end - begin) for begin, end in some]

    def block_of(step):
        start = (place.f ^ step) * width
        return lax.dynamic_slice_in_dim(highway_weight, start, width, axis=2).astype(BF16)

    from_owner = [block_of(0)] + [place.over_filt(block_of(step), step) for step in range(1, n_filt)]
    kept = convolve(splits[: len(splits) // 2], narrow)
    from_owner, kept, narrow = settle(from_owner, kept, narrow)
    blocks = choose_units(highway_owner, from_owner, proj_weight, direct)
    bias_float = lax.reduce_precision(dense_bias, 8, 7)

    def half_bias(unit):
        starts = [unit * width_full + (2 * (place.y ^ step) + place.x) * width for step in range(n_y)]
        return jnp.concatenate([lax.dynamic_slice_in_dim(bias_float, start, width) for start in starts])

    layer_bias = [jnp.stack([half_bias(2 * layer), half_bias(2 * layer + 1)]) for layer in range(2)]

    blocks, narrow, sent, layer_bias = settle(blocks, narrow, out_grad, layer_bias)
    grad_mate = over_x(sent)
    if direct:
        first_y = [over_y(block, 1) for block in blocks]
        near = [over_z(blocks[0], k) for k in (1, 3)]
    kept = kept + convolve(splits[len(splits) // 2 :], narrow)
    placed = [place_words(part, [parts[0] for parts in kept]) for part in rank_parts]
    own = [placed[0]] + [over_y(placed[step], step) for step in steps_y]
    if direct:
        near, first_y, placed, grad_mate, blocks = settle(near, first_y, placed, grad_mate, blocks)
        own = [placed[0], over_y(placed[1], 1)]
        mate = [over_x(placed[0])]
        far = over_z(blocks[0], 2)
        sent = jnp.stack([near[0], near[1], jnp.zeros_like(near[0])])
        own, mate, far, sent, blocks, first_y, layer_bias, grad_mate = settle(
            own, mate, far, sent, blocks, first_y, layer_bias, grad_mate
        )

        out_grads = [jnp.where(mine_first, out_grad, grad_mate), jnp.where(mine_first, grad_mate, out_grad)]
        out_sum = jnp.sum(out_grad, axis=0, dtype=F32)
        sent = lax.dynamic_update_index_in_dim(sent, far, 2, 0)
        sent_y = over_y(sent, 1)
        mate = mate + [over_x(own[1])]
        near_one = [over_z(blocks[1], k) for k in (1, 3)]
        sent_core = over_core(sent)
        start = jnp.stack([blocks[0], first_y[0]])
        table = [gather_table(place, layer, rows, width, rows_proj) for layer in range(2)]
        sent_y, sent_core, start, mate, near_one, blocks, out_grads, table, out_sum = settle(
            sent_y, sent_core, start, mate, near_one, blocks, out_grads, table, out_sum
        )

        gathered = [(table[0], [start, sent, sent_y, over_core(start), sent_core, over_core(sent_y)], rows)]
        far_one = over_z(blocks[1], 2)
        near_y = over_y(jnp.stack(near_one), 1)
    else:
        mate = [over_x(part) for part in own]
        gathered = [(*found, rows) for found in gather_general(place, blocks)]
        out_sum = jnp.sum(out_grad, axis=0, dtype=F32)
        out_grads = [jnp.where(mine_first, out_grad, grad_mate), jnp.where(mine_first, grad_mate, out_grad)]

    forward, x_one_mate = [], []
    for chunk in chunks:
        forward.append(highway_forward(*gathered[0], layer_bias[0], own, mate, chunk, chunk_words))
        x_one_mate.append(over_x(forward[chunk][1]))
        if direct and chunk == 0:
            forward[0], near_one, layer_bias[0] = settle(forward[0], near_one, layer_bias[0])
            start = jnp.stack([blocks[1], first_y[1], near_one[0], near_one[1]])
            start_core = over_core(start)
    if direct:
        far_one, near_y, forward[1] = settle(far_one, near_y, forward[1])
        far_y = over_y(far_one, 1)
        far_y, x_one_mate[0] = settle(far_y, x_one_mate[0])
        last = jnp.stack([near_y[0], near_y[1], far_one, far_y])
        gathered.append((table[1], [start, last, start_core, over_core(last)], rows))
        proj_half = None
    else:
        proj_own = jnp.stack([proj_weight.astype(BF16)] + [over_y(proj_weight.astype(BF16), step) for step in steps_y])
        proj_half = lax.all_gather(proj_own, "dp", axis=1).reshape(half, out_width)
    x_one, x_one_low, first_zero, second_zero, gate_zero = zip(*forward)
    turned, arrived = [], []
    for chunk in chunks:
        bias_one = layer_bias[1] if chunk == 0 else settle(layer_bias[1], turned[0])[0]
        turned.append(
            highway_turn(*gathered[1], bias_one, x_one_low[chunk], x_one_mate[chunk], x_one[chunk], out_grads[chunk], proj_half, width)
        )
        arrived.append(over_x(turned[chunk][4]))
    x_two_low, d_first_one, d_gate_one, up_one, _, vectors, sums = (list(parts) for parts in zip(*turned))
    sums_one = sums[0] + sums[1]

    targets = sum_table(place, rows, width)
    blocks = highway_weight_grad(
        targets, [[x_one_low[chunk], x_one_mate[chunk]] for chunk in chunks], d_first_one, d_gate_one, rows, width
    )
    blocks, up_one[0], arrived[0] = settle(blocks, up_one[0], arrived[0])
    if not direct:
        sum_one = sum_general(place, blocks)

    partial, parts_zero, arrived_zero = [], [], []
    for chunk in chunks:
        partial.append(highway_back(*gathered[1], d_first_one[chunk], d_gate_one[chunk], up_one[chunk]))
        if chunk == 0 and direct:
            partial[0], arrived[1], blocks = settle(partial[0], arrived[1], blocks)
            one = (blocks[:2], over_core(blocks[2]))
        parts_zero.append(
            highway_slopes(*gathered[0], partial[chunk], arrived[chunk], first_zero[chunk], second_zero[chunk], gate_zero[chunk], width)
        )
        if chunk == 0 and direct:
            one, parts_zero[0], up_one[1] = settle(one, parts_zero[0], up_one[1])
            sent = sent_over_y(one, slice(0, place.n_z))
            sent, up_one[1] = settle(sent, up_one[1])
            one_y = over_y(sent, 1)
        arrived_zero.append(over_x(parts_zero[chunk][3]))
    d_first, d_gate, up, _, sums = (list(parts) for parts in zip(*parts_zero))
    sums_zero = sums[0] + sums[1]
    blocks = highway_weight_grad(targets, [own + mate], d_first, d_gate, rows, width)
    blocks, up, arrived_zero[0] = settle(blocks, up, arrived_zero[0])
    groups = [slice(2, 4), slice(0, 2)]
    if not direct:
        sum_zero = sum_general(place, blocks)
    partial = [highway_back(*gathered[0], d_first[chunk], d_gate[chunk], up[chunk]) for chunk in chunks]
    if direct:
        partial, blocks, arrived_zero[1], one_y = settle(partial, blocks, arrived_zero[1], one_y)
        zero = (blocks[:2], over_core(blocks[2]))
    if direct:
        one_here = kept_over_y(one, one_y, slice(0, place.n_z))
        one_sent = [one_here[k].astype(BF16) for k in (2, 1, 3)]
        one_here = one_here[0]
        one_sent, one_here, partial = settle(one_sent, one_here, partial)
        one_z = [over_z(value, k) for value, k in zip(one_sent, (2, 1, 3))]
    groups = [slice(2, 4), slice(0, 2)]
    if not direct:
        sum_zero = sum_general(place, blocks)
    partial = [highway_back(*gathered[0], d_first[chunk], d_gate[chunk], up[chunk]) for chunk in chunks]
    if direct:
        partial, blocks, arrived_zero[1], one_y = settle(partial, blocks, arrived_zero[1], one_y)
        zero = (blocks[:2], over_core(blocks[2]))
    feature_grad = []
    for step in range(n_y):
        cols = slice(step * width, (step + 1) * width)
        feature_grad.append(
            jnp.concatenate(
                [(partial[chunk][:, cols] + arrived_zero[chunk][:, cols].astype(F32)).astype(BF16) for chunk in chunks]
            )
        )
    groups = [slice(2, 4), slice(0, 2)]
    returned = [over_y(value, step) if step else value for step, value in enumerate(feature_grad)]
    if direct:
        returned[0], x_two_low, vectors = settle(returned[0], x_two_low, vectors)
        zero_y = [over_y(sent_over_y(zero, groups[0]), 1)]
    proj_part = (tn(x_two_low[0], out_grads[0]) + tn(x_two_low[1], out_grads[1])).reshape(n_y, width, out_width)
    proj_here, proj_away = proj_part[0], [proj_part[step].astype(BF16) for step in steps_y]
    vectors_away = jnp.where(mine_first, vectors[1], vectors[0]).astype(BF16)
    vectors_here = jnp.where(mine_first, vectors[0], vectors[1])
    ranks = [part.T for part in rank_parts]

    if direct:
        zero_sent = sent_over_y(zero, groups[1])
        returned, narrow, ranks, zero_sent = settle(returned, narrow, ranks, zero_sent)

    def convolve_back(n, narrow, so_far):
        (begin, _), (_, lse, sorted_ids, embedded) = splits[n], kept[n]
        return conv_backward(
            ranks, sorted_ids, embedded, vocab_count, conv_t, conv_back, width_col, narrow, lse, returned, width, begin, tile, so_far
        )

    home = jnp.arange(n_filt, dtype=jnp.int32)

    def natural(values):
        parts = values.reshape(n_y, 1, width)
        out = jnp.zeros((n_filt, width), F32)
        for step in range(n_y):
            out = jnp.where((home == 2 * (place.y ^ step) + place.x)[:, None], parts[step], out)
        return out.reshape(-1)

    bias_local = jnp.concatenate(
        [natural(sums[unit]) for sums in (sums_zero, sums_one) for unit in range(2)] + [out_sum]
    )
    table_rows = table_t.shape[1] // LANES * CHAR_DIM
    bias_rows = -(-bias_local.size // DEPTH)
    bias_rows += -(width + table_rows + bias_rows) % 16
    bias_flat = jnp.pad(bias_local, (0, bias_rows * DEPTH - bias_local.size)).reshape(bias_rows, DEPTH)
    small = jnp.concatenate([jnp.zeros((width + table_rows, DEPTH), F32), bias_flat])
    if direct:
        small, returned, narrow = settle(small, returned, narrow)
    back = small
    for n in range(len(splits)):
        back = convolve_back(n, narrow, back)
        if direct and n == 0:
            back, narrow, one_z, zero_y[0], zero, vectors_away, proj_away = settle(
                back, narrow, one_z, zero_y[0], zero, vectors_away, proj_away
            )
            zero_here = kept_over_y(zero, zero_y[0], groups[0])
            zero_z, zero_sent, narrow = settle([value.astype(BF16) for value in zero_here], zero_sent, narrow)
            zero_z = [over_z(value, k) for value, k in zip(zero_z, (2, 3))]
            zero_y.append(over_y(zero_sent, 1))
            vectors_arrived = over_x(vectors_away)
        if direct and n == 2:
            back, zero_z, narrow, zero_y, vectors_arrived, proj_away = settle(back, zero_z, narrow, zero_y, vectors_arrived, proj_away)
            zero_here, last = kept_over_y(zero, zero_y[1], groups[1])
            last, zero_here, narrow = settle(last.astype(BF16), zero_here, narrow)
            last = over_z(last, 1)
            proj_y = over_y(proj_away[0], 1)
    if direct:
        back, last, proj_y = settle(back, last, proj_y)
        slot_grads = return_units(highway_owner, [[zero_here] + zero_z + [last], [one_here] + one_z], n_filt)
    else:
        proj_y = [over_y(value, step) for value, step in zip(proj_away, steps_y)]
        proj_grad = lax.psum_scatter(proj_here + sum(value.astype(F32) for value in proj_y), "dp", scatter_dimension=0, tiled=True)
    if not direct:
        vectors_arrived = over_x(vectors_away)
    small = back
    if direct:
        small = small + over_core(small)
    else:
        small = lax.psum(small, "dp")
        small = jnp.concatenate([small[:width], sum_filt(place, small[width:])])

    optimizer = (highway_weight, highway_moment_one, highway_moment_two, highway_average)
    columns = (place.f ^ jnp.arange(n_filt, dtype=jnp.int32)) * width
    if direct:
        slot_grads, small, proj_y, vectors_arrived = settle(slot_grads, small, proj_y, vectors_arrived)
        proj_rows = rows_over_core(place, proj_here + proj_y.astype(F32))
        arrived_slots = [place.over_filt(slot_grads[step], step) for step in range(1, n_filt)]
        small = small + swap_z(place, small.astype(BF16), 1).astype(F32)
        small = small + swap_z(place, small.astype(BF16), 2).astype(F32)
        small, arrived_slots, proj_rows = settle(small, arrived_slots, proj_rows)
        conv_sums, small = small[:width], small[width:]
        slot_grads = [slot_grads[0]] + arrived_slots
        small = small + over_x(small)
        proj_rows = swap_rows(place, proj_rows[0] + proj_rows[1].astype(F32), 2)
        updates = owner_update(0, columns, slot_grads, *optimizer)
        updates, small, proj_rows, slot_grads = settle(updates, small, proj_rows, slot_grads)
        small = small + over_y(small, 1)
        proj_rows = swap_rows(place, proj_rows[0] + proj_rows[1].astype(F32), 1)
        updates = owner_update(1, columns, slot_grads, *optimizer, updates)
        updates, small, proj_rows = settle(updates, small, proj_rows)
        proj_grad = (proj_rows[0] + proj_rows[1].astype(F32)).reshape(rows_proj, out_width)
    else:
        slot_grads = return_units(highway_owner, [[sum_zero], [sum_one]], n_filt)
        slot_grads = [slot_grads[0]] + [place.over_filt(slot_grads[step], step) for step in range(1, n_filt)]
        conv_sums, small = small[:width], small[width:]
        updates = owner_update(0, columns, slot_grads, *optimizer)
        updates = owner_update(1, columns, slot_grads, *optimizer, updates)
    highway_grad, highway_second, highway_new, highway_average_new = updates
    word_vectors = vectors_here + vectors_arrived.astype(F32) + bias_float[UNITS * width_full :]
    conv_grad, conv_bias_grad = conv_sums[:, :TAPS].T * tap_mask, conv_sums[:, TAPS]
    table_grad = small[:table_rows].reshape(-1, CHAR_DIM, LANES).transpose(0, 2, 1).reshape(-1, CHAR_DIM)[:vocab_count]
    bias_grad = small[table_rows:].reshape(-1)[: bias_local.size]
    table_second, table_new = adam_update(
        char_table, table_grad, table_moment_one, table_moment_two, 1.0
    )
    conv_second, conv_new = adam_update(
        conv_weight, conv_grad, conv_moment_one, conv_moment_two, 0.1
    )
    conv_bias_second, conv_bias_new = adam_update(
        conv_bias, conv_bias_grad, conv_bias_moment_one, conv_bias_moment_two, 0.3
    )
    proj_second, proj_new = adam_update(
        proj_weight, proj_grad, proj_moment_one, proj_moment_two, 0.02
    )
    bias_second, bias_new = adam_update(
        dense_bias, bias_grad, bias_moment_one, bias_moment_two, 0.3
    )
    return (
        word_vectors,
        table_grad,
        table_second,
        table_new,
        conv_grad,
        conv_second,
        conv_new,
        conv_bias_grad,
        conv_bias_second,
        conv_bias_new,
        highway_grad,
        highway_second,
        highway_new,
        highway_average_new,
        proj_grad,
        proj_second,
        proj_new,
        bias_grad,
        bias_second,
        bias_new,
    )


def solution(mesh):
    return jax.shard_map(
        per_device,
        mesh=mesh,
        in_specs=(
            P("dp", None),
            P("dp"),
            P(("dp", "filt"), None),
            P(),
            P(),
            P(None, "filt"),
            P("filt"),
            P("filt", "dp", None),
            P(("filt", "dp"), None),
            P(),
            P(),
            P(),
            P(None, "filt"),
            P(None, "filt"),
            P("filt"),
            P("filt"),
            P("filt", "dp", None),
            P("filt", "dp", None),
            P("filt", "dp", None),
            P(("filt", "dp"), None),
            P(("filt", "dp"), None),
            P(),
            P(),
        ),
        out_specs=(
            P(("dp", "filt"), None),
            P(),
            P(),
            P(),
            P(None, "filt"),
            P(None, "filt"),
            P(None, "filt"),
            P("filt"),
            P("filt"),
            P("filt"),
            P("filt", "dp", None),
            P("filt", "dp", None),
            P("filt", "dp", None),
            P("filt", "dp", None),
            P(("filt", "dp"), None),
            P(("filt", "dp"), None),
            P(("filt", "dp"), None),
            P(),
            P(),
            P(),
        ),
        check_vma=False,
    )
```

```python
import functools

import jax
import jax.numpy as jnp
from jax import lax
from jax.experimental import pallas as pl
from jax.experimental.pallas import tpu as pltpu
from jax.sharding import PartitionSpec as P

CHAR_DIM = 16
MAX_CHARS = 50
MAX_WIDTH = 7
FILTERS = 2048
UNITS = 4
SLOTS = 2
STEP = 10
TAPS = MAX_WIDTH * CHAR_DIM
DEPTH = 128
ID_SHIFT = 128
ID_ROWS = 64
SLOTS_E = MAX_CHARS + MAX_WIDTH - 1 + 8
LANES = 128
STEP_P = 4
ROWS = 256
beta_one = 0.9
beta_two = 0.999
adam_eps = 1e-08
decay_rate = 0.01
average_keep = 0.9
F32, BF16 = jnp.float32, jnp.bfloat16
MIB = 1 << 20


def lasting(us):
    return pl.CostEstimate(flops=int(us * 1e7), bytes_accessed=int(us * 3e4), transcendentals=0)


def nt(a, b):
    return lax.dot_general(a, b, (((1,), (1,)), ((), ())), preferred_element_type=F32)


def nn(a, b):
    return lax.dot_general(a, b, (((1,), (0,)), ((), ())), preferred_element_type=F32)


def tn(a, b):
    return lax.dot_general(a, b, (((0,), (0,)), ((), ())), preferred_element_type=F32)


def embed_tile(ids_ref, table_ref, lens, e_ref, longest):
    tile = lens.shape[1]
    e_ref[...] = jnp.zeros_like(e_ref)
    pieces = table_ref.shape[1] // LANES

    def fill(s, carry):
        for i in range(STEP_P):
            p = s * STEP_P + i
            row = ids_ref[pl.ds(p, 1), :].astype(jnp.int32)
            parts = []
            for lane in range(tile // LANES):
                idx = jnp.broadcast_to(row[:, lane * LANES : (lane + 1) * LANES], (CHAR_DIM, LANES))
                low = jnp.bitwise_and(idx, LANES - 1)
                value = jnp.zeros((CHAR_DIM, LANES), F32)
                for piece in range(pieces):
                    got = jnp.take_along_axis(table_ref[:, piece * LANES : (piece + 1) * LANES], low, axis=1)
                    value = jnp.where(lax.shift_right_logical(idx, 7) == piece, got, value)
                parts.append(value)
            value = jnp.concatenate(parts, axis=1) if len(parts) > 1 else parts[0]
            value = jnp.where(p < lens, value, 0.0)
            e_ref[pl.ds(pl.multiple_of(p * CHAR_DIM, CHAR_DIM), CHAR_DIM), :] = value.astype(BF16)
        return carry

    lax.fori_loop(0, (longest + STEP_P - 1) // STEP_P, fill, 0)


def limits_of(lens):
    row = lax.broadcasted_iota(jnp.int32, (CHAR_DIM, lens.shape[1]), 0)
    past = jnp.maximum(lens - (row - 2), 0)
    return jnp.where(row < 3, -1, jnp.where(row < 3 + MAX_WIDTH, past, 1 << 20))


def window_at(e_ref, limit, p):
    extra = jnp.where(p > limit, 1.0, 0.0).astype(BF16)
    taps = e_ref[pl.ds(pl.multiple_of(p * CHAR_DIM, CHAR_DIM), TAPS), :]
    return jnp.concatenate([taps, extra], axis=0)


SUB = 32


def windows_at(e_ref, limit, s):
    return jnp.concatenate([window_at(e_ref, limit, s * STEP_P + i) for i in range(STEP_P)], axis=1)


def in_halves(step, channels, longest, narrow_ref):
    both = steps_of(longest, narrow_ref[1])
    lax.fori_loop(0, both, functools.partial(step, channels), 0)
    lax.fori_loop(both, jnp.maximum(both, steps_of(longest, narrow_ref[0])), functools.partial(step, channels // 2), 0)


def steps_of(longest, narrow):
    return (jnp.maximum(longest - narrow, 0) + STEP_P) // STEP_P


def conv_forward_kernel(cblock, base, narrow_ref, rank_ref, data_ref, table_ref, conv_ref, width_ref, feat_ref, lse_ref, ids_ref, e_ref, top, total, pre):
    tile = ids_ref.shape[1]
    words = rank_ref.shape[0]
    first = (base + pl.program_id(0)) * tile
    lane = first + lax.broadcasted_iota(jnp.int32, (words, tile), 1)
    hot = jnp.where(rank_ref[...] == lane, 1.0, 0.0).astype(BF16)
    moved = nn(data_ref[...], hot)
    shift = jnp.where(lax.broadcasted_iota(jnp.int32, moved.shape, 0) < MAX_CHARS, float(ID_SHIFT), 0.0)
    moved = moved + shift
    ids_ref[...] = moved
    lens = (moved[MAX_CHARS : MAX_CHARS + 1, :] + 0.5).astype(jnp.int32)
    longest = jnp.max(lens)
    embed_tile(ids_ref, table_ref, lens, e_ref, longest)
    limit = limits_of(lens)
    channels = conv_ref.shape[0]
    top[...] = jnp.full_like(top, -1e30)
    total[...] = jnp.zeros_like(total)

    def step(rows, s, carry):
        pre[:rows, :] = nn(conv_ref[:rows, :], windows_at(e_ref, limit, s))
        for sub in range(0, rows, SUB):
            part = slice(sub, sub + SUB)
            values = [pre[part, i * tile : (i + 1) * tile] for i in range(STEP_P)]
            before = top[part, :]
            best = functools.reduce(jnp.maximum, values, before)
            top[part, :] = best
            total[part, :] = total[part, :] * jnp.exp(before - best) + sum(jnp.exp(value - best) for value in values)
        return carry

    in_halves(step, channels, longest, narrow_ref)
    span = jnp.maximum(lens - width_ref[...], 0)
    lse = top[...] + jnp.log(total[...])
    lse_ref[...] = lse
    pooled = lse - jnp.log((span + 1).astype(F32))
    feat_ref[...] = (pooled * jax.nn.sigmoid(pooled)).astype(BF16)


def place_kernel(rank_ref, *refs):
    feats, out_ref = refs[:-1], refs[-1]
    total, base = 0.0, 0
    for feat_ref in feats:
        shape = (rank_ref.shape[0], feat_ref.shape[1])
        lane = base + lax.broadcasted_iota(jnp.int32, shape, 1)
        hot = jnp.where(rank_ref[...] == lane, 1.0, 0.0).astype(BF16)
        total = total + nt(hot, feat_ref[...])
        base += shape[1]
    out_ref[...] = total.astype(BF16)


def conv_forward(rank, data, table_t, conv_t, widths, narrow, cblock, base, count):
    words, channels = rank.shape[0], conv_t.shape[0]
    tile = min(256, words)
    span = count * tile
    full = lambda *shape: pl.BlockSpec(shape, lambda i: (0,) * len(shape))
    column = lambda depth: pl.BlockSpec((depth, tile), lambda i: (0, i))
    return pl.pallas_call(
        functools.partial(conv_forward_kernel, cblock, base),
        grid=(count,),
        in_specs=[
            pl.BlockSpec(memory_space=pltpu.SMEM),
            full(words, 1),
            full(*data.shape),
            full(*table_t.shape),
            full(*conv_t.shape),
            full(channels, 1),
        ],
        out_specs=[column(channels), column(channels), column(ID_ROWS), column(SLOTS_E * CHAR_DIM)],
        out_shape=[
            jax.ShapeDtypeStruct((channels, span), BF16),
            pltpu.HBM((channels, span), F32),
            pltpu.HBM((ID_ROWS, span), F32),
            pltpu.HBM((SLOTS_E * CHAR_DIM, span), BF16),
        ],
        scratch_shapes=[
            pltpu.VMEM((cblock, tile), F32),
            pltpu.VMEM((cblock, tile), F32),
            pltpu.VMEM((cblock, STEP_P * tile), F32),
        ],
        compiler_params=pltpu.CompilerParams(vmem_limit_bytes=48 * MIB),
        cost_estimate=lasting(11),
        name="conv_forward",
    )(narrow, rank, data, table_t, conv_t, widths)


def place_words(rank, feats):
    words, channels = rank.shape[0], feats[0].shape[0]
    rows = min(256, words)
    return pl.pallas_call(
        place_kernel,
        grid=(words // rows,),
        in_specs=[pl.BlockSpec((rows, 1), lambda i: (i, 0))] + [pl.BlockSpec(feat.shape, lambda i: (0, 0)) for feat in feats],
        out_specs=pl.BlockSpec((rows, channels), lambda i: (i, 0)),
        out_shape=jax.ShapeDtypeStruct((words, channels), BF16),
        compiler_params=pltpu.CompilerParams(vmem_limit_bytes=48 * MIB),
        cost_estimate=lasting(4),
        name="place_words",
    )(rank, *feats)


def conv_backward_kernel(cblock, n_parts, base, narrow_ref, ids_ref, e_ref, conv_ref, back_ref, width_ref, lse_ref, *refs):
    ranks, grads, refs = refs[:n_parts], refs[n_parts : 2 * n_parts], refs[2 * n_parts :]
    so_far, sums_ref, table_grad_ref, de_ref, dpool, pre, d_pre, found = refs
    tile = ids_ref.shape[1]
    lanes = table_grad_ref.shape[0]
    channels = conv_ref.shape[0]
    first = (base + pl.program_id(0)) * tile

    @pl.when(pl.program_id(0) == 0)
    def _():
        sums_ref[...] = so_far[...]
        table_grad_ref[...] = jnp.zeros_like(table_grad_ref)

    lens = (ids_ref[MAX_CHARS : MAX_CHARS + 1, :] + 0.5).astype(jnp.int32)
    longest = jnp.max(lens)
    limit = limits_of(lens)
    de_ref[...] = jnp.zeros_like(de_ref)
    moved = 0.0
    for rank_ref, grad_ref in zip(ranks, grads):
        row = first + lax.broadcasted_iota(jnp.int32, (tile, rank_ref.shape[1]), 0)
        moved = moved + nn(jnp.where(rank_ref[...] == row, 1.0, 0.0).astype(BF16), grad_ref[...])
    moved = moved.T
    span = jnp.maximum(lens - width_ref[...], 0)
    pooled = lse_ref[...] - jnp.log((span + 1).astype(F32))
    sigma = jax.nn.sigmoid(pooled)
    dpool[...] = moved * (sigma + pooled * sigma * (1 - sigma))

    def step(rows, s, carry):
        windows = windows_at(e_ref, limit, s)
        pre[:rows, :] = nn(conv_ref[:rows, :], windows)
        for sub in range(0, rows, SUB):
            part = slice(sub, sub + SUB)
            low, scale = lse_ref[part, :], dpool[part, :]
            for i in range(STEP_P):
                cols = slice(i * tile, (i + 1) * tile)
                d_pre[part, cols] = (jnp.exp(pre[part, cols] - low) * scale).astype(BF16)
        back = nn(back_ref[:, :rows], d_pre[:rows, :])
        for i in range(STEP_P):
            at = pl.ds(pl.multiple_of((s * STEP_P + i) * CHAR_DIM, CHAR_DIM), TAPS)
            de_ref[at, :] += back[:TAPS, i * tile : (i + 1) * tile]
        sums_ref[:rows, :] += nt(d_pre[:rows, :], windows)
        return carry

    in_halves(step, channels, longest, narrow_ref)
    letter = lax.broadcasted_iota(jnp.int32, (found.shape[0], tile), 0)

    def spread(s, carry):
        parts = []
        for i in range(STEP_P):
            p = s * STEP_P + i
            at = pl.ds(pl.multiple_of(p * CHAR_DIM, CHAR_DIM), CHAR_DIM)
            value = jnp.where(p < lens, de_ref[at, :], 0.0)
            high = value.astype(BF16)
            parts.append(jnp.concatenate([high, (value - high.astype(F32)).astype(BF16)], axis=0))
            row = ids_ref[pl.ds(p, 1), :].astype(jnp.int32)
            found[:, i * tile : (i + 1) * tile] = jnp.where(letter == row, 1.0, 0.0).astype(BF16)
        table_grad_ref[: found.shape[0], :] += nt(found[...], jnp.concatenate(parts, axis=1))
        return carry

    lax.fori_loop(0, (longest + STEP_P - 1) // STEP_P, spread, 0)

    @pl.when(pl.program_id(0) == pl.num_programs(0) - 1)
    def _():
        both = table_grad_ref[...].T
        total = both[:CHAR_DIM] + both[CHAR_DIM:]
        for piece in range(lanes // LANES):
            at = channels + piece * CHAR_DIM
            sums_ref[at : at + CHAR_DIM, :] += total[:, piece * LANES : (piece + 1) * LANES]


def conv_backward(ranks, ids, embedded, vocab, conv_t, conv_back, widths, narrow, lse, grads, cblock, base, tile, so_far):
    channels, words = conv_t.shape[0], ids.shape[1]
    full = lambda *shape: pl.BlockSpec(shape, lambda i: (0,) * len(shape))
    return pl.pallas_call(
        functools.partial(conv_backward_kernel, cblock, len(ranks), base),
        grid=(words // tile,),
        in_specs=[
            pl.BlockSpec(memory_space=pltpu.SMEM),
            pl.BlockSpec((ID_ROWS, tile), lambda i: (0, i)),
            pl.BlockSpec((SLOTS_E * CHAR_DIM, tile), lambda i: (0, i)),
            full(*conv_t.shape),
            full(*conv_back.shape),
            full(channels, 1),
            pl.BlockSpec((channels, tile), lambda i: (0, i)),
        ]
        + [full(*part.shape) for part in ranks]
        + [full(*part.shape) for part in grads]
        + [full(*so_far.shape)],
        out_specs=full(*so_far.shape),
        out_shape=jax.ShapeDtypeStruct(so_far.shape, F32),
        scratch_shapes=[
            pltpu.VMEM((-(-vocab // LANES) * LANES, 2 * CHAR_DIM), F32),
            pltpu.VMEM((SLOTS_E * CHAR_DIM, tile), F32),
            pltpu.VMEM((cblock, tile), F32),
            pltpu.VMEM((cblock, STEP_P * tile), F32),
            pltpu.VMEM((cblock, STEP_P * tile), BF16),
            pltpu.VMEM((-(-vocab // 16) * 16, STEP_P * tile), BF16),
        ],
        compiler_params=pltpu.CompilerParams(vmem_limit_bytes=48 * MIB),
        cost_estimate=lasting(15),
        name="conv_backward",
    )(narrow, ids, pltpu.with_memory_space_constraint(embedded, pltpu.HBM), conv_t, conv_back, widths, lse, *ranks, *grads, so_far)


def word_order(lengths):
    count = lengths.shape[0]
    key = lengths * count - jnp.arange(count, dtype=jnp.int32)
    return jnp.sum((key[None, :] > key[:, None]).astype(jnp.int32), axis=1, keepdims=True)


def conv_operands(char_ids, lengths, char_table, conv_weight, conv_bias, widths, cblock):
    words = char_ids.shape[0]
    channels = conv_weight.shape[1]
    vocab = char_table.shape[0]
    lanes = -(-vocab // LANES) * LANES
    rank = word_order(lengths)
    data = jnp.concatenate([char_ids.T - ID_SHIFT, lengths[None, :]], axis=0)
    data = jnp.pad(data, ((0, ID_ROWS - MAX_CHARS - 1), (0, 0))).astype(BF16)
    offsets = jnp.arange(TAPS, dtype=jnp.int32) // CHAR_DIM
    taps = jnp.where(offsets[:, None] < widths[None, :], conv_weight, 0.0).astype(BF16)
    parts, rest = [], conv_bias
    for _ in range(3):
        part = lax.reduce_precision(rest, 8, 7)
        parts.append(part)
        rest = rest - part
    kinds = jnp.arange(1, MAX_WIDTH + 1, dtype=jnp.int32)
    spans = jnp.where(kinds[:, None] == widths[None, :], -1e30, 0.0)
    under = jnp.concatenate([jnp.stack(parts), spans, jnp.zeros((DEPTH - TAPS - 3 - MAX_WIDTH, channels), F32)])
    conv_all = jnp.concatenate([taps, under.astype(BF16)])
    conv_back = jnp.pad(taps, ((0, DEPTH - TAPS), (0, 0)))
    table_t = jnp.pad(lax.reduce_precision(char_table, 8, 7).T, ((0, 0), (0, lanes - vocab)))
    narrow = widths[:: channels // 2]
    return rank, data, table_t, conv_all.T, conv_back, widths[:, None], narrow


def channel_widths(start, count, whole):
    channel = start + jnp.arange(count, dtype=jnp.int32)
    widths = jnp.ones((count,), jnp.int32)
    for power in range(6):
        widths = widths + (channel >= whole * 2**power // 64).astype(jnp.int32)
    return widths


def load_pieces(table_ref, pieces, rows, dest, sems, half=None, proj=None):
    cols = pieces[0].shape[3]
    depth = dest.shape[1]

    def each(act):
        at = 0
        for ref in pieces:
            for j in range(ref.shape[0]):
                row, col = table_ref[0, at], table_ref[1, at]
                row = row if half is None else row - half * depth
                sem = sems.at[at]

                def go(ref=ref, j=j, row=row, col=col, sem=sem):
                    place = (slice(None), pl.ds(pl.multiple_of(row, rows), rows), pl.ds(pl.multiple_of(col, cols), cols))
                    act(pltpu.make_async_copy(ref.at[j, :, :rows, :], dest.at[place], sem))

                if half is None:
                    go()
                else:
                    pl.when((row >= 0) & (row < depth))(go)
                if proj is not None:
                    under = ref.shape[2] - rows
                    part = proj[0].shape[1] // 2
                    to = pl.ds(pl.multiple_of(table_ref[2, at], under), under)
                    for side in range(2):
                        source = ref.at[j, side, rows:, :part]
                        act(pltpu.make_async_copy(source, proj[0].at[to, side * part : (side + 1) * part], proj[1].at[2 * at + side]))
                at += 1

    each(lambda copy: copy.start())
    each(lambda copy: copy.wait())


def hidden_of(xs, weight, unit, cols, bias_ref):
    at, total = 0, None
    for x in xs:
        term = nn(x[...], weight[unit, at : at + x.shape[1], cols])
        total = term if total is None else total + term
        at += x.shape[1]
    return total + bias_ref[unit : unit + 1, cols]


def sigmoid(value):
    return 0.5 * jnp.tanh(0.5 * value) + 0.5


def factors(x, a, g):
    s = sigmoid(a)
    gate = sigmoid(g)
    nonlinear = a * s
    left = 1 - gate
    gap = x - nonlinear
    return nonlinear + gate * gap, left * (s + nonlinear * (1 - s)), gap * gate * left, gate


def forward_kernel(n_own, n_pieces, rows, width, table_ref, bias_ref, *refs):
    own, refs = refs[:n_own], refs[n_own:]
    mate, refs = refs[:n_own], refs[n_own:]
    pieces, refs = refs[:n_pieces], refs[n_pieces:]
    next_ref, low_ref, first_ref, second_ref, gate_ref, weight, sems = refs

    @pl.when(pl.program_id(0) == 0)
    def _():
        load_pieces(table_ref, pieces, rows, weight, sems)

    for j, x in enumerate(own):
        cols = slice(j * width, (j + 1) * width)
        a = hidden_of(own + mate, weight, 0, cols, bias_ref)
        g = hidden_of(own + mate, weight, 1, cols, bias_ref)
        value, first, second, gate = factors(x[...].astype(F32), a, g)
        next_ref[:, cols] = value
        low_ref[:, cols] = value.astype(BF16)
        first_ref[:, cols] = first.astype(BF16)
        second_ref[:, cols] = second.astype(BF16)
        gate_ref[:, cols] = gate.astype(BF16)


def column_sums(sums_ref, cols, d_first, d_gate):
    sums_ref[0:1, cols] += jnp.sum(d_first.astype(F32), axis=0, keepdims=True)
    sums_ref[1:2, cols] += jnp.sum(d_gate.astype(F32), axis=0, keepdims=True)


def product_back(out_ref, d_first, d_gate, weight, base, up=None):
    width = min(512, out_ref.shape[1])
    for j in range(out_ref.shape[1] // width):
        cols = slice(j * width, (j + 1) * width)
        rows = slice(base + j * width, base + (j + 1) * width)
        value = nt(d_first[...], weight[0, rows, :]) + nt(d_gate[...], weight[1, rows, :])
        if up is not None:
            value = value + up[:, cols]
        out_ref[:, cols] = value.astype(out_ref.dtype)


def turn_kernel(n_pieces, rows, width, packed, table_ref, bias_ref, own, mate, exact, out_grad, *refs):
    if packed:
        pieces, refs = refs[:n_pieces], refs[n_pieces:]
        low_ref, d_first_ref, d_gate_ref, up_ref, leaving_ref, vectors_ref, sums_ref, weight, sems, proj, proj_sems = refs
        proj_rows = (proj, proj_sems)
    else:
        proj, pieces, refs = refs[0], refs[1 : n_pieces + 1], refs[n_pieces + 1 :]
        low_ref, d_first_ref, d_gate_ref, up_ref, leaving_ref, vectors_ref, sums_ref, weight, sems = refs
        proj_rows = None

    @pl.when(pl.program_id(0) == 0)
    def _():
        load_pieces(table_ref, pieces, rows, weight, sems, None, proj_rows)
        sums_ref[...] = jnp.zeros_like(sums_ref)

    half = own.shape[1]
    for j in range(half // width):
        cols = slice(j * width, (j + 1) * width)
        a = hidden_of((own, mate), weight, 0, cols, bias_ref)
        g = hidden_of((own, mate), weight, 1, cols, bias_ref)
        dy = nt(out_grad[...], proj[cols, :])
        value, first, second, gate = factors(exact[:, cols], a, g)
        low_ref[:, cols] = value.astype(BF16)
        d_first, d_gate = (dy * first).astype(BF16), (dy * second).astype(BF16)
        d_first_ref[:, cols] = d_first
        d_gate_ref[:, cols] = d_gate
        up_ref[:, cols] = dy * gate
        column_sums(sums_ref, cols, d_first, d_gate)
    product_back(leaving_ref, d_first_ref, d_gate_ref, weight, half)
    vectors_ref[...] = nn(low_ref[...], proj[...])


def slope_kernel(n_pieces, rows, width, table_ref, partial, arrived, first_ref, second_ref, gate_ref, *refs):
    pieces, refs = refs[:n_pieces], refs[n_pieces:]
    d_first_ref, d_gate_ref, up_ref, leaving_ref, sums_ref, weight, sems = refs

    @pl.when(pl.program_id(0) == 0)
    def _():
        load_pieces(table_ref, pieces, rows, weight, sems, 1)
        sums_ref[...] = jnp.zeros_like(sums_ref)

    for j in range(partial.shape[1] // width):
        cols = slice(j * width, (j + 1) * width)
        dy = partial[:, cols] + arrived[:, cols].astype(F32)
        d_first, d_gate = (dy * first_ref[:, cols].astype(F32)).astype(BF16), (dy * second_ref[:, cols].astype(F32)).astype(BF16)
        d_first_ref[:, cols] = d_first
        d_gate_ref[:, cols] = d_gate
        up_ref[:, cols] = dy * gate_ref[:, cols].astype(F32)
        column_sums(sums_ref, cols, d_first, d_gate)
    product_back(leaving_ref, d_first_ref, d_gate_ref, weight, 0)


def back_kernel(n_pieces, rows, table_ref, d_first, d_gate, up, *refs):
    pieces, refs = refs[:n_pieces], refs[n_pieces:]
    out_ref, weight, sems = refs

    @pl.when(pl.program_id(0) == 0)
    def _():
        load_pieces(table_ref, pieces, rows, weight, sems, 0)

    product_back(out_ref, d_first, d_gate, weight, 0, up)


def weight_grad_kernel(n_chunks, n_cols, n_d, width, table_ref, *refs):
    xs, refs = refs[: n_chunks * n_cols], refs[n_chunks * n_cols :]
    d_first, d_gate, refs = refs[:n_d], refs[n_d : 2 * n_d], refs[2 * n_d :]
    outs, turned = refs[:-1], refs[-1]
    rows = outs[0].shape[2]

    @pl.when(pl.program_id(0) == 0)
    def _():
        word = 0
        for chunk in range(n_chunks):
            at = 0
            for x in xs[chunk * n_cols : (chunk + 1) * n_cols]:
                turned[at : at + x.shape[1], word : word + x.shape[0]] = x[...].T
                at += x.shape[1]
            word += x.shape[0]

    blocks = d_first[0].shape[1] // width
    for side in range(2):
        row = table_ref[side, pl.program_id(0)]
        left = turned[pl.ds(pl.multiple_of(row, rows), rows), :]
        for j in range(blocks):
            cols = slice(j * width, (j + 1) * width)
            out = outs[blocks].at[j] if side else outs[j]
            for unit, ds in enumerate((d_first, d_gate)):
                total, word = 0.0, 0
                for d in ds:
                    total = total + nn(left[:, word : word + d.shape[0]], d[:, cols])
                    word += d.shape[0]
                out[0, unit] = total.astype(BF16)


SMEM_SPEC = pl.BlockSpec(memory_space=pltpu.SMEM)
HBM_SPEC = pl.BlockSpec(memory_space=pltpu.HBM)


def whole(array):
    return pl.BlockSpec(array.shape, lambda i: (0,) * array.ndim)


def by_rows(rows, width, base=0):
    return pl.BlockSpec((rows, width), lambda i: (base + i, 0))


def params(**kw):
    return pltpu.CompilerParams(vmem_limit_bytes=58 * MIB, **kw)


def count_of(pieces):
    return sum(piece.shape[0] for piece in pieces)


def highway_forward(table, pieces, block_rows, bias, own, mate, chunk, words):
    width = own[0].shape[1]
    half = width * len(own)
    rows = min(ROWS, words)
    steps = words // rows
    tile = by_rows(rows, width, chunk * steps)
    out = by_rows(rows, half)
    return pl.pallas_call(
        functools.partial(forward_kernel, len(own), len(pieces), block_rows, width),
        grid=(steps,),
        in_specs=[SMEM_SPEC, whole(bias)] + [tile] * (2 * len(own)) + [HBM_SPEC] * len(pieces),
        out_specs=[out] * 5,
        out_shape=[jax.ShapeDtypeStruct((words, half), kind) for kind in (F32, BF16, BF16, BF16, BF16)],
        scratch_shapes=[pltpu.VMEM((2, 2 * half, half), BF16), pltpu.SemaphoreType.DMA((count_of(pieces),))],
        compiler_params=params(),
        cost_estimate=lasting(10),
        name="highway_forward",
    )(table, bias, *own, *mate, *pieces)


def highway_turn(table, pieces, block_rows, bias, own, mate, exact, out_grad, proj, width):
    words, half = own.shape
    out_width = out_grad.shape[1]
    rows = min(ROWS, words)
    tile = by_rows(rows, half)
    packed = proj is None
    scratch = [pltpu.VMEM((2, 2 * half, half), BF16), pltpu.SemaphoreType.DMA((count_of(pieces),))]
    if packed:
        scratch += [pltpu.VMEM((half, out_width), BF16), pltpu.SemaphoreType.DMA((2 * count_of(pieces),))]
    return pl.pallas_call(
        functools.partial(turn_kernel, len(pieces), block_rows, width, packed),
        grid=(words // rows,),
        in_specs=[SMEM_SPEC, whole(bias), tile, tile, tile, by_rows(rows, out_width)]
        + ([] if packed else [whole(proj)])
        + [HBM_SPEC] * len(pieces),
        out_specs=[tile] * 5 + [by_rows(rows, out_width), pl.BlockSpec((2, half), lambda i: (0, 0))],
        out_shape=[jax.ShapeDtypeStruct((words, half), kind) for kind in (BF16, BF16, BF16, F32, BF16)]
        + [jax.ShapeDtypeStruct((words, out_width), F32), jax.ShapeDtypeStruct((2, half), F32)],
        scratch_shapes=scratch,
        compiler_params=params(),
        cost_estimate=lasting(16),
        name="highway_turn",
    )(table, bias, own, mate, exact, out_grad, *([] if packed else [proj]), *pieces)


def highway_slopes(table, pieces, block_rows, partial, arrived, first, second, gate, width):
    words, half = partial.shape
    rows = min(ROWS, words)
    tile = by_rows(rows, half)
    return pl.pallas_call(
        functools.partial(slope_kernel, len(pieces), block_rows, width),
        grid=(words // rows,),
        in_specs=[SMEM_SPEC] + [tile] * 5 + [HBM_SPEC] * len(pieces),
        out_specs=[tile, tile, tile, tile, pl.BlockSpec((2, half), lambda i: (0, 0))],
        out_shape=[jax.ShapeDtypeStruct((words, half), kind) for kind in (BF16, BF16, F32, BF16)] + [jax.ShapeDtypeStruct((2, half), F32)],
        scratch_shapes=[pltpu.VMEM((2, half, half), BF16), pltpu.SemaphoreType.DMA((count_of(pieces),))],
        compiler_params=params(),
        cost_estimate=lasting(8),
        name="highway_slopes",
    )(table, partial, arrived, first, second, gate, *pieces)


def highway_back(table, pieces, block_rows, d_first, d_gate, up):
    words, width = d_first.shape
    rows = min(ROWS, words)
    tile = by_rows(rows, width)
    return pl.pallas_call(
        functools.partial(back_kernel, len(pieces), block_rows),
        grid=(words // rows,),
        in_specs=[SMEM_SPEC, tile, tile, tile] + [HBM_SPEC] * len(pieces),
        out_specs=tile,
        out_shape=jax.ShapeDtypeStruct((words, width), F32),
        scratch_shapes=[pltpu.VMEM((2, width, width), BF16), pltpu.SemaphoreType.DMA((count_of(pieces),))],
        compiler_params=params(),
        cost_estimate=lasting(6),
        name="highway_back",
    )(table, d_first, d_gate, up, *pieces)


def highway_weight_grad(table, xs, d_first, d_gate, rows, width):
    half = d_first[0].shape[1]
    words = sum(d.shape[0] for d in d_first)
    flat = [x for row in xs for x in row]
    steps = table.shape[1]
    blocks = half // width
    block = pl.BlockSpec((1, 2, rows, width), lambda i: (i, 0, 0, 0))
    return pl.pallas_call(
        functools.partial(weight_grad_kernel, len(xs), len(xs[0]), len(d_first), width),
        grid=(steps,),
        in_specs=[SMEM_SPEC] + [whole(x) for x in flat] + [whole(d) for d in d_first + d_gate],
        out_specs=[block] * blocks + [pl.BlockSpec((blocks, 1, 2, rows, width), lambda i: (0, i, 0, 0, 0))],
        out_shape=[jax.ShapeDtypeStruct((steps, 2, rows, width), BF16)] * blocks
        + [jax.ShapeDtypeStruct((blocks, steps, 2, rows, width), BF16)],
        scratch_shapes=[pltpu.VMEM((2 * half, words), BF16)],
        compiler_params=params(),
        cost_estimate=lasting(15),
        name="highway_weight_grad",
    )(table, *flat, *d_first, *d_gate)


def adam_update(weight, grad, moment_one, moment_two, rate):
    first_new = beta_one * moment_one + (1 - beta_one) * grad
    second_new = beta_two * moment_two + (1 - beta_two) * grad * grad
    corrected_one = first_new / (1 - beta_one**STEP)
    corrected_two = second_new / (1 - beta_two**STEP)
    updated = weight - rate * (
        corrected_one / (jnp.sqrt(corrected_two) + adam_eps) + decay_rate * weight
    )
    return (second_new, updated)


def owner_kernel(n_grads, at_ref, *refs):
    grads, refs = refs[:n_grads], refs[n_grads:]
    weight, one, two, average = refs[:4]
    grad, second, new, average_new = refs[-4:]
    width = grads[0].shape[1]
    for j, ref in enumerate(grads):
        at = pl.ds(pl.multiple_of(at_ref[j], LANES), width)
        grad[0, :, at] = ref[...].astype(F32)
    second_new, updated = adam_update(weight[...], grad[...], one[...], two[...], 0.02)
    second[...] = second_new
    new[...] = updated
    average_new[...] = average_keep * average[...] + (1 - average_keep) * updated


def owner_update(slot, at, grads, weight, one, two, average, so_far=()):
    rows, width = grads[0].shape
    part = min(64, rows)
    block = pl.BlockSpec((1, part, weight.shape[2]), lambda i: (slot, i, 0))
    given = len(grads) + 5
    return pl.pallas_call(
        functools.partial(owner_kernel, len(grads)),
        grid=(rows // part,),
        in_specs=[SMEM_SPEC]
        + [pl.BlockSpec((part, width), lambda i: (i, 0))] * len(grads)
        + [block] * 4
        + [HBM_SPEC] * len(so_far),
        out_specs=[block] * 4,
        out_shape=[jax.ShapeDtypeStruct(weight.shape, F32)] * 4,
        input_output_aliases={given + n: n for n in range(len(so_far))},
        compiler_params=params(),
        cost_estimate=lasting(8),
        name="owner_update",
    )(at, *grads, weight, one, two, average, *so_far)


def slot_of(owner_ref, unit):
    return sum(jnp.where(owner_ref[before] == owner_ref[unit], 1, 0) for before in range(unit)) if unit else 0


def choose_kernel(n_from, owner_ref, proj, *refs):
    arrived, outs = refs[:n_from], refs[n_from:]
    rows, width = arrived[0].shape[1:]
    here = lax.axis_index("filt")
    for unit in range(UNITS):
        for step, ref in enumerate(arrived):

            @pl.when(owner_ref[unit] ^ here == step)
            def _(ref=ref, unit=unit):
                outs[unit // 2][unit % 2, :rows, :] = ref[slot_of(owner_ref, unit)]

    under, part = proj.shape[0], proj.shape[1] // 2
    if outs[1].shape[1] > rows:
        outs[1][:, rows:, :] = jnp.zeros((2, under, width), BF16)
        for side in range(2):
            outs[1][side, rows:, :part] = proj[:, side * part : (side + 1) * part].astype(BF16)


def choose_units(owners, arrived, proj, packed):
    slots, rows, width = arrived[0].shape
    shapes = [(2, rows, width), (2, rows + (proj.shape[0] if packed else 0), width)]
    return pl.pallas_call(
        functools.partial(choose_kernel, len(arrived)),
        grid=(1,),
        in_specs=[SMEM_SPEC, whole(proj)] + [whole(part) for part in arrived],
        out_specs=[pl.BlockSpec(shape, lambda i: (0, 0, 0)) for shape in shapes],
        out_shape=[jax.ShapeDtypeStruct(shape, BF16) for shape in shapes],
        compiler_params=params(),
        cost_estimate=lasting(3),
        name="choose_units",
    )(owners, proj, *arrived)


def return_kernel(counts, owner_ref, *refs):
    layers = (refs[: counts[0]], refs[counts[0] : counts[0] + counts[1]])
    here = lax.axis_index("filt")
    outs = refs[counts[0] + counts[1] :]
    for step in range(len(outs) // SLOTS):
        for slot in range(SLOTS):
            out = outs[SLOTS * step + slot]
            taken = -1
            for unit in range(UNITS):
                fits = (owner_ref[unit] ^ here == step) & (slot_of(owner_ref, unit) == slot)
                taken = jnp.where(fits, unit, taken)
            for unit in range(UNITS):

                @pl.when(taken == unit)
                def _(unit=unit, out=out):
                    out[...] = sum(ref[unit % 2].astype(F32) for ref in layers[unit // 2]).astype(BF16)

            @pl.when(taken < 0)
            def _(out=out):
                out[...] = jnp.zeros(out.shape, BF16)


def return_units(owners, layers, count):
    shape = layers[0][0].shape
    part = min(128, shape[1])
    block = pl.BlockSpec((2, part, shape[2]), lambda i: (0, i, 0))
    terms = list(layers[0]) + list(layers[1])
    return pl.pallas_call(
        functools.partial(return_kernel, [len(layer) for layer in layers]),
        grid=(shape[1] // part,),
        in_specs=[SMEM_SPEC] + [block] * len(terms),
        out_specs=[pl.BlockSpec((part, shape[2]), lambda i: (i, 0))] * (SLOTS * count),
        out_shape=[jax.ShapeDtypeStruct(shape[1:], BF16)] * (SLOTS * count),
        compiler_params=params(),
        cost_estimate=lasting(3),
        name="return_units",
    )(owners, *terms)


class Places:
    def __init__(self):
        self.n_filt, self.n_dp = lax.axis_size("filt"), lax.axis_size("dp")
        self.n_y, self.n_z = self.n_filt // 2, self.n_dp // 2
        self.f, self.d = lax.axis_index("filt"), lax.axis_index("dp")
        self.y, self.x = self.f // 2, self.f % 2
        self.z, self.c = self.d // 2, self.d % 2
        self.direct = self.n_y == 2 and self.n_z == 4

    def over_filt(self, value, step):
        return lax.ppermute(value, "filt", [(i, i ^ step) for i in range(self.n_filt)])

    def over_x(self, value):
        return self.over_filt(value, 1)

    def over_y(self, value, step):
        return self.over_filt(value, 2 * step)

    def over_core(self, value):
        return lax.ppermute(value, "dp", [(i, i ^ 1) for i in range(self.n_dp)])

    def over_z(self, value, step):
        pairs = [(i, (i // 2 + step) % self.n_z * 2 + i % 2) for i in range(self.n_dp)]
        return lax.ppermute(value, "dp", pairs)

    def far_first(self):
        return sorted(range(1, self.n_z), key=lambda k: (min(k, self.n_z - k), k))

    def row_of(self, d, rows, width):
        f = d * rows // width
        half = self.n_y * width
        return (f % 2 ^ self.x) * half + (f // 2 ^ self.y) * width + d * rows % width


def after(value, *earlier):
    return lax.optimization_barrier((value, earlier))[0]


def settle(*values):
    return lax.optimization_barrier(values)


def gather_general(place, blocks):
    rows, width = blocks[0].shape[1:]
    out = []
    for piece in blocks:
        spread = lax.all_gather(lax.all_gather(piece, "dp"), "filt")
        spread = spread.reshape((place.n_y, 2) + spread.shape[1:])
        spread = lax.dynamic_index_in_dim(spread, place.x, 1, keepdims=False)
        spread = spread.reshape((place.n_y * place.n_dp,) + piece.shape)
        d = jnp.tile(jnp.arange(place.n_dp, dtype=jnp.int32), place.n_y)
        y = jnp.repeat(jnp.arange(place.n_y, dtype=jnp.int32), place.n_dp)
        table = jnp.stack([place.row_of(d, rows, width), (y ^ place.y) * width]).astype(jnp.int32)
        out.append((table, [spread]))
    return out


BLOCK_STEPS = (
    [(0, 0), (0, 1), (1, 0), (3, 0), (2, 0), (1, 1), (3, 1), (2, 1)],
    [(0, 0), (0, 1), (1, 0), (3, 0), (1, 1), (3, 1), (2, 0), (2, 1)],
)


def gather_table(place, layer, rows, width, rows_proj):
    at_rows, at_cols, at_proj = [], [], []
    for other in range(2):
        for k, step in BLOCK_STEPS[layer]:
            d = (place.z - k) % place.n_z * 2 + (place.c ^ other)
            at_rows.append(place.row_of(d, rows, width))
            at_cols.append(jnp.int32(step * width))
            at_proj.append(step * width + d * rows_proj)
    return jnp.stack([jnp.stack(at_rows), jnp.stack(at_cols), jnp.stack(at_proj)]).astype(jnp.int32)


def sum_table(place, rows, width):
    z = jnp.arange(place.n_z, dtype=jnp.int32)
    z, c = ((place.z + z) % place.n_z, place.c) if place.direct else (z, 0)
    return jnp.stack([place.row_of(z * 2 + c, rows, width), place.row_of(z * 2 + (1 - c), rows, width)]).astype(jnp.int32)


def sent_over_y(parts, group):
    near, arrived = parts
    return (near[1][group].astype(F32) + arrived[1][group].astype(F32)).astype(BF16)


def kept_over_y(parts, turned, group):
    near, arrived = parts
    steps = range(group.start, group.stop)
    return [near[0][k].astype(F32) + arrived[0][k].astype(F32) + turned[n].astype(F32) for n, k in enumerate(steps)]


def sum_general(place, blocks):
    n_y = place.n_y
    near, far = blocks[:n_y], list(blocks[n_y])
    steps = jnp.arange(n_y, dtype=jnp.int32) ^ place.y
    pairs = jnp.stack([jnp.stack(near), jnp.stack(far)], axis=2)
    pairs = jnp.take(pairs, steps, axis=0)
    pairs = pairs.reshape((n_y, place.n_dp) + pairs.shape[3:])
    mine = lax.psum_scatter(pairs, "dp", scatter_dimension=1)
    sides = jnp.arange(2, dtype=jnp.int32).reshape(1, 2, 1, 1, 1)
    mine = jnp.where(sides == place.x, mine[:, None], jnp.zeros((), BF16))
    mine = mine.reshape((place.n_filt,) + mine.shape[2:])
    return lax.psum_scatter(mine, "filt", scatter_dimension=0).astype(F32)


def pick(array, at, axis=0):
    return lax.dynamic_index_in_dim(array, at, axis, keepdims=False)


def rows_over_core(place, value):
    parts = value.reshape((place.n_z, 2, -1) + value.shape[1:])
    return pick(parts, place.c, 1), over_core_low(place, pick(parts, 1 - place.c, 1))


def over_core_low(place, value):
    return place.over_core(value.astype(BF16))


def swap_z(place, value, step):
    pairs = [(i, i ^ (2 * step)) for i in range(place.n_dp)]
    return lax.ppermute(value, "dp", pairs)


def swap_rows(place, parts, step):
    upper = place.z // step % 2
    halves = parts.reshape((2, -1) + parts.shape[1:])
    return pick(halves, upper), swap_z(place, pick(halves, 1 - upper).astype(BF16), step)


def sum_filt(place, value):
    if not place.direct:
        return lax.psum(value, "filt")
    step = 1
    while step < place.n_filt:
        value = value + place.over_filt(value, step)
        step *= 2
    return value


def per_device(
    char_ids,
    word_lengths,
    out_grad,
    highway_owner,
    char_table,
    conv_weight,
    conv_bias,
    highway_weight,
    proj_weight,
    dense_bias,
    table_moment_one,
    table_moment_two,
    conv_moment_one,
    conv_moment_two,
    conv_bias_moment_one,
    conv_bias_moment_two,
    highway_moment_one,
    highway_moment_two,
    highway_average,
    proj_moment_one,
    proj_moment_two,
    bias_moment_one,
    bias_moment_two,
):
    place = Places()
    n_y, n_filt, direct = place.n_y, place.n_filt, place.direct
    width = conv_weight.shape[1]
    rows, width_full = highway_weight.shape[1:]
    half = width_full // 2
    rows_proj, out_width = proj_weight.shape
    vocab_count = char_table.shape[0]
    words_dev = char_ids.shape[0]
    words_y = words_dev // n_y
    chunks, chunk_words = range(2), words_y // 2
    steps_y = list(range(1, n_y))
    mine_first = place.x == 0
    over_core, over_x, over_y, over_z = place.over_core, place.over_x, place.over_y, place.over_z

    widths = channel_widths(place.f * width, width, FILTERS)
    offsets = jnp.arange(TAPS, dtype=jnp.int32) // CHAR_DIM
    tap_mask = (offsets[:, None] < widths[None, :]).astype(jnp.float32)
    tile = min(256, words_dev)
    n_tiles = words_dev // tile
    cuts = [0, 1, 2, 4, 8] if n_tiles == 8 else [0, n_tiles]
    splits = list(zip(cuts[:-1], cuts[1:]))
    rank, data, table_t, conv_t, conv_back, width_col, narrow = conv_operands(
        char_ids, word_lengths, char_table, conv_weight, conv_bias, widths, width
    )
    rank_parts = [lax.dynamic_slice_in_dim(rank, (place.y ^ step) * words_y, words_y, axis=0) for step in range(n_y)]

    def convolve(some, narrow):
        return [conv_forward(rank, data, table_t, conv_t, width_col, narrow, width, begin, end - begin) for begin, end in some]

    def block_of(step):
        start = (place.f ^ step) * width
        return lax.dynamic_slice_in_dim(highway_weight, start, width, axis=2).astype(BF16)

    from_owner = [block_of(0)] + [place.over_filt(block_of(step), step) for step in range(1, n_filt)]
    kept = convolve(splits[: len(splits) // 2], narrow)
    from_owner, kept, narrow = settle(from_owner, kept, narrow)
    blocks = choose_units(highway_owner, from_owner, proj_weight, direct)
    bias_float = lax.reduce_precision(dense_bias, 8, 7)

    def half_bias(unit):
        starts = [unit * width_full + (2 * (place.y ^ step) + place.x) * width for step in range(n_y)]
        return jnp.concatenate([lax.dynamic_slice_in_dim(bias_float, start, width) for start in starts])

    layer_bias = [jnp.stack([half_bias(2 * layer), half_bias(2 * layer + 1)]) for layer in range(2)]

    blocks, narrow, sent, layer_bias = settle(blocks, narrow, out_grad, layer_bias)
    grad_mate = over_x(sent)
    if direct:
        first_y = [over_y(block, 1) for block in blocks]
        near = [over_z(blocks[0], k) for k in (1, 3)]
    kept = kept + convolve(splits[len(splits) // 2 :], narrow)
    placed = [place_words(part, [parts[0] for parts in kept]) for part in rank_parts]
    own = [placed[0]] + [over_y(placed[step], step) for step in steps_y]
    if direct:
        near, first_y, placed, grad_mate, blocks = settle(near, first_y, placed, grad_mate, blocks)
        own = [placed[0], over_y(placed[1], 1)]
        mate = [over_x(placed[0])]
        far = over_z(blocks[0], 2)
        sent = jnp.stack([near[0], near[1], jnp.zeros_like(near[0])])
        own, mate, far, sent, blocks, first_y, layer_bias, grad_mate = settle(
            own, mate, far, sent, blocks, first_y, layer_bias, grad_mate
        )

        out_grads = [jnp.where(mine_first, out_grad, grad_mate), jnp.where(mine_first, grad_mate, out_grad)]
        out_sum = jnp.sum(out_grad, axis=0, dtype=F32)
        sent = lax.dynamic_update_index_in_dim(sent, far, 2, 0)
        sent_y = over_y(sent, 1)
        mate = mate + [over_x(own[1])]
        near_one = [over_z(blocks[1], k) for k in (1, 3)]
        sent_core = over_core(sent)
        start = jnp.stack([blocks[0], first_y[0]])
        table = [gather_table(place, layer, rows, width, rows_proj) for layer in range(2)]
        sent_y, sent_core, start, mate, near_one, blocks, out_grads, table, out_sum = settle(
            sent_y, sent_core, start, mate, near_one, blocks, out_grads, table, out_sum
        )

        gathered = [(table[0], [start, sent, sent_y, over_core(start), sent_core, over_core(sent_y)], rows)]
        far_one = over_z(blocks[1], 2)
        near_y = over_y(jnp.stack(near_one), 1)
    else:
        mate = [over_x(part) for part in own]
        gathered = [(*found, rows) for found in gather_general(place, blocks)]
        out_sum = jnp.sum(out_grad, axis=0, dtype=F32)
        out_grads = [jnp.where(mine_first, out_grad, grad_mate), jnp.where(mine_first, grad_mate, out_grad)]

    forward, x_one_mate = [], []
    for chunk in chunks:
        forward.append(highway_forward(*gathered[0], layer_bias[0], own, mate, chunk, chunk_words))
        x_one_mate.append(over_x(forward[chunk][1]))
        if direct and chunk == 0:
            forward[0], near_one, layer_bias[0] = settle(forward[0], near_one, layer_bias[0])
            start = jnp.stack([blocks[1], first_y[1], near_one[0], near_one[1]])
            start_core = over_core(start)
    if direct:
        far_one, near_y, forward[1] = settle(far_one, near_y, forward[1])
        far_y = over_y(far_one, 1)
        far_y, x_one_mate[0] = settle(far_y, x_one_mate[0])
        last = jnp.stack([near_y[0], near_y[1], far_one, far_y])
        gathered.append((table[1], [start, last, start_core, over_core(last)], rows))
        proj_half = None
    else:
        proj_own = jnp.stack([proj_weight.astype(BF16)] + [over_y(proj_weight.astype(BF16), step) for step in steps_y])
        proj_half = lax.all_gather(proj_own, "dp", axis=1).reshape(half, out_width)
    x_one, x_one_low, first_zero, second_zero, gate_zero = zip(*forward)
    turned, arrived = [], []
    for chunk in chunks:
        bias_one = layer_bias[1] if chunk == 0 else settle(layer_bias[1], turned[0])[0]
        turned.append(
            highway_turn(*gathered[1], bias_one, x_one_low[chunk], x_one_mate[chunk], x_one[chunk], out_grads[chunk], proj_half, width)
        )
        arrived.append(over_x(turned[chunk][4]))
    x_two_low, d_first_one, d_gate_one, up_one, _, vectors, sums = (list(parts) for parts in zip(*turned))
    sums_one = sums[0] + sums[1]

    targets = sum_table(place, rows, width)
    blocks = highway_weight_grad(
        targets, [[x_one_low[chunk], x_one_mate[chunk]] for chunk in chunks], d_first_one, d_gate_one, rows, width
    )
    blocks, up_one[0], arrived[0] = settle(blocks, up_one[0], arrived[0])
    if not direct:
        sum_one = sum_general(place, blocks)

    partial, parts_zero, arrived_zero = [], [], []
    for chunk in chunks:
        partial.append(highway_back(*gathered[1], d_first_one[chunk], d_gate_one[chunk], up_one[chunk]))
        if chunk == 0 and direct:
            partial[0], arrived[1], blocks = settle(partial[0], arrived[1], blocks)
            one = (blocks[:2], over_core(blocks[2]))
        parts_zero.append(
            highway_slopes(*gathered[0], partial[chunk], arrived[chunk], first_zero[chunk], second_zero[chunk], gate_zero[chunk], width)
        )
        if chunk == 0 and direct:
            one, parts_zero[0], up_one[1] = settle(one, parts_zero[0], up_one[1])
            sent = sent_over_y(one, slice(0, place.n_z))
            sent, up_one[1] = settle(sent, up_one[1])
            one_y = over_y(sent, 1)
        arrived_zero.append(over_x(parts_zero[chunk][3]))
    d_first, d_gate, up, _, sums = (list(parts) for parts in zip(*parts_zero))
    sums_zero = sums[0] + sums[1]
    blocks = highway_weight_grad(targets, [own + mate], d_first, d_gate, rows, width)
    blocks, up, arrived_zero[0] = settle(blocks, up, arrived_zero[0])
    groups = [slice(2, 4), slice(0, 2)]
    if not direct:
        sum_zero = sum_general(place, blocks)
    partial = [highway_back(*gathered[0], d_first[chunk], d_gate[chunk], up[chunk]) for chunk in chunks]
    if direct:
        partial, blocks, arrived_zero[1], one_y = settle(partial, blocks, arrived_zero[1], one_y)
        zero = (blocks[:2], over_core(blocks[2]))
    if direct:
        one_here = kept_over_y(one, one_y, slice(0, place.n_z))
        one_sent = [one_here[k].astype(BF16) for k in (2, 1, 3)]
        one_here = one_here[0]
        one_sent, one_here, partial = settle(one_sent, one_here, partial)
        one_z = [over_z(value, k) for value, k in zip(one_sent, (2, 1, 3))]
    groups = [slice(2, 4), slice(0, 2)]
    if not direct:
        sum_zero = sum_general(place, blocks)
    partial = [highway_back(*gathered[0], d_first[chunk], d_gate[chunk], up[chunk]) for chunk in chunks]
    if direct:
        partial, blocks, arrived_zero[1], one_y = settle(partial, blocks, arrived_zero[1], one_y)
        zero = (blocks[:2], over_core(blocks[2]))
    feature_grad = []
    for step in range(n_y):
        cols = slice(step * width, (step + 1) * width)
        feature_grad.append(
            jnp.concatenate(
                [(partial[chunk][:, cols] + arrived_zero[chunk][:, cols].astype(F32)).astype(BF16) for chunk in chunks]
            )
        )
    groups = [slice(2, 4), slice(0, 2)]
    returned = [over_y(value, step) if step else value for step, value in enumerate(feature_grad)]
    if direct:
        returned[0], x_two_low, vectors = settle(returned[0], x_two_low, vectors)
        zero_y = [over_y(sent_over_y(zero, groups[0]), 1)]
    proj_part = (tn(x_two_low[0], out_grads[0]) + tn(x_two_low[1], out_grads[1])).reshape(n_y, width, out_width)
    proj_here, proj_away = proj_part[0], [proj_part[step].astype(BF16) for step in steps_y]
    vectors_away = jnp.where(mine_first, vectors[1], vectors[0]).astype(BF16)
    vectors_here = jnp.where(mine_first, vectors[0], vectors[1])
    ranks = [part.T for part in rank_parts]

    if direct:
        zero_sent = sent_over_y(zero, groups[1])
        returned, narrow, ranks, zero_sent = settle(returned, narrow, ranks, zero_sent)

    def convolve_back(n, narrow, so_far):
        (begin, _), (_, lse, sorted_ids, embedded) = splits[n], kept[n]
        return conv_backward(
            ranks, sorted_ids, embedded, vocab_count, conv_t, conv_back, width_col, narrow, lse, returned, width, begin, tile, so_far
        )

    home = jnp.arange(n_filt, dtype=jnp.int32)

    def natural(values):
        parts = values.reshape(n_y, 1, width)
        out = jnp.zeros((n_filt, width), F32)
        for step in range(n_y):
            out = jnp.where((home == 2 * (place.y ^ step) + place.x)[:, None], parts[step], out)
        return out.reshape(-1)

    bias_local = jnp.concatenate(
        [natural(sums[unit]) for sums in (sums_zero, sums_one) for unit in range(2)] + [out_sum]
    )
    table_rows = table_t.shape[1] // LANES * CHAR_DIM
    bias_rows = -(-bias_local.size // DEPTH)
    bias_rows += -(width + table_rows + bias_rows) % 16
    bias_flat = jnp.pad(bias_local, (0, bias_rows * DEPTH - bias_local.size)).reshape(bias_rows, DEPTH)
    small = jnp.concatenate([jnp.zeros((width + table_rows, DEPTH), F32), bias_flat])
    if direct:
        small, returned, narrow = settle(small, returned, narrow)
    back = small
    for n in range(len(splits)):
        back = convolve_back(n, narrow, back)
        if direct and n == 0:
            back, narrow, one_z, zero_y[0], zero, vectors_away, proj_away = settle(
                back, narrow, one_z, zero_y[0], zero, vectors_away, proj_away
            )
            zero_here = kept_over_y(zero, zero_y[0], groups[0])
            zero_z, zero_sent, narrow = settle([value.astype(BF16) for value in zero_here], zero_sent, narrow)
            zero_z = [over_z(value, k) for value, k in zip(zero_z, (2, 3))]
            zero_y.append(over_y(zero_sent, 1))
            vectors_arrived = over_x(vectors_away)
        if direct and n == 2:
            back, zero_z, narrow, zero_y, vectors_arrived, proj_away = settle(back, zero_z, narrow, zero_y, vectors_arrived, proj_away)
            zero_here, last = kept_over_y(zero, zero_y[1], groups[1])
            last, zero_here, narrow = settle(last.astype(BF16), zero_here, narrow)
            last = over_z(last, 1)
            proj_y = over_y(proj_away[0], 1)
    if direct:
        back, last, proj_y = settle(back, last, proj_y)
        slot_grads = return_units(highway_owner, [[zero_here] + zero_z + [last], [one_here] + one_z], n_filt)
    else:
        proj_y = [over_y(value, step) for value, step in zip(proj_away, steps_y)]
        proj_grad = lax.psum_scatter(proj_here + sum(value.astype(F32) for value in proj_y), "dp", scatter_dimension=0, tiled=True)
    if not direct:
        vectors_arrived = over_x(vectors_away)
    small = back
    if direct:
        small = small + over_core(small)
    else:
        small = lax.psum(small, "dp")
        small = jnp.concatenate([small[:width], sum_filt(place, small[width:])])

    optimizer = (highway_weight, highway_moment_one, highway_moment_two, highway_average)
    columns = (place.f ^ jnp.arange(n_filt, dtype=jnp.int32)) * width
    if direct:
        slot_grads, proj_y, vectors_arrived = settle(slot_grads, proj_y, vectors_arrived)
        proj_rows = rows_over_core(place, proj_here + proj_y.astype(F32))
        by_slot = [slot_grads[slot::SLOTS] for slot in range(SLOTS)]
        to_owner = lambda grads: [grads[0]] + [place.over_filt(grads[step], step) for step in range(1, n_filt)]
        by_slot[0] = to_owner(by_slot[0])
        small = small + swap_z(place, small.astype(BF16), 1).astype(F32)
        by_slot, small, proj_rows = settle(by_slot, small, proj_rows)
        by_slot[1] = to_owner(by_slot[1])
        small = small + swap_z(place, small.astype(BF16), 2).astype(F32)
        proj_rows = swap_rows(place, proj_rows[0] + proj_rows[1].astype(F32), 2)
        updates = owner_update(0, columns, by_slot[0], *optimizer)
        updates, small, proj_rows, by_slot[1] = settle(updates, small, proj_rows, by_slot[1])
        conv_sums, small = small[:width], small[width:]
        others = [place.over_filt(small, step) for step in range(1, n_filt)]
        proj_rows = swap_rows(place, proj_rows[0] + proj_rows[1].astype(F32), 1)
        updates = owner_update(1, columns, by_slot[1], *optimizer, updates)
        updates, others, proj_rows = settle(updates, others, proj_rows)
        small = (small + others[0]) + (others[1] + others[2])
        proj_grad = (proj_rows[0] + proj_rows[1].astype(F32)).reshape(rows_proj, out_width)
    else:
        slot_grads = return_units(highway_owner, [[sum_zero], [sum_one]], n_filt)
        conv_sums, small = small[:width], small[width:]
        updates = ()
        for slot in range(SLOTS):
            grads = slot_grads[slot::SLOTS]
            grads = [grads[0]] + [place.over_filt(grads[step], step) for step in range(1, n_filt)]
            updates = owner_update(slot, columns, grads, *optimizer, updates)
    highway_grad, highway_second, highway_new, highway_average_new = updates
    word_vectors = vectors_here + vectors_arrived.astype(F32) + bias_float[UNITS * width_full :]
    conv_grad, conv_bias_grad = conv_sums[:, :TAPS].T * tap_mask, conv_sums[:, TAPS]
    table_grad = small[:table_rows].reshape(-1, CHAR_DIM, LANES).transpose(0, 2, 1).reshape(-1, CHAR_DIM)[:vocab_count]
    bias_grad = small[table_rows:].reshape(-1)[: bias_local.size]
    table_second, table_new = adam_update(
        char_table, table_grad, table_moment_one, table_moment_two, 1.0
    )
    conv_second, conv_new = adam_update(
        conv_weight, conv_grad, conv_moment_one, conv_moment_two, 0.1
    )
    conv_bias_second, conv_bias_new = adam_update(
        conv_bias, conv_bias_grad, conv_bias_moment_one, conv_bias_moment_two, 0.3
    )
    proj_second, proj_new = adam_update(
        proj_weight, proj_grad, proj_moment_one, proj_moment_two, 0.02
    )
    bias_second, bias_new = adam_update(
        dense_bias, bias_grad, bias_moment_one, bias_moment_two, 0.3
    )
    return (
        word_vectors,
        table_grad,
        table_second,
        table_new,
        conv_grad,
        conv_second,
        conv_new,
        conv_bias_grad,
        conv_bias_second,
        conv_bias_new,
        highway_grad,
        highway_second,
        highway_new,
        highway_average_new,
        proj_grad,
        proj_second,
        proj_new,
        bias_grad,
        bias_second,
        bias_new,
    )


def solution(mesh):
    return jax.shard_map(
        per_device,
        mesh=mesh,
        in_specs=(
            P("dp", None),
            P("dp"),
            P(("dp", "filt"), None),
            P(),
            P(),
            P(None, "filt"),
            P("filt"),
            P("filt", "dp", None),
            P(("filt", "dp"), None),
            P(),
            P(),
            P(),
            P(None, "filt"),
            P(None, "filt"),
            P("filt"),
            P("filt"),
            P("filt", "dp", None),
            P("filt", "dp", None),
            P("filt", "dp", None),
            P(("filt", "dp"), None),
            P(("filt", "dp"), None),
            P(),
            P(),
        ),
        out_specs=(
            P(("dp", "filt"), None),
            P(),
            P(),
            P(),
            P(None, "filt"),
            P(None, "filt"),
            P(None, "filt"),
            P("filt"),
            P("filt"),
            P("filt"),
            P("filt", "dp", None),
            P("filt", "dp", None),
            P("filt", "dp", None),
            P("filt", "dp", None),
            P(("filt", "dp"), None),
            P(("filt", "dp"), None),
            P(("filt", "dp"), None),
            P(),
            P(),
            P(),
        ),
        check_vma=False,
    )
```

```python
import functools

import jax
import jax.numpy as jnp
from jax import lax
from jax.experimental import pallas as pl
from jax.experimental.pallas import tpu as pltpu
from jax.sharding import PartitionSpec as P

CHAR_DIM = 16
MAX_CHARS = 50
MAX_WIDTH = 7
FILTERS = 2048
UNITS = 4
SLOTS = 2
STEP = 10
TAPS = MAX_WIDTH * CHAR_DIM
DEPTH = 128
ID_SHIFT = 128
ID_ROWS = 64
SLOTS_E = MAX_CHARS + MAX_WIDTH - 1 + 8
LANES = 128
STEP_P = 4
ROWS = 256
beta_one = 0.9
beta_two = 0.999
adam_eps = 1e-08
decay_rate = 0.01
average_keep = 0.9
F32, BF16 = jnp.float32, jnp.bfloat16
MIB = 1 << 20


def lasting(us):
    return pl.CostEstimate(flops=int(us * 1e7), bytes_accessed=int(us * 3e4), transcendentals=0)


def nt(a, b):
    return lax.dot_general(a, b, (((1,), (1,)), ((), ())), preferred_element_type=F32)


def nn(a, b):
    return lax.dot_general(a, b, (((1,), (0,)), ((), ())), preferred_element_type=F32)


def tn(a, b):
    return lax.dot_general(a, b, (((0,), (0,)), ((), ())), preferred_element_type=F32)


def embed_tile(ids_ref, table_ref, lens, e_ref, longest):
    tile = lens.shape[1]
    e_ref[...] = jnp.zeros_like(e_ref)
    pieces = table_ref.shape[1] // LANES

    def fill(s, carry):
        for i in range(STEP_P):
            p = s * STEP_P + i
            row = ids_ref[pl.ds(p, 1), :].astype(jnp.int32)
            parts = []
            for lane in range(tile // LANES):
                idx = jnp.broadcast_to(row[:, lane * LANES : (lane + 1) * LANES], (CHAR_DIM, LANES))
                low = jnp.bitwise_and(idx, LANES - 1)
                value = jnp.zeros((CHAR_DIM, LANES), F32)
                for piece in range(pieces):
                    got = jnp.take_along_axis(table_ref[:, piece * LANES : (piece + 1) * LANES], low, axis=1)
                    value = jnp.where(lax.shift_right_logical(idx, 7) == piece, got, value)
                parts.append(value)
            value = jnp.concatenate(parts, axis=1) if len(parts) > 1 else parts[0]
            value = jnp.where(p < lens, value, 0.0)
            e_ref[pl.ds(pl.multiple_of(p * CHAR_DIM, CHAR_DIM), CHAR_DIM), :] = value.astype(BF16)
        return carry

    lax.fori_loop(0, (longest + STEP_P - 1) // STEP_P, fill, 0)


def limits_of(lens):
    row = lax.broadcasted_iota(jnp.int32, (CHAR_DIM, lens.shape[1]), 0)
    past = jnp.maximum(lens - (row - 2), 0)
    return jnp.where(row < 3, -1, jnp.where(row < 3 + MAX_WIDTH, past, 1 << 20))


def window_at(e_ref, limit, p):
    extra = jnp.where(p > limit, 1.0, 0.0).astype(BF16)
    taps = e_ref[pl.ds(pl.multiple_of(p * CHAR_DIM, CHAR_DIM), TAPS), :]
    return jnp.concatenate([taps, extra], axis=0)


SUB = 32


def windows_at(e_ref, limit, s):
    return jnp.concatenate([window_at(e_ref, limit, s * STEP_P + i) for i in range(STEP_P)], axis=1)


def in_halves(step, channels, longest, narrow_ref):
    both = steps_of(longest, narrow_ref[1])
    lax.fori_loop(0, both, functools.partial(step, channels), 0)
    lax.fori_loop(both, jnp.maximum(both, steps_of(longest, narrow_ref[0])), functools.partial(step, channels // 2), 0)


def steps_of(longest, narrow):
    return (jnp.maximum(longest - narrow, 0) + STEP_P) // STEP_P


def conv_forward_kernel(cblock, base, narrow_ref, rank_ref, data_ref, table_ref, conv_ref, width_ref, feat_ref, lse_ref, ids_ref, e_ref, top, total, pre):
    tile = ids_ref.shape[1]
    words = rank_ref.shape[0]
    first = (base + pl.program_id(0)) * tile
    lane = first + lax.broadcasted_iota(jnp.int32, (words, tile), 1)
    hot = jnp.where(rank_ref[...] == lane, 1.0, 0.0).astype(BF16)
    moved = nn(data_ref[...], hot)
    shift = jnp.where(lax.broadcasted_iota(jnp.int32, moved.shape, 0) < MAX_CHARS, float(ID_SHIFT), 0.0)
    moved = moved + shift
    ids_ref[...] = moved
    lens = (moved[MAX_CHARS : MAX_CHARS + 1, :] + 0.5).astype(jnp.int32)
    longest = jnp.max(lens)
    embed_tile(ids_ref, table_ref, lens, e_ref, longest)
    limit = limits_of(lens)
    channels = conv_ref.shape[0]
    top[...] = jnp.full_like(top, -1e30)
    total[...] = jnp.zeros_like(total)

    def step(rows, s, carry):
        pre[:rows, :] = nn(conv_ref[:rows, :], windows_at(e_ref, limit, s))
        for sub in range(0, rows, SUB):
            part = slice(sub, sub + SUB)
            values = [pre[part, i * tile : (i + 1) * tile] for i in range(STEP_P)]
            before = top[part, :]
            best = functools.reduce(jnp.maximum, values, before)
            top[part, :] = best
            total[part, :] = total[part, :] * jnp.exp(before - best) + sum(jnp.exp(value - best) for value in values)
        return carry

    in_halves(step, channels, longest, narrow_ref)
    span = jnp.maximum(lens - width_ref[...], 0)
    lse = top[...] + jnp.log(total[...])
    lse_ref[...] = lse
    pooled = lse - jnp.log((span + 1).astype(F32))
    feat_ref[...] = (pooled * jax.nn.sigmoid(pooled)).astype(BF16)


def place_kernel(rank_ref, *refs):
    feats, out_ref = refs[:-1], refs[-1]
    total, base = 0.0, 0
    for feat_ref in feats:
        shape = (rank_ref.shape[0], feat_ref.shape[1])
        lane = base + lax.broadcasted_iota(jnp.int32, shape, 1)
        hot = jnp.where(rank_ref[...] == lane, 1.0, 0.0).astype(BF16)
        total = total + nt(hot, feat_ref[...])
        base += shape[1]
    out_ref[...] = total.astype(BF16)


def conv_forward(rank, data, table_t, conv_t, widths, narrow, cblock, base, count):
    words, channels = rank.shape[0], conv_t.shape[0]
    tile = min(256, words)
    span = count * tile
    full = lambda *shape: pl.BlockSpec(shape, lambda i: (0,) * len(shape))
    column = lambda depth: pl.BlockSpec((depth, tile), lambda i: (0, i))
    return pl.pallas_call(
        functools.partial(conv_forward_kernel, cblock, base),
        grid=(count,),
        in_specs=[
            pl.BlockSpec(memory_space=pltpu.SMEM),
            full(words, 1),
            full(*data.shape),
            full(*table_t.shape),
            full(*conv_t.shape),
            full(channels, 1),
        ],
        out_specs=[column(channels), column(channels), column(ID_ROWS), column(SLOTS_E * CHAR_DIM)],
        out_shape=[
            jax.ShapeDtypeStruct((channels, span), BF16),
            pltpu.HBM((channels, span), F32),
            pltpu.HBM((ID_ROWS, span), F32),
            pltpu.HBM((SLOTS_E * CHAR_DIM, span), BF16),
        ],
        scratch_shapes=[
            pltpu.VMEM((cblock, tile), F32),
            pltpu.VMEM((cblock, tile), F32),
            pltpu.VMEM((cblock, STEP_P * tile), F32),
        ],
        compiler_params=pltpu.CompilerParams(vmem_limit_bytes=48 * MIB),
        cost_estimate=lasting(11),
        name="conv_forward",
    )(narrow, rank, data, table_t, conv_t, widths)


def place_words(rank, feats):
    words, channels = rank.shape[0], feats[0].shape[0]
    rows = min(256, words)
    return pl.pallas_call(
        place_kernel,
        grid=(words // rows,),
        in_specs=[pl.BlockSpec((rows, 1), lambda i: (i, 0))] + [pl.BlockSpec(feat.shape, lambda i: (0, 0)) for feat in feats],
        out_specs=pl.BlockSpec((rows, channels), lambda i: (i, 0)),
        out_shape=jax.ShapeDtypeStruct((words, channels), BF16),
        compiler_params=pltpu.CompilerParams(vmem_limit_bytes=48 * MIB),
        cost_estimate=lasting(4),
        name="place_words",
    )(rank, *feats)


def conv_backward_kernel(cblock, n_parts, base, narrow_ref, ids_ref, e_ref, conv_ref, back_ref, width_ref, lse_ref, *refs):
    ranks, grads, refs = refs[:n_parts], refs[n_parts : 2 * n_parts], refs[2 * n_parts :]
    so_far, sums_ref, table_grad_ref, de_ref, dpool, pre, d_pre, found = refs
    tile = ids_ref.shape[1]
    lanes = table_grad_ref.shape[0]
    channels = conv_ref.shape[0]
    first = (base + pl.program_id(0)) * tile

    @pl.when(pl.program_id(0) == 0)
    def _():
        sums_ref[...] = so_far[...]
        table_grad_ref[...] = jnp.zeros_like(table_grad_ref)

    lens = (ids_ref[MAX_CHARS : MAX_CHARS + 1, :] + 0.5).astype(jnp.int32)
    longest = jnp.max(lens)
    limit = limits_of(lens)
    de_ref[...] = jnp.zeros_like(de_ref)
    moved = 0.0
    for rank_ref, grad_ref in zip(ranks, grads):
        row = first + lax.broadcasted_iota(jnp.int32, (tile, rank_ref.shape[1]), 0)
        moved = moved + nn(jnp.where(rank_ref[...] == row, 1.0, 0.0).astype(BF16), grad_ref[...])
    moved = moved.T
    span = jnp.maximum(lens - width_ref[...], 0)
    pooled = lse_ref[...] - jnp.log((span + 1).astype(F32))
    sigma = jax.nn.sigmoid(pooled)
    dpool[...] = moved * (sigma + pooled * sigma * (1 - sigma))

    def step(rows, s, carry):
        windows = windows_at(e_ref, limit, s)
        pre[:rows, :] = nn(conv_ref[:rows, :], windows)
        for sub in range(0, rows, SUB):
            part = slice(sub, sub + SUB)
            low, scale = lse_ref[part, :], dpool[part, :]
            for i in range(STEP_P):
                cols = slice(i * tile, (i + 1) * tile)
                d_pre[part, cols] = (jnp.exp(pre[part, cols] - low) * scale).astype(BF16)
        back = nn(back_ref[:, :rows], d_pre[:rows, :])
        for i in range(STEP_P):
            at = pl.ds(pl.multiple_of((s * STEP_P + i) * CHAR_DIM, CHAR_DIM), TAPS)
            de_ref[at, :] += back[:TAPS, i * tile : (i + 1) * tile]
        sums_ref[:rows, :] += nt(d_pre[:rows, :], windows)
        return carry

    in_halves(step, channels, longest, narrow_ref)
    letter = lax.broadcasted_iota(jnp.int32, (found.shape[0], tile), 0)

    def spread(s, carry):
        parts = []
        for i in range(STEP_P):
            p = s * STEP_P + i
            at = pl.ds(pl.multiple_of(p * CHAR_DIM, CHAR_DIM), CHAR_DIM)
            value = jnp.where(p < lens, de_ref[at, :], 0.0)
            high = value.astype(BF16)
            parts.append(jnp.concatenate([high, (value - high.astype(F32)).astype(BF16)], axis=0))
            row = ids_ref[pl.ds(p, 1), :].astype(jnp.int32)
            found[:, i * tile : (i + 1) * tile] = jnp.where(letter == row, 1.0, 0.0).astype(BF16)
        table_grad_ref[: found.shape[0], :] += nt(found[...], jnp.concatenate(parts, axis=1))
        return carry

    lax.fori_loop(0, (longest + STEP_P - 1) // STEP_P, spread, 0)

    @pl.when(pl.program_id(0) == pl.num_programs(0) - 1)
    def _():
        both = table_grad_ref[...].T
        total = both[:CHAR_DIM] + both[CHAR_DIM:]
        for piece in range(lanes // LANES):
            at = channels + piece * CHAR_DIM
            sums_ref[at : at + CHAR_DIM, :] += total[:, piece * LANES : (piece + 1) * LANES]


def conv_backward(ranks, ids, embedded, vocab, conv_t, conv_back, widths, narrow, lse, grads, cblock, base, tile, so_far):
    channels, words = conv_t.shape[0], ids.shape[1]
    full = lambda *shape: pl.BlockSpec(shape, lambda i: (0,) * len(shape))
    return pl.pallas_call(
        functools.partial(conv_backward_kernel, cblock, len(ranks), base),
        grid=(words // tile,),
        in_specs=[
            pl.BlockSpec(memory_space=pltpu.SMEM),
            pl.BlockSpec((ID_ROWS, tile), lambda i: (0, i)),
            pl.BlockSpec((SLOTS_E * CHAR_DIM, tile), lambda i: (0, i)),
            full(*conv_t.shape),
            full(*conv_back.shape),
            full(channels, 1),
            pl.BlockSpec((channels, tile), lambda i: (0, i)),
        ]
        + [full(*part.shape) for part in ranks]
        + [full(*part.shape) for part in grads]
        + [full(*so_far.shape)],
        out_specs=full(*so_far.shape),
        out_shape=jax.ShapeDtypeStruct(so_far.shape, F32),
        scratch_shapes=[
            pltpu.VMEM((-(-vocab // LANES) * LANES, 2 * CHAR_DIM), F32),
            pltpu.VMEM((SLOTS_E * CHAR_DIM, tile), F32),
            pltpu.VMEM((cblock, tile), F32),
            pltpu.VMEM((cblock, STEP_P * tile), F32),
            pltpu.VMEM((cblock, STEP_P * tile), BF16),
            pltpu.VMEM((-(-vocab // 16) * 16, STEP_P * tile), BF16),
        ],
        compiler_params=pltpu.CompilerParams(vmem_limit_bytes=48 * MIB),
        cost_estimate=lasting(15),
        name="conv_backward",
    )(narrow, ids, pltpu.with_memory_space_constraint(embedded, pltpu.HBM), conv_t, conv_back, widths, lse, *ranks, *grads, so_far)


def word_order(lengths):
    count = lengths.shape[0]
    key = lengths * count - jnp.arange(count, dtype=jnp.int32)
    return jnp.sum((key[None, :] > key[:, None]).astype(jnp.int32), axis=1, keepdims=True)


def conv_operands(char_ids, lengths, char_table, conv_weight, conv_bias, widths, cblock):
    words = char_ids.shape[0]
    channels = conv_weight.shape[1]
    vocab = char_table.shape[0]
    lanes = -(-vocab // LANES) * LANES
    rank = word_order(lengths)
    data = jnp.concatenate([char_ids.T - ID_SHIFT, lengths[None, :]], axis=0)
    data = jnp.pad(data, ((0, ID_ROWS - MAX_CHARS - 1), (0, 0))).astype(BF16)
    offsets = jnp.arange(TAPS, dtype=jnp.int32) // CHAR_DIM
    taps = jnp.where(offsets[:, None] < widths[None, :], conv_weight, 0.0).astype(BF16)
    parts, rest = [], conv_bias
    for _ in range(3):
        part = lax.reduce_precision(rest, 8, 7)
        parts.append(part)
        rest = rest - part
    kinds = jnp.arange(1, MAX_WIDTH + 1, dtype=jnp.int32)
    spans = jnp.where(kinds[:, None] == widths[None, :], -1e30, 0.0)
    under = jnp.concatenate([jnp.stack(parts), spans, jnp.zeros((DEPTH - TAPS - 3 - MAX_WIDTH, channels), F32)])
    conv_all = jnp.concatenate([taps, under.astype(BF16)])
    conv_back = jnp.pad(taps, ((0, DEPTH - TAPS), (0, 0)))
    table_t = jnp.pad(lax.reduce_precision(char_table, 8, 7).T, ((0, 0), (0, lanes - vocab)))
    narrow = widths[:: channels // 2]
    return rank, data, table_t, conv_all.T, conv_back, widths[:, None], narrow


def channel_widths(start, count, whole):
    channel = start + jnp.arange(count, dtype=jnp.int32)
    widths = jnp.ones((count,), jnp.int32)
    for power in range(6):
        widths = widths + (channel >= whole * 2**power // 64).astype(jnp.int32)
    return widths


def packing(height, under, cols):
    rest, half = height - under, cols // 2
    return [
        (0, 0, under, 0, 0, 0, cols),
        (1, 0, rest, 0, under, 0, cols),
        (1, rest, height // 2, 0, 0, cols, half),
        (1, rest, height // 2, half, height // 2, cols, half),
    ]


def load_pieces(table_ref, pieces, rows, dest, sems, half=None, proj=None):
    cols = pieces[0].shape[3]
    depth = dest.shape[1]

    def each(act):
        at = 0
        for ref in pieces:
            for j in range(ref.shape[0]):
                row, col = table_ref[0, at], table_ref[1, at]
                row = row if half is None else row - half * depth
                sem = sems.at[at]

                def go(ref=ref, j=j, row=row, col=col, sem=sem):
                    place = (slice(None), pl.ds(pl.multiple_of(row, rows), rows), pl.ds(pl.multiple_of(col, cols), cols))
                    act(pltpu.make_async_copy(ref.at[j, :, :rows, :], dest.at[place], sem))

                if half is None:
                    go()
                else:
                    pl.when((row >= 0) & (row < depth))(go)
                if proj is not None:
                    under, height = ref.shape[2] - rows, proj[2]
                    first = pl.multiple_of(table_ref[2, at], height)
                    for n, (side, begin, count, left, row, out_left, wide) in enumerate(packing(height, under, cols)):
                        source = ref.at[j, side, rows + begin : rows + begin + count, left : left + wide]
                        to = proj[0].at[pl.ds(first + row, count), out_left : out_left + wide]
                        act(pltpu.make_async_copy(source, to, proj[1].at[4 * at + n]))
                at += 1

    each(lambda copy: copy.start())
    each(lambda copy: copy.wait())


def hidden_of(xs, weight, unit, cols, bias_ref):
    at, total = 0, None
    for x in xs:
        term = nn(x[...], weight[unit, at : at + x.shape[1], cols])
        total = term if total is None else total + term
        at += x.shape[1]
    return total + bias_ref[unit : unit + 1, cols]


def sigmoid(value):
    return 0.5 * jnp.tanh(0.5 * value) + 0.5


def factors(x, a, g):
    s = sigmoid(a)
    gate = sigmoid(g)
    nonlinear = a * s
    left = 1 - gate
    gap = x - nonlinear
    return nonlinear + gate * gap, left * (s + nonlinear * (1 - s)), gap * gate * left, gate


def forward_kernel(n_own, n_pieces, rows, width, table_ref, bias_ref, *refs):
    own, refs = refs[:n_own], refs[n_own:]
    mate, refs = refs[:n_own], refs[n_own:]
    pieces, refs = refs[:n_pieces], refs[n_pieces:]
    next_ref, low_ref, first_ref, second_ref, gate_ref, weight, sems = refs

    @pl.when(pl.program_id(0) == 0)
    def _():
        load_pieces(table_ref, pieces, rows, weight, sems)

    for j, x in enumerate(own):
        cols = slice(j * width, (j + 1) * width)
        a = hidden_of(own + mate, weight, 0, cols, bias_ref)
        g = hidden_of(own + mate, weight, 1, cols, bias_ref)
        value, first, second, gate = factors(x[...].astype(F32), a, g)
        next_ref[:, cols] = value
        low_ref[:, cols] = value.astype(BF16)
        first_ref[:, cols] = first.astype(BF16)
        second_ref[:, cols] = second.astype(BF16)
        gate_ref[:, cols] = gate.astype(BF16)


def column_sums(sums_ref, cols, d_first, d_gate):
    sums_ref[0:1, cols] += jnp.sum(d_first.astype(F32), axis=0, keepdims=True)
    sums_ref[1:2, cols] += jnp.sum(d_gate.astype(F32), axis=0, keepdims=True)


def product_back(out_ref, d_first, d_gate, weight, base, up=None):
    width = min(512, out_ref.shape[1])
    for j in range(out_ref.shape[1] // width):
        cols = slice(j * width, (j + 1) * width)
        rows = slice(base + j * width, base + (j + 1) * width)
        value = nt(d_first[...], weight[0, rows, :]) + nt(d_gate[...], weight[1, rows, :])
        if up is not None:
            value = value + up[:, cols]
        out_ref[:, cols] = value.astype(out_ref.dtype)


def turn_kernel(n_pieces, rows, width, packed, table_ref, bias_ref, own, mate, exact, out_grad, *refs):
    if packed:
        pieces, refs = refs[:n_pieces], refs[n_pieces:]
        low_ref, d_first_ref, d_gate_ref, up_ref, leaving_ref, vectors_ref, sums_ref, weight, sems, proj, proj_sems = refs
        proj_rows = (proj, proj_sems, proj.shape[0] // table_ref.shape[1])
    else:
        proj, pieces, refs = refs[0], refs[1 : n_pieces + 1], refs[n_pieces + 1 :]
        low_ref, d_first_ref, d_gate_ref, up_ref, leaving_ref, vectors_ref, sums_ref, weight, sems = refs
        proj_rows = None

    @pl.when(pl.program_id(0) == 0)
    def _():
        load_pieces(table_ref, pieces, rows, weight, sems, None, proj_rows)
        sums_ref[...] = jnp.zeros_like(sums_ref)

    half = own.shape[1]
    for j in range(half // width):
        cols = slice(j * width, (j + 1) * width)
        a = hidden_of((own, mate), weight, 0, cols, bias_ref)
        g = hidden_of((own, mate), weight, 1, cols, bias_ref)
        dy = nt(out_grad[...], proj[cols, :])
        value, first, second, gate = factors(exact[:, cols], a, g)
        low_ref[:, cols] = value.astype(BF16)
        d_first, d_gate = (dy * first).astype(BF16), (dy * second).astype(BF16)
        d_first_ref[:, cols] = d_first
        d_gate_ref[:, cols] = d_gate
        up_ref[:, cols] = dy * gate
        column_sums(sums_ref, cols, d_first, d_gate)
    product_back(leaving_ref, d_first_ref, d_gate_ref, weight, half)
    vectors_ref[...] = nn(low_ref[...], proj[...])


def slope_kernel(n_pieces, rows, width, table_ref, partial, arrived, first_ref, second_ref, gate_ref, *refs):
    pieces, refs = refs[:n_pieces], refs[n_pieces:]
    d_first_ref, d_gate_ref, up_ref, leaving_ref, sums_ref, weight, sems = refs

    @pl.when(pl.program_id(0) == 0)
    def _():
        load_pieces(table_ref, pieces, rows, weight, sems, 1)
        sums_ref[...] = jnp.zeros_like(sums_ref)

    for j in range(partial.shape[1] // width):
        cols = slice(j * width, (j + 1) * width)
        dy = partial[:, cols] + arrived[:, cols].astype(F32)
        d_first, d_gate = (dy * first_ref[:, cols].astype(F32)).astype(BF16), (dy * second_ref[:, cols].astype(F32)).astype(BF16)
        d_first_ref[:, cols] = d_first
        d_gate_ref[:, cols] = d_gate
        up_ref[:, cols] = dy * gate_ref[:, cols].astype(F32)
        column_sums(sums_ref, cols, d_first, d_gate)
    product_back(leaving_ref, d_first_ref, d_gate_ref, weight, 0)


def back_kernel(n_pieces, rows, table_ref, d_first, d_gate, up, *refs):
    pieces, refs = refs[:n_pieces], refs[n_pieces:]
    out_ref, weight, sems = refs

    @pl.when(pl.program_id(0) == 0)
    def _():
        load_pieces(table_ref, pieces, rows, weight, sems, 0)

    product_back(out_ref, d_first, d_gate, weight, 0, up)


def weight_grad_kernel(n_chunks, n_cols, n_d, width, table_ref, *refs):
    xs, refs = refs[: n_chunks * n_cols], refs[n_chunks * n_cols :]
    d_first, d_gate, refs = refs[:n_d], refs[n_d : 2 * n_d], refs[2 * n_d :]
    outs, turned = refs[:-1], refs[-1]
    rows = outs[0].shape[2]

    @pl.when(pl.program_id(0) == 0)
    def _():
        word = 0
        for chunk in range(n_chunks):
            at = 0
            for x in xs[chunk * n_cols : (chunk + 1) * n_cols]:
                turned[at : at + x.shape[1], word : word + x.shape[0]] = x[...].T
                at += x.shape[1]
            word += x.shape[0]

    blocks = d_first[0].shape[1] // width
    for side in range(2):
        row = table_ref[side, pl.program_id(0)]
        left = turned[pl.ds(pl.multiple_of(row, rows), rows), :]
        for j in range(blocks):
            cols = slice(j * width, (j + 1) * width)
            out = outs[blocks].at[j] if side else outs[j]
            for unit, ds in enumerate((d_first, d_gate)):
                total, word = 0.0, 0
                for d in ds:
                    total = total + nn(left[:, word : word + d.shape[0]], d[:, cols])
                    word += d.shape[0]
                out[0, unit] = total.astype(BF16)


SMEM_SPEC = pl.BlockSpec(memory_space=pltpu.SMEM)
HBM_SPEC = pl.BlockSpec(memory_space=pltpu.HBM)


def whole(array):
    return pl.BlockSpec(array.shape, lambda i: (0,) * array.ndim)


def by_rows(rows, width, base=0):
    return pl.BlockSpec((rows, width), lambda i: (base + i, 0))


def params(**kw):
    return pltpu.CompilerParams(vmem_limit_bytes=58 * MIB, **kw)


def count_of(pieces):
    return sum(piece.shape[0] for piece in pieces)


def highway_forward(table, pieces, block_rows, bias, own, mate, chunk, words):
    width = own[0].shape[1]
    half = width * len(own)
    rows = min(ROWS, words)
    steps = words // rows
    tile = by_rows(rows, width, chunk * steps)
    out = by_rows(rows, half)
    return pl.pallas_call(
        functools.partial(forward_kernel, len(own), len(pieces), block_rows, width),
        grid=(steps,),
        in_specs=[SMEM_SPEC, whole(bias)] + [tile] * (2 * len(own)) + [HBM_SPEC] * len(pieces),
        out_specs=[out] * 5,
        out_shape=[jax.ShapeDtypeStruct((words, half), kind) for kind in (F32, BF16, BF16, BF16, BF16)],
        scratch_shapes=[pltpu.VMEM((2, 2 * half, half), BF16), pltpu.SemaphoreType.DMA((count_of(pieces),))],
        compiler_params=params(),
        cost_estimate=lasting(10),
        name="highway_forward",
    )(table, bias, *own, *mate, *pieces)


def highway_turn(table, pieces, block_rows, bias, own, mate, exact, out_grad, proj, width):
    words, half = own.shape
    out_width = out_grad.shape[1]
    rows = min(ROWS, words)
    tile = by_rows(rows, half)
    packed = proj is None
    scratch = [pltpu.VMEM((2, 2 * half, half), BF16), pltpu.SemaphoreType.DMA((count_of(pieces),))]
    if packed:
        scratch += [pltpu.VMEM((half, out_width), BF16), pltpu.SemaphoreType.DMA((4 * count_of(pieces),))]
    return pl.pallas_call(
        functools.partial(turn_kernel, len(pieces), block_rows, width, packed),
        grid=(words // rows,),
        in_specs=[SMEM_SPEC, whole(bias), tile, tile, tile, by_rows(rows, out_width)]
        + ([] if packed else [whole(proj)])
        + [HBM_SPEC] * len(pieces),
        out_specs=[tile] * 5 + [by_rows(rows, out_width), pl.BlockSpec((2, half), lambda i: (0, 0))],
        out_shape=[jax.ShapeDtypeStruct((words, half), kind) for kind in (BF16, BF16, BF16, F32, BF16)]
        + [jax.ShapeDtypeStruct((words, out_width), F32), jax.ShapeDtypeStruct((2, half), F32)],
        scratch_shapes=scratch,
        compiler_params=params(),
        cost_estimate=lasting(16),
        name="highway_turn",
    )(table, bias, own, mate, exact, out_grad, *([] if packed else [proj]), *pieces)


def highway_slopes(table, pieces, block_rows, partial, arrived, first, second, gate, width):
    words, half = partial.shape
    rows = min(ROWS, words)
    tile = by_rows(rows, half)
    return pl.pallas_call(
        functools.partial(slope_kernel, len(pieces), block_rows, width),
        grid=(words // rows,),
        in_specs=[SMEM_SPEC] + [tile] * 5 + [HBM_SPEC] * len(pieces),
        out_specs=[tile, tile, tile, tile, pl.BlockSpec((2, half), lambda i: (0, 0))],
        out_shape=[jax.ShapeDtypeStruct((words, half), kind) for kind in (BF16, BF16, F32, BF16)] + [jax.ShapeDtypeStruct((2, half), F32)],
        scratch_shapes=[pltpu.VMEM((2, half, half), BF16), pltpu.SemaphoreType.DMA((count_of(pieces),))],
        compiler_params=params(),
        cost_estimate=lasting(8),
        name="highway_slopes",
    )(table, partial, arrived, first, second, gate, *pieces)


def highway_back(table, pieces, block_rows, d_first, d_gate, up):
    words, width = d_first.shape
    rows = min(ROWS, words)
    tile = by_rows(rows, width)
    return pl.pallas_call(
        functools.partial(back_kernel, len(pieces), block_rows),
        grid=(words // rows,),
        in_specs=[SMEM_SPEC, tile, tile, tile] + [HBM_SPEC] * len(pieces),
        out_specs=tile,
        out_shape=jax.ShapeDtypeStruct((words, width), F32),
        scratch_shapes=[pltpu.VMEM((2, width, width), BF16), pltpu.SemaphoreType.DMA((count_of(pieces),))],
        compiler_params=params(),
        cost_estimate=lasting(6),
        name="highway_back",
    )(table, d_first, d_gate, up, *pieces)


def highway_weight_grad(table, xs, d_first, d_gate, rows, width):
    half = d_first[0].shape[1]
    words = sum(d.shape[0] for d in d_first)
    flat = [x for row in xs for x in row]
    steps = table.shape[1]
    blocks = half // width
    block = pl.BlockSpec((1, 2, rows, width), lambda i: (i, 0, 0, 0))
    return pl.pallas_call(
        functools.partial(weight_grad_kernel, len(xs), len(xs[0]), len(d_first), width),
        grid=(steps,),
        in_specs=[SMEM_SPEC] + [whole(x) for x in flat] + [whole(d) for d in d_first + d_gate],
        out_specs=[block] * blocks + [pl.BlockSpec((blocks, 1, 2, rows, width), lambda i: (0, i, 0, 0, 0))],
        out_shape=[jax.ShapeDtypeStruct((steps, 2, rows, width), BF16)] * blocks
        + [jax.ShapeDtypeStruct((blocks, steps, 2, rows, width), BF16)],
        scratch_shapes=[pltpu.VMEM((2 * half, words), BF16)],
        compiler_params=params(),
        cost_estimate=lasting(15),
        name="highway_weight_grad",
    )(table, *flat, *d_first, *d_gate)


def adam_update(weight, grad, moment_one, moment_two, rate):
    first_new = beta_one * moment_one + (1 - beta_one) * grad
    second_new = beta_two * moment_two + (1 - beta_two) * grad * grad
    corrected_one = first_new / (1 - beta_one**STEP)
    corrected_two = second_new / (1 - beta_two**STEP)
    updated = weight - rate * (
        corrected_one / (jnp.sqrt(corrected_two) + adam_eps) + decay_rate * weight
    )
    return (second_new, updated)


def owner_kernel(n_grads, at_ref, *refs):
    grads, refs = refs[:n_grads], refs[n_grads:]
    weight, one, two, average = refs[:4]
    grad, second, new, average_new = refs[-4:]
    width = grads[0].shape[1]
    for j, ref in enumerate(grads):
        at = pl.ds(pl.multiple_of(at_ref[j], LANES), width)
        grad[0, :, at] = ref[...].astype(F32)
    second_new, updated = adam_update(weight[...], grad[...], one[...], two[...], 0.02)
    second[...] = second_new
    new[...] = updated
    average_new[...] = average_keep * average[...] + (1 - average_keep) * updated


def owner_update(slot, at, grads, weight, one, two, average, so_far=()):
    rows, width = grads[0].shape
    part = min(64, rows)
    block = pl.BlockSpec((1, part, weight.shape[2]), lambda i: (slot, i, 0))
    given = len(grads) + 5
    return pl.pallas_call(
        functools.partial(owner_kernel, len(grads)),
        grid=(rows // part,),
        in_specs=[SMEM_SPEC]
        + [pl.BlockSpec((part, width), lambda i: (i, 0))] * len(grads)
        + [block] * 4
        + [HBM_SPEC] * len(so_far),
        out_specs=[block] * 4,
        out_shape=[jax.ShapeDtypeStruct(weight.shape, F32)] * 4,
        input_output_aliases={given + n: n for n in range(len(so_far))},
        compiler_params=params(),
        cost_estimate=lasting(8),
        name="owner_update",
    )(at, *grads, weight, one, two, average, *so_far)


def slot_of(owner_ref, unit):
    return sum(jnp.where(owner_ref[before] == owner_ref[unit], 1, 0) for before in range(unit)) if unit else 0


def choose_kernel(n_from, owner_ref, proj, *refs):
    arrived, outs = refs[:n_from], refs[n_from:]
    rows, width = arrived[0].shape[1:]
    here = lax.axis_index("filt")
    for unit in range(UNITS):
        for step, ref in enumerate(arrived):

            @pl.when(owner_ref[unit] ^ here == step)
            def _(ref=ref, unit=unit):
                outs[unit // 2][unit % 2, :rows, :] = ref[slot_of(owner_ref, unit)]

    under = outs[1].shape[1] - rows
    if under:
        for side, begin, count, left, row, out_left, wide in packing(proj.shape[0], under, width):
            value = proj[row : row + count, out_left : out_left + wide].astype(BF16)
            outs[1][side, rows + begin : rows + begin + count, left : left + wide] = value


def choose_units(owners, arrived, proj, packed):
    slots, rows, width = arrived[0].shape
    shapes = [(2, rows, width), (2, rows + (proj.size // (2 * width) if packed else 0), width)]
    return pl.pallas_call(
        functools.partial(choose_kernel, len(arrived)),
        grid=(1,),
        in_specs=[SMEM_SPEC, whole(proj)] + [whole(part) for part in arrived],
        out_specs=[pl.BlockSpec(shape, lambda i: (0, 0, 0)) for shape in shapes],
        out_shape=[jax.ShapeDtypeStruct(shape, BF16) for shape in shapes],
        compiler_params=params(),
        cost_estimate=lasting(3),
        name="choose_units",
    )(owners, proj, *arrived)


def return_kernel(counts, owner_ref, *refs):
    layers = (refs[: counts[0]], refs[counts[0] : counts[0] + counts[1]])
    here = lax.axis_index("filt")
    outs = refs[counts[0] + counts[1] :]
    for step in range(len(outs) // SLOTS):
        for slot in range(SLOTS):
            out = outs[SLOTS * step + slot]
            taken = -1
            for unit in range(UNITS):
                fits = (owner_ref[unit] ^ here == step) & (slot_of(owner_ref, unit) == slot)
                taken = jnp.where(fits, unit, taken)
            for unit in range(UNITS):

                @pl.when(taken == unit)
                def _(unit=unit, out=out):
                    out[...] = sum(ref[unit % 2].astype(F32) for ref in layers[unit // 2]).astype(BF16)

            @pl.when(taken < 0)
            def _(out=out):
                out[...] = jnp.zeros(out.shape, BF16)


def return_units(owners, layers, count):
    shape = layers[0][0].shape
    part = min(128, shape[1])
    block = pl.BlockSpec((2, part, shape[2]), lambda i: (0, i, 0))
    terms = list(layers[0]) + list(layers[1])
    return pl.pallas_call(
        functools.partial(return_kernel, [len(layer) for layer in layers]),
        grid=(shape[1] // part,),
        in_specs=[SMEM_SPEC] + [block] * len(terms),
        out_specs=[pl.BlockSpec((part, shape[2]), lambda i: (i, 0))] * (SLOTS * count),
        out_shape=[jax.ShapeDtypeStruct(shape[1:], BF16)] * (SLOTS * count),
        compiler_params=params(),
        cost_estimate=lasting(3),
        name="return_units",
    )(owners, *terms)


class Places:
    def __init__(self):
        self.n_filt, self.n_dp = lax.axis_size("filt"), lax.axis_size("dp")
        self.n_y, self.n_z = self.n_filt // 2, self.n_dp // 2
        self.f, self.d = lax.axis_index("filt"), lax.axis_index("dp")
        self.y, self.x = self.f // 2, self.f % 2
        self.z, self.c = self.d // 2, self.d % 2
        self.direct = self.n_y == 2 and self.n_z == 4

    def over_filt(self, value, step):
        return lax.ppermute(value, "filt", [(i, i ^ step) for i in range(self.n_filt)])

    def over_x(self, value):
        return self.over_filt(value, 1)

    def over_y(self, value, step):
        return self.over_filt(value, 2 * step)

    def over_core(self, value):
        return lax.ppermute(value, "dp", [(i, i ^ 1) for i in range(self.n_dp)])

    def over_z(self, value, step):
        pairs = [(i, (i // 2 + step) % self.n_z * 2 + i % 2) for i in range(self.n_dp)]
        return lax.ppermute(value, "dp", pairs)

    def far_first(self):
        return sorted(range(1, self.n_z), key=lambda k: (min(k, self.n_z - k), k))

    def row_of(self, d, rows, width):
        f = d * rows // width
        half = self.n_y * width
        return (f % 2 ^ self.x) * half + (f // 2 ^ self.y) * width + d * rows % width


def after(value, *earlier):
    return lax.optimization_barrier((value, earlier))[0]


def settle(*values):
    return lax.optimization_barrier(values)


def gather_general(place, blocks):
    rows, width = blocks[0].shape[1:]
    out = []
    for piece in blocks:
        spread = lax.all_gather(lax.all_gather(piece, "dp"), "filt")
        spread = spread.reshape((place.n_y, 2) + spread.shape[1:])
        spread = lax.dynamic_index_in_dim(spread, place.x, 1, keepdims=False)
        spread = spread.reshape((place.n_y * place.n_dp,) + piece.shape)
        d = jnp.tile(jnp.arange(place.n_dp, dtype=jnp.int32), place.n_y)
        y = jnp.repeat(jnp.arange(place.n_y, dtype=jnp.int32), place.n_dp)
        table = jnp.stack([place.row_of(d, rows, width), (y ^ place.y) * width]).astype(jnp.int32)
        out.append((table, [spread]))
    return out


BLOCK_STEPS = (
    [(0, 0), (0, 1), (1, 0), (3, 0), (2, 0), (1, 1), (3, 1), (2, 1)],
    [(0, 0), (0, 1), (1, 0), (3, 0), (1, 1), (3, 1), (2, 0), (2, 1)],
)


def gather_table(place, layer, rows, width, rows_proj):
    at_rows, at_cols, at_proj = [], [], []
    for other in range(2):
        for k, step in BLOCK_STEPS[layer]:
            d = (place.z - k) % place.n_z * 2 + (place.c ^ other)
            at_rows.append(place.row_of(d, rows, width))
            at_cols.append(jnp.int32(step * width))
            at_proj.append(step * width + d * rows_proj)
    return jnp.stack([jnp.stack(at_rows), jnp.stack(at_cols), jnp.stack(at_proj)]).astype(jnp.int32)


Z_SEQUENCE = (1, 3, 2, 0)


def sum_table(place, rows, width):
    z = jnp.arange(place.n_z, dtype=jnp.int32)
    z, c = ((place.z + jnp.asarray(Z_SEQUENCE, jnp.int32)) % place.n_z, place.c) if place.direct else (z, 0)
    return jnp.stack([place.row_of(z * 2 + c, rows, width), place.row_of(z * 2 + (1 - c), rows, width)]).astype(jnp.int32)


def sent_over_y(parts, group):
    near, arrived = parts
    return (near[1][group].astype(F32) + arrived[1][group].astype(F32)).astype(BF16)


def kept_over_y(parts, turned, group):
    near, arrived = parts
    steps = range(group.start, group.stop)
    return [near[0][k].astype(F32) + arrived[0][k].astype(F32) + turned[n].astype(F32) for n, k in enumerate(steps)]


def sum_general(place, blocks):
    n_y = place.n_y
    near, far = blocks[:n_y], list(blocks[n_y])
    steps = jnp.arange(n_y, dtype=jnp.int32) ^ place.y
    pairs = jnp.stack([jnp.stack(near), jnp.stack(far)], axis=2)
    pairs = jnp.take(pairs, steps, axis=0)
    pairs = pairs.reshape((n_y, place.n_dp) + pairs.shape[3:])
    mine = lax.psum_scatter(pairs, "dp", scatter_dimension=1)
    sides = jnp.arange(2, dtype=jnp.int32).reshape(1, 2, 1, 1, 1)
    mine = jnp.where(sides == place.x, mine[:, None], jnp.zeros((), BF16))
    mine = mine.reshape((place.n_filt,) + mine.shape[2:])
    return lax.psum_scatter(mine, "filt", scatter_dimension=0).astype(F32)


def pick(array, at, axis=0):
    return lax.dynamic_index_in_dim(array, at, axis, keepdims=False)


def rows_over_core(place, value):
    parts = value.reshape((place.n_z, 2, -1) + value.shape[1:])
    return pick(parts, place.c, 1), over_core_low(place, pick(parts, 1 - place.c, 1))


def over_core_low(place, value):
    return place.over_core(value.astype(BF16))


def swap_z(place, value, step):
    pairs = [(i, i ^ (2 * step)) for i in range(place.n_dp)]
    return lax.ppermute(value, "dp", pairs)


def swap_rows(place, parts, step):
    upper = place.z // step % 2
    halves = parts.reshape((2, -1) + parts.shape[1:])
    return pick(halves, upper), swap_z(place, pick(halves, 1 - upper).astype(BF16), step)


def sum_filt(place, value):
    if not place.direct:
        return lax.psum(value, "filt")
    step = 1
    while step < place.n_filt:
        value = value + place.over_filt(value, step)
        step *= 2
    return value


def per_device(
    char_ids,
    word_lengths,
    out_grad,
    highway_owner,
    char_table,
    conv_weight,
    conv_bias,
    highway_weight,
    proj_weight,
    dense_bias,
    table_moment_one,
    table_moment_two,
    conv_moment_one,
    conv_moment_two,
    conv_bias_moment_one,
    conv_bias_moment_two,
    highway_moment_one,
    highway_moment_two,
    highway_average,
    proj_moment_one,
    proj_moment_two,
    bias_moment_one,
    bias_moment_two,
):
    place = Places()
    n_y, n_filt, direct = place.n_y, place.n_filt, place.direct
    width = conv_weight.shape[1]
    rows, width_full = highway_weight.shape[1:]
    half = width_full // 2
    rows_proj, out_width = proj_weight.shape
    vocab_count = char_table.shape[0]
    words_dev = char_ids.shape[0]
    words_y = words_dev // n_y
    chunks, chunk_words = range(2), words_y // 2
    steps_y = list(range(1, n_y))
    mine_first = place.x == 0
    over_core, over_x, over_y, over_z = place.over_core, place.over_x, place.over_y, place.over_z

    widths = channel_widths(place.f * width, width, FILTERS)
    offsets = jnp.arange(TAPS, dtype=jnp.int32) // CHAR_DIM
    tap_mask = (offsets[:, None] < widths[None, :]).astype(jnp.float32)
    tile = min(256, words_dev)
    n_tiles = words_dev // tile
    cuts = [0, 1, 2, 4, 8] if n_tiles == 8 else [0, n_tiles]
    splits = list(zip(cuts[:-1], cuts[1:]))
    rank, data, table_t, conv_t, conv_back, width_col, narrow = conv_operands(
        char_ids, word_lengths, char_table, conv_weight, conv_bias, widths, width
    )
    rank_parts = [lax.dynamic_slice_in_dim(rank, (place.y ^ step) * words_y, words_y, axis=0) for step in range(n_y)]

    def convolve(some, narrow):
        return [conv_forward(rank, data, table_t, conv_t, width_col, narrow, width, begin, end - begin) for begin, end in some]

    def block_of(step):
        start = (place.f ^ step) * width
        return lax.dynamic_slice_in_dim(highway_weight, start, width, axis=2).astype(BF16)

    from_owner = [block_of(0)] + [place.over_filt(block_of(step), step) for step in range(1, n_filt)]
    kept = convolve(splits[: len(splits) // 2], narrow)
    from_owner, kept, narrow = settle(from_owner, kept, narrow)
    blocks = choose_units(highway_owner, from_owner, proj_weight, direct)
    bias_float = lax.reduce_precision(dense_bias, 8, 7)

    def half_bias(unit):
        starts = [unit * width_full + (2 * (place.y ^ step) + place.x) * width for step in range(n_y)]
        return jnp.concatenate([lax.dynamic_slice_in_dim(bias_float, start, width) for start in starts])

    layer_bias = [jnp.stack([half_bias(2 * layer), half_bias(2 * layer + 1)]) for layer in range(2)]

    blocks, narrow, sent, layer_bias = settle(blocks, narrow, out_grad, layer_bias)
    grad_mate = over_x(sent)
    if direct:
        first_y = [over_y(block, 1) for block in blocks]
        near = [over_z(blocks[0], k) for k in (1, 3)]
    kept = kept + convolve(splits[len(splits) // 2 :], narrow)
    placed = [place_words(part, [parts[0] for parts in kept]) for part in rank_parts]
    own = [placed[0]] + [over_y(placed[step], step) for step in steps_y]
    if direct:
        near, first_y, placed, grad_mate, blocks = settle(near, first_y, placed, grad_mate, blocks)
        own = [placed[0], over_y(placed[1], 1)]
        mate = [over_x(placed[0])]
        far = over_z(blocks[0], 2)
        sent = jnp.stack([near[0], near[1], jnp.zeros_like(near[0])])
        own, mate, far, sent, blocks, first_y, layer_bias, grad_mate = settle(
            own, mate, far, sent, blocks, first_y, layer_bias, grad_mate
        )

        out_grads = [jnp.where(mine_first, out_grad, grad_mate), jnp.where(mine_first, grad_mate, out_grad)]
        out_sum = jnp.sum(out_grad, axis=0, dtype=F32)
        sent = lax.dynamic_update_index_in_dim(sent, far, 2, 0)
        sent_y = over_y(sent, 1)
        mate = mate + [over_x(own[1])]
        near_one = [over_z(blocks[1], k) for k in (1, 3)]
        sent_core = over_core(sent)
        start = jnp.stack([blocks[0], first_y[0]])
        table = [gather_table(place, layer, rows, width, rows_proj) for layer in range(2)]
        sent_y, sent_core, start, mate, near_one, blocks, out_grads, table, out_sum = settle(
            sent_y, sent_core, start, mate, near_one, blocks, out_grads, table, out_sum
        )

        gathered = [(table[0], [start, sent, sent_y, over_core(start), sent_core, over_core(sent_y)], rows)]
        far_one = over_z(blocks[1], 2)
        near_y = over_y(jnp.stack(near_one), 1)
    else:
        mate = [over_x(part) for part in own]
        gathered = [(*found, rows) for found in gather_general(place, blocks)]
        out_sum = jnp.sum(out_grad, axis=0, dtype=F32)
        out_grads = [jnp.where(mine_first, out_grad, grad_mate), jnp.where(mine_first, grad_mate, out_grad)]

    forward, x_one_mate = [], []
    for chunk in chunks:
        forward.append(highway_forward(*gathered[0], layer_bias[0], own, mate, chunk, chunk_words))
        x_one_mate.append(over_x(forward[chunk][1]))
        if direct and chunk == 0:
            forward[0], near_one, layer_bias[0] = settle(forward[0], near_one, layer_bias[0])
            start = jnp.stack([blocks[1], first_y[1], near_one[0], near_one[1]])
            start_core = over_core(start)
    if direct:
        far_one, near_y, forward[1] = settle(far_one, near_y, forward[1])
        far_y = over_y(far_one, 1)
        far_y, x_one_mate[0] = settle(far_y, x_one_mate[0])
        last = jnp.stack([near_y[0], near_y[1], far_one, far_y])
        gathered.append((table[1], [start, last, start_core, over_core(last)], rows))
        proj_half = None
    else:
        proj_own = jnp.stack([proj_weight.astype(BF16)] + [over_y(proj_weight.astype(BF16), step) for step in steps_y])
        proj_half = lax.all_gather(proj_own, "dp", axis=1).reshape(half, out_width)
    x_one, x_one_low, first_zero, second_zero, gate_zero = zip(*forward)
    turned, arrived = [], []
    for chunk in chunks:
        bias_one = layer_bias[1] if chunk == 0 else settle(layer_bias[1], turned[0])[0]
        turned.append(
            highway_turn(*gathered[1], bias_one, x_one_low[chunk], x_one_mate[chunk], x_one[chunk], out_grads[chunk], proj_half, width)
        )
        arrived.append(over_x(turned[chunk][4]))
    x_two_low, d_first_one, d_gate_one, up_one, _, vectors, sums = (list(parts) for parts in zip(*turned))
    sums_one = sums[0] + sums[1]

    targets = sum_table(place, rows, width)
    blocks = highway_weight_grad(
        targets, [[x_one_low[chunk], x_one_mate[chunk]] for chunk in chunks], d_first_one, d_gate_one, rows, width
    )
    blocks, up_one[0], arrived[0] = settle(blocks, up_one[0], arrived[0])
    if not direct:
        sum_one = sum_general(place, blocks)

    partial, parts_zero, arrived_zero = [], [], []
    for chunk in chunks:
        partial.append(highway_back(*gathered[1], d_first_one[chunk], d_gate_one[chunk], up_one[chunk]))
        if chunk == 0 and direct:
            partial[0], arrived[1], blocks = settle(partial[0], arrived[1], blocks)
            one = (blocks[:2], over_core(blocks[2]))
        parts_zero.append(
            highway_slopes(*gathered[0], partial[chunk], arrived[chunk], first_zero[chunk], second_zero[chunk], gate_zero[chunk], width)
        )
        if chunk == 0 and direct:
            one, parts_zero[0], up_one[1] = settle(one, parts_zero[0], up_one[1])
            sent = sent_over_y(one, slice(0, place.n_z))
            sent, up_one[1] = settle(sent, up_one[1])
            one_y = over_y(sent, 1)
        arrived_zero.append(over_x(parts_zero[chunk][3]))
    d_first, d_gate, up, _, sums = (list(parts) for parts in zip(*parts_zero))
    sums_zero = sums[0] + sums[1]
    blocks = highway_weight_grad(targets, [own + mate], d_first, d_gate, rows, width)
    blocks, up, arrived_zero[0] = settle(blocks, up, arrived_zero[0])
    groups = [slice(0, 2), slice(2, 4)]
    if not direct:
        sum_zero = sum_general(place, blocks)
    partial = [highway_back(*gathered[0], d_first[chunk], d_gate[chunk], up[chunk]) for chunk in chunks]
    if direct:
        partial, blocks, arrived_zero[1], one_y = settle(partial, blocks, arrived_zero[1], one_y)
        zero = (blocks[:2], over_core(blocks[2]))
    if direct:
        one_here = kept_over_y(one, one_y, slice(0, place.n_z))
        one_sent = [one_here[n].astype(BF16) for n in (2, 0, 1)]
        one_here = one_here[3]
        one_sent, one_here, partial = settle(one_sent, one_here, partial)
        one_z = [over_z(value, k) for value, k in zip(one_sent, (2, 1, 3))]
    groups = [slice(0, 2), slice(2, 4)]
    if not direct:
        sum_zero = sum_general(place, blocks)
    partial = [highway_back(*gathered[0], d_first[chunk], d_gate[chunk], up[chunk]) for chunk in chunks]
    if direct:
        partial, blocks, arrived_zero[1], one_y = settle(partial, blocks, arrived_zero[1], one_y)
        zero = (blocks[:2], over_core(blocks[2]))
    feature_grad = []
    for step in range(n_y):
        cols = slice(step * width, (step + 1) * width)
        feature_grad.append(
            jnp.concatenate(
                [(partial[chunk][:, cols] + arrived_zero[chunk][:, cols].astype(F32)).astype(BF16) for chunk in chunks]
            )
        )
    groups = [slice(0, 2), slice(2, 4)]
    returned = [over_y(value, step) if step else value for step, value in enumerate(feature_grad)]
    if direct:
        returned[0], x_two_low, vectors = settle(returned[0], x_two_low, vectors)
        zero_y = [over_y(sent_over_y(zero, groups[0]), 1)]
    proj_part = (tn(x_two_low[0], out_grads[0]) + tn(x_two_low[1], out_grads[1])).reshape(n_y, width, out_width)
    proj_here, proj_away = proj_part[0], [proj_part[step].astype(BF16) for step in steps_y]
    vectors_away = jnp.where(mine_first, vectors[1], vectors[0]).astype(BF16)
    vectors_here = jnp.where(mine_first, vectors[0], vectors[1])
    ranks = [part.T for part in rank_parts]

    if direct:
        zero_sent = sent_over_y(zero, groups[1])
        returned, narrow, ranks, zero_sent = settle(returned, narrow, ranks, zero_sent)

    def convolve_back(n, narrow, so_far):
        (begin, _), (_, lse, sorted_ids, embedded) = splits[n], kept[n]
        return conv_backward(
            ranks, sorted_ids, embedded, vocab_count, conv_t, conv_back, width_col, narrow, lse, returned, width, begin, tile, so_far
        )

    home = jnp.arange(n_filt, dtype=jnp.int32)

    def natural(values):
        parts = values.reshape(n_y, 1, width)
        out = jnp.zeros((n_filt, width), F32)
        for step in range(n_y):
            out = jnp.where((home == 2 * (place.y ^ step) + place.x)[:, None], parts[step], out)
        return out.reshape(-1)

    bias_local = jnp.concatenate(
        [natural(sums[unit]) for sums in (sums_zero, sums_one) for unit in range(2)] + [out_sum]
    )
    table_rows = table_t.shape[1] // LANES * CHAR_DIM
    bias_rows = -(-bias_local.size // DEPTH)
    bias_rows += -(width + table_rows + bias_rows) % 16
    bias_flat = jnp.pad(bias_local, (0, bias_rows * DEPTH - bias_local.size)).reshape(bias_rows, DEPTH)
    small = jnp.concatenate([jnp.zeros((width + table_rows, DEPTH), F32), bias_flat])
    if direct:
        small, returned, narrow = settle(small, returned, narrow)
    back = small
    for n in range(len(splits)):
        back = convolve_back(n, narrow, back)
        if direct and n == 0:
            back, narrow, one_z, zero_y[0], zero, vectors_away, proj_away = settle(
                back, narrow, one_z, zero_y[0], zero, vectors_away, proj_away
            )
            zero_here = kept_over_y(zero, zero_y[0], groups[0])
            zero_z, zero_sent, narrow = settle([value.astype(BF16) for value in zero_here], zero_sent, narrow)
            zero_z = [over_z(value, k) for value, k in zip(zero_z, (1, 3))]
            zero_y.append(over_y(zero_sent, 1))
        if direct and n == 2:
            back, zero_z, narrow, zero_y, vectors_away, proj_away = settle(back, zero_z, narrow, zero_y, vectors_away, proj_away)
            vectors_arrived = over_x(vectors_away)
            last, zero_here = kept_over_y(zero, zero_y[1], groups[1])
            last, zero_here, narrow = settle(last.astype(BF16), zero_here, narrow)
            last = over_z(last, 2)
            proj_y = over_y(proj_away[0], 1)
    if direct:
        small = back + over_core(back)
        last, proj_y, small = settle(last, proj_y, small)
        small = small + swap_z(place, small.astype(BF16), 1).astype(F32)
        slot_grads = return_units(highway_owner, [[zero_here] + zero_z + [last], [one_here] + one_z], n_filt)
    else:
        proj_y = [over_y(value, step) for value, step in zip(proj_away, steps_y)]
        proj_grad = lax.psum_scatter(proj_here + sum(value.astype(F32) for value in proj_y), "dp", scatter_dimension=0, tiled=True)
    if not direct:
        vectors_arrived = over_x(vectors_away)
    if not direct:
        small = lax.psum(back, "dp")
        small = jnp.concatenate([small[:width], sum_filt(place, small[width:])])

    optimizer = (highway_weight, highway_moment_one, highway_moment_two, highway_average)
    columns = (place.f ^ jnp.arange(n_filt, dtype=jnp.int32)) * width
    if direct:
        slot_grads, proj_y, vectors_arrived, small = settle(slot_grads, proj_y, vectors_arrived, small)
        proj_rows = rows_over_core(place, proj_here + proj_y.astype(F32))
        by_slot = [slot_grads[slot::SLOTS] for slot in range(SLOTS)]
        to_owner = lambda grads: [grads[0]] + [place.over_filt(grads[step], step) for step in range(1, n_filt)]
        by_slot[0] = to_owner(by_slot[0])
        small = small + swap_z(place, small.astype(BF16), 2).astype(F32)
        by_slot, small, proj_rows = settle(by_slot, small, proj_rows)
        by_slot[1] = to_owner(by_slot[1])
        conv_sums, small = small[:width], small[width:]
        small = small + over_x(small)
        proj_rows = swap_rows(place, proj_rows[0] + proj_rows[1].astype(F32), 2)
        updates = owner_update(0, columns, by_slot[0], *optimizer)
        updates, small, proj_rows, by_slot[1] = settle(updates, small, proj_rows, by_slot[1])
        small = small + over_y(small, 1)
        proj_rows = swap_rows(place, proj_rows[0] + proj_rows[1].astype(F32), 1)
        updates = owner_update(1, columns, by_slot[1], *optimizer, updates)
        updates, small, proj_rows = settle(updates, small, proj_rows)
        proj_grad = (proj_rows[0] + proj_rows[1].astype(F32)).reshape(rows_proj, out_width)
    else:
        slot_grads = return_units(highway_owner, [[sum_zero], [sum_one]], n_filt)
        conv_sums, small = small[:width], small[width:]
        updates = ()
        for slot in range(SLOTS):
            grads = slot_grads[slot::SLOTS]
            grads = [grads[0]] + [place.over_filt(grads[step], step) for step in range(1, n_filt)]
            updates = owner_update(slot, columns, grads, *optimizer, updates)
    highway_grad, highway_second, highway_new, highway_average_new = updates
    word_vectors = vectors_here + vectors_arrived.astype(F32) + bias_float[UNITS * width_full :]
    conv_grad, conv_bias_grad = conv_sums[:, :TAPS].T * tap_mask, conv_sums[:, TAPS]
    table_grad = small[:table_rows].reshape(-1, CHAR_DIM, LANES).transpose(0, 2, 1).reshape(-1, CHAR_DIM)[:vocab_count]
    bias_grad = small[table_rows:].reshape(-1)[: bias_local.size]
    table_second, table_new = adam_update(
        char_table, table_grad, table_moment_one, table_moment_two, 1.0
    )
    conv_second, conv_new = adam_update(
        conv_weight, conv_grad, conv_moment_one, conv_moment_two, 0.1
    )
    conv_bias_second, conv_bias_new = adam_update(
        conv_bias, conv_bias_grad, conv_bias_moment_one, conv_bias_moment_two, 0.3
    )
    proj_second, proj_new = adam_update(
        proj_weight, proj_grad, proj_moment_one, proj_moment_two, 0.02
    )
    bias_second, bias_new = adam_update(
        dense_bias, bias_grad, bias_moment_one, bias_moment_two, 0.3
    )
    return (
        word_vectors,
        table_grad,
        table_second,
        table_new,
        conv_grad,
        conv_second,
        conv_new,
        conv_bias_grad,
        conv_bias_second,
        conv_bias_new,
        highway_grad,
        highway_second,
        highway_new,
        highway_average_new,
        proj_grad,
        proj_second,
        proj_new,
        bias_grad,
        bias_second,
        bias_new,
    )


def solution(mesh):
    return jax.shard_map(
        per_device,
        mesh=mesh,
        in_specs=(
            P("dp", None),
            P("dp"),
            P(("dp", "filt"), None),
            P(),
            P(),
            P(None, "filt"),
            P("filt"),
            P("filt", "dp", None),
            P(("filt", "dp"), None),
            P(),
            P(),
            P(),
            P(None, "filt"),
            P(None, "filt"),
            P("filt"),
            P("filt"),
            P("filt", "dp", None),
            P("filt", "dp", None),
            P("filt", "dp", None),
            P(("filt", "dp"), None),
            P(("filt", "dp"), None),
            P(),
            P(),
        ),
        out_specs=(
            P(("dp", "filt"), None),
            P(),
            P(),
            P(),
            P(None, "filt"),
            P(None, "filt"),
            P(None, "filt"),
            P("filt"),
            P("filt"),
            P("filt"),
            P("filt", "dp", None),
            P("filt", "dp", None),
            P("filt", "dp", None),
            P("filt", "dp", None),
            P(("filt", "dp"), None),
            P(("filt", "dp"), None),
            P(("filt", "dp"), None),
            P(),
            P(),
            P(),
        ),
        check_vma=False,
    )
```
